128 devices in a mesh: sq: 8 (over z, core), sk: 16 (over y, x).
Axes of the slice: x: 4, y: 4, z: 4, core: 2. Of those that a mesh axis runs over, the one named last changes fastest.
Arguments:
- queries: bfloat16 [2048, 128, 576], P('sk', 'sq'), may hold values from -40 to 40
- out_grad: bfloat16 [2048, 128, 512], P('sk', 'sq'), may hold values from -24 to 24
- latent_keys: bfloat16 [256, 128, 576], P('sk'), may hold values from -6 to 6
- index_queries: bfloat16 [2048, 64, 128], P('sk', 'sq'), may hold values from -7 to 7
- index_weights: float32 [2048, 64], P('sk', 'sq'), may hold values from 1 to 16
- index_keys: bfloat16 [256, 128, 128], P('sk'), may hold values from -6 to 6
- picks: int32 [16, 16], replicated, may hold values from 0 to 255, as said below
Outputs:
- query_grad: bfloat16 [2048, 128, 576], P('sk', 'sq')
- latent_key_grad: float32 [256, 128, 576], P('sk', 'sq')
- index_query_grad: float32 [2048, 64, 128], P('sk', 'sq')
- index_weight_grad: float32 [2048, 64], P('sk', 'sq')
- index_key_grad: float32 [256, 128, 128], P('sk', 'sq')
The draws below stay inside these ranges and needn't reach their ends.
Inputs may be any that keep to these rules, and one draw needn't show every extreme that they name: `picks`: row t lists 16 distinct key blocks for the queries of tile t. Within a row at most 2 blocks fall in one aligned range of 16 consecutive blocks, and every row has a range that holds exactly 2 of them.
All inputs are finite; a program needn't handle non-finite values.
Results may differ from the reference program's by a relative error of at most 0.0045.
Values may be sent and summed in bfloat16 or wider, within the bound.
A program may use at most 192 MiB of HBM per device.

```python
import math
import jax
import jax.numpy as jnp
from jax import lax

H = 128
LATENT = 512
ROPE = 64
HI = 64
ID = 128
TOPB = 16
BLOCK = 128
CAP = 2
Q_DEV = 128
KBS = 16
KDIM = 576
NQ = 2048
KEYS = 32768


def pick_blocks(base_key):
    base_key = jax.random.fold_in(base_key, 7)
    tile_count = NQ // Q_DEV
    shard_count = KEYS // (KBS * BLOCK)
    slot_count = shard_count * CAP
    first_key, order_key, local_key, shuffle_key = jax.random.split(base_key, 4)
    chosen = jax.random.randint(first_key, (tile_count,), 0, shard_count)

    def one_tile(tile_key, favored):
        order = jax.random.permutation(tile_key, slot_count)
        slot_ids = jnp.arange(slot_count, dtype=jnp.int32)
        priority = jnp.zeros((slot_count,), jnp.int32).at[order].set(slot_ids)
        priority = jnp.where(slot_ids // CAP == favored, -1 - slot_ids % CAP, priority)
        return jnp.argsort(priority, stable=True)[:TOPB].astype(jnp.int32)
    slot_pick = jax.vmap(one_tile)(jax.random.split(order_key, tile_count), chosen)
    local_table = jax.vmap(lambda sub_key: jax.random.permutation(sub_key, KBS)[:CAP])(jax.random.split(local_key, tile_count * shard_count)).reshape(tile_count, shard_count, CAP)
    shard_of = slot_pick // CAP
    rank_of = slot_pick % CAP
    local_block = local_table[jnp.arange(tile_count)[:, None], shard_of, rank_of]
    blocks = shard_of * KBS + local_block
    shuffle = jax.vmap(lambda sub_key: jax.random.permutation(sub_key, TOPB))(jax.random.split(shuffle_key, tile_count))
    return jnp.take_along_axis(blocks, shuffle, axis=1).astype(jnp.int32)


def key_fields(base_key):
    latent = jax.random.normal(jax.random.fold_in(base_key, 101), (KEYS // BLOCK, BLOCK, KDIM), jnp.float32)
    index = jax.random.normal(jax.random.fold_in(base_key, 102), (KEYS // BLOCK, BLOCK, ID), jnp.float32)
    return (jnp.clip(latent, -6.0, 6.0), jnp.clip(index, -6.0, 6.0))


def draw_picks(key, part):
    return pick_blocks(key)


def draw_latent_keys(key, part):
    return key_fields(key)[0].astype(jnp.bfloat16)


def draw_index_keys(key, part):
    return key_fields(key)[1].astype(jnp.bfloat16)


def draw_queries(key, part):
    key = jax.random.fold_in(key, 21)
    return jnp.clip(0.5 * jax.random.normal(key, (NQ, H, KDIM), jnp.float32), -3.0, 3.0).astype(jnp.bfloat16)


def draw_index_queries(key, part):
    key = jax.random.fold_in(key, 22)
    return jnp.clip(jax.random.normal(key, (NQ, HI, ID), jnp.float32), -6.0, 6.0).astype(jnp.bfloat16)


def shard_levels(own_key, extent, shards, smallest, high):
    def one(dim, blocks):
        heights = jax.random.uniform(jax.random.fold_in(jax.random.fold_in(own_key, 6), dim), (blocks,), jnp.float32, smallest / len(shards), high / len(shards))
        return jnp.repeat(jnp.exp(heights), extent[dim] // blocks).reshape((-1,) + (1,) * (len(extent) - dim - 1))

    level = one(*shards[0])
    for cut in shards[1:]:
        level = level * one(*cut)
    return level


def bell_draw(own_key, extent, scale, bound, cuts=(), held_as=jnp.bfloat16):
    drawn = jax.random.normal(own_key, extent, jnp.float32) * scale
    if len(cuts) > 0:
        drawn = shard_levels(own_key, extent, cuts, -0.22, 0.18) * drawn
    return jnp.clip(drawn, min=-bound, max=bound).astype(held_as)


def setup_inputs(seed: int = 0) -> dict:
    seeds = jax.random.split(jax.random.key(seed), 8)
    return {
        "queries": draw_queries(jax.random.fold_in(seeds[7], 71), 0),
        "out_grad": bell_draw(seeds[1], (NQ, H, LATENT), 4.0, 24.0, ((0, 16), (1, 8))),
        "latent_keys": draw_latent_keys(jax.random.fold_in(seeds[7], 71), 0),
        "index_queries": draw_index_queries(jax.random.fold_in(seeds[7], 71), 0),
        "index_weights": jnp.clip(jnp.exp(math.log(16.0) - 2.7725887 * jax.random.uniform(seeds[4], (NQ, HI), jnp.float32) ** shard_levels(seeds[4], (NQ, HI), ((0, 16), (1, 8)), -0.2, 0.2)), 1.0, 16.0),
        "index_keys": draw_index_keys(jax.random.fold_in(seeds[7], 71), 0),
        "picks": draw_picks(jax.random.fold_in(seeds[7], 71), 0),
    }


ATTN_SCALE = 0.1353

def lower(values):
    rounded = lax.optimization_barrier(values.astype(jnp.bfloat16))
    return rounded.astype(jnp.float32)

def tile_terms(tile_query, tile_grad, tile_index, tile_weight, latent_pick, index_pick):
    query_wide = tile_query.astype(jnp.float32)
    keys_wide = latent_pick.astype(jnp.float32)
    grad_wide = tile_grad.astype(jnp.float32)
    scores = ATTN_SCALE * jnp.einsum('qhd,kd->qhk', query_wide, keys_wide)
    attn_probs = jax.nn.softmax(scores, axis=-1)
    dprobs = jnp.einsum('qhv,kv->qhk', grad_wide, keys_wide[:, :LATENT])
    rowdot = lax.optimization_barrier(jnp.sum(attn_probs * dprobs, axis=-1, keepdims=True))
    dscore = lower(attn_probs * (dprobs - rowdot))
    query_grad = (ATTN_SCALE * jnp.einsum('qhk,kd->qhd', dscore, keys_wide)).astype(jnp.bfloat16)
    key_part = ATTN_SCALE * jnp.einsum('qhk,qhd->kd', dscore, query_wide)
    value_part = jnp.einsum('qhk,qhv->kv', lower(attn_probs), grad_wide)
    key_part = key_part + jnp.pad(value_part, ((0, 0), (0, ROPE)))
    target = lax.optimization_barrier(jnp.sum(attn_probs, axis=1)) / H
    index_wide = tile_index.astype(jnp.float32)
    ikeys_wide = index_pick.astype(jnp.float32)
    index_scale = 1.0 / math.sqrt(ID * HI)
    index_sim = jnp.einsum('qjd,kd->qjk', index_wide, ikeys_wide)
    active = jnp.maximum(index_sim, 0.0)
    logits = index_scale * lax.optimization_barrier(jnp.sum(tile_weight[:, :, None] * active, axis=1))
    dlogit = jax.nn.softmax(logits, axis=-1) - target
    index_dsim = lower(jnp.where(index_sim > 0, index_scale * dlogit[:, None, :] * tile_weight[:, :, None], 0.0))
    index_query_grad = jnp.einsum('qjk,kd->qjd', index_dsim, ikeys_wide)
    index_weight_grad = index_scale * lax.optimization_barrier(jnp.sum(dlogit[:, None, :] * active, axis=2))
    index_part = jnp.einsum('qjk,qjd->kd', index_dsim, index_wide)
    return (query_grad, key_part, index_query_grad, index_weight_grad, index_part)

def reference(queries, out_grad, latent_keys, index_queries, index_weights, index_keys, picks):
    tile_count = NQ // Q_DEV

    def tile_step(running, inputs):
        latent_sum, index_sum = running
        tile_query, tile_grad, tile_index, tile_weight, tile_pick = inputs
        latent_pick = jnp.take(latent_keys, tile_pick, axis=0).reshape(TOPB * BLOCK, KDIM)
        index_pick = jnp.take(index_keys, tile_pick, axis=0).reshape(TOPB * BLOCK, ID)
        query_grad, key_part, index_query_grad, index_weight_grad, index_part = tile_terms(tile_query, tile_grad, tile_index, tile_weight, latent_pick, index_pick)
        latent_sum = latent_sum.at[tile_pick].add(key_part.reshape(TOPB, BLOCK, KDIM))
        index_sum = index_sum.at[tile_pick].add(index_part.reshape(TOPB, BLOCK, ID))
        return ((latent_sum, index_sum), (query_grad, index_query_grad, index_weight_grad))
    start = (jnp.zeros((KEYS // BLOCK, BLOCK, KDIM), jnp.float32), jnp.zeros((KEYS // BLOCK, BLOCK, ID), jnp.float32))
    inputs = (queries.reshape(tile_count, Q_DEV, H, KDIM), out_grad.reshape(tile_count, Q_DEV, H, LATENT), index_queries.reshape(tile_count, Q_DEV, HI, ID), index_weights.reshape(tile_count, Q_DEV, HI), picks.astype(jnp.int32))
    (latent_key_grad, index_key_grad), stacked = lax.scan(tile_step, start, inputs)
    query_grad = stacked[0].reshape(NQ, H, KDIM)
    index_query_grad = stacked[1].reshape(NQ, HI, ID)
    index_weight_grad = stacked[2].reshape(NQ, HI)
    return (query_grad, latent_key_grad, index_query_grad, index_weight_grad, index_key_grad)
```

```python
import math

import jax
import jax.numpy as jnp
from jax import lax
from jax.experimental import pallas as pl
from jax.experimental.pallas import tpu as pltpu
from jax.sharding import PartitionSpec as P

H = 128
HI = 64
ID = 128
CAP = 2
LAT = 512
KD = 576
ATTN_SCALE = 0.1353
INDEX_SCALE = 1.0 / math.sqrt(ID * HI)
LOG2E = 1.4426950408889634

MESH = pl.DeviceIdType.MESH
F32 = jnp.float32
BF16 = jnp.bfloat16

NK = 16
NS = 8
NZ = 4
SUB = 16
PICKS = 16
CH = PICKS * SUB
KEYS = NS * CH
ROWS = 2048
QT = 128
HL = 16
JL = 8
QL = 16
SLOT = CAP * SUB
W = 768
IO = 640
R = 256
KC = 256


def dot(a, b):
    return jnp.dot(a, b, preferred_element_type=F32)


def dot_nt(a, b):
    return lax.dot_general(a, b, (((1,), (1,)), ((), ())), preferred_element_type=F32)


def onehot(index, shape, axis):
    hit = lax.broadcasted_iota(jnp.int32, shape, axis) == index
    return jnp.where(hit, 1.0, 0.0).astype(BF16)


def kernel(
    q_hbm, do_hbm, lat_hbm, iq_hbm, iw_hbm, idx_hbm, slot_col, slot_row, pick_col, pick_row,
    dq_out, dlat_out, diq_out, diw_out, didx_out,
    qv, dov, xl, xi, sendb, recvb, kb, kt, pt, dst, sv, dpv, dqv,
    iqr, iwr, massv, mcr, mzs, mzr, dlv, wv, dsv, iqt, diqs, diws,
    gs, gown, gcr, gzs, gzr, hs, hown, hcr, hzs, hzr, ob, orx, hb, hrx, dlat_v, didx_v,
    ld_sem, iq_ss, iq_rs, iw_ss, iw_rs, xs_ss, xs_rs, ag_ss, ag_rs, dq_sem,
    m_ss, m_rs, mz_ss, mz_rs, g_ss, g_rs, gz_ss, gz_rs, h_ss, h_rs, hz_ss, hz_rs,
    o_ss, o_rs, p_ss, p_rs, b_ss, b_rs, v_ss, v_rs, fin_sem,
):
    me_k = lax.axis_index("sk")
    me_s = lax.axis_index("sq")
    z = lax.div(me_s, 2)
    c = lax.rem(me_s, 2)
    zp = lax.rem(z + 1, NZ)
    zo = lax.rem(z + 2, NZ)
    zm = lax.rem(z + 3, NZ)
    mate = z * 2 + (1 - c)

    def send(src, dst_ref, ss, rs, sk, sq):
        copy = pltpu.make_async_remote_copy(
            src_ref=src, dst_ref=dst_ref, send_sem=ss, recv_sem=rs,
            device_id=(sq, sk), device_id_type=MESH,
        )
        copy.start()
        return copy

    def arrived(dst_ref, ss, rs):
        pltpu.make_async_remote_copy(
            src_ref=dst_ref, dst_ref=dst_ref, send_sem=ss, recv_sem=rs,
            device_id=(mate, me_k), device_id_type=MESH,
        ).wait_recv()

    def peer_k(d):
        return lax.rem(me_k + d, NK)

    def from_k(d):
        return lax.rem(me_k + NK - d, NK)

    def peer_s(d):
        return lax.rem(me_s + d, NS)

    def from_s(d):
        return lax.rem(me_s + NS - d, NS)

    def rows(ref, at, count):
        return ref.at[pl.ds(pl.multiple_of(at * count, count), count)]

    sub = pl.ds(pl.multiple_of(me_s * SUB, SUB), SUB)
    loads = [
        pltpu.make_async_copy(lat_hbm.at[:, sub, :], xl, ld_sem.at[0]),
        pltpu.make_async_copy(idx_hbm.at[:, sub, :], xi, ld_sem.at[1]),
        pltpu.make_async_copy(rows(iq_hbm, me_s, QL * JL), iqr.at[me_s], ld_sem.at[2]),
        pltpu.make_async_copy(rows(iw_hbm, me_s, QL), iwr.at[me_s], ld_sem.at[3]),
        pltpu.make_async_copy(q_hbm, qv, ld_sem.at[4]),
        pltpu.make_async_copy(do_hbm, dov, ld_sem.at[5]),
    ]
    for load in loads:
        load.start()

    barrier = pltpu.get_barrier_semaphore()

    def greet_k(d, carry):
        pl.semaphore_signal(barrier, inc=1, device_id=(me_s, peer_k(d)), device_id_type=MESH)
        return carry

    def greet_s(d, carry):
        pl.semaphore_signal(barrier, inc=1, device_id=(peer_s(d), me_k), device_id_type=MESH)
        return carry

    lax.fori_loop(1, NK, greet_k, 0)
    lax.fori_loop(1, NS, greet_s, 0)
    pl.semaphore_wait(barrier, NK - 1 + NS - 1)

    loads[0].wait()
    loads[1].wait()
    pack = onehot(slot_col[...], (NK * SLOT, CH), 1)
    sendb[:, 0:KD] = dot(pack, xl[...].reshape(CH, KD)).astype(BF16)
    sendb[:, KD:IO] = jnp.zeros((NK * SLOT, IO - KD), BF16)
    sendb[:, IO:W] = dot(pack, xi[...].reshape(CH, ID)).astype(BF16)

    def ship(d, carry):
        send(rows(sendb, peer_k(d), SLOT), rows(recvb, me_k, SLOT), xs_ss.at[d], xs_rs.at[d], peer_k(d), me_s)
        return carry

    lax.fori_loop(1, NK, ship, 0)
    own = pl.ds(pl.multiple_of(me_k * SLOT, SLOT), SLOT)
    recvb[own, :] = sendb[own, :]

    def ship_iq(d, carry):
        send(rows(iq_hbm, peer_s(d), QL * JL), iqr.at[me_s], iq_ss.at[d], iq_rs.at[d], me_k, peer_s(d))
        send(rows(iw_hbm, peer_s(d), QL), iwr.at[me_s], iw_ss.at[d], iw_rs.at[d], me_k, peer_s(d))
        return carry

    lax.fori_loop(1, NS, ship_iq, 0)

    def landed(d, carry):
        arrived(rows(recvb, from_k(d), SLOT), xs_ss.at[d], xs_rs.at[d])
        return carry

    lax.fori_loop(1, NK, landed, 0)
    keep = onehot(pick_col[...], (CH, NK * SLOT), 1)
    mine = pl.ds(pl.multiple_of(me_s * CH, CH), CH)
    kb[mine, :] = dot(keep, recvb[...]).astype(BF16)

    fwd_from = jnp.where(c == 0, zm, zp)
    fwd_to = jnp.where(c == 0, zp, zm)

    def pass_on(chunk, lane, sq):
        return send(rows(kb, chunk, CH), rows(kb, chunk, CH), ag_ss.at[lane], ag_rs.at[chunk], me_k, sq)

    def chunk_here(chunk):
        arrived(rows(kb, chunk, CH), ag_ss.at[0], ag_rs.at[chunk])

    out = [
        pass_on(me_s, 0, zp * 2 + c),
        pass_on(me_s, 1, zm * 2 + c),
        pass_on(me_s, 2, mate),
    ]
    chunk_here(fwd_from * 2 + c)
    out.append(pass_on(fwd_from * 2 + c, 3, fwd_to * 2 + c))
    out.append(pass_on(fwd_from * 2 + c, 4, mate))
    chunk_here(fwd_to * 2 + c)
    out.append(pass_on(fwd_to * 2 + c, 5, mate))
    chunk_here(zo * 2 + c)
    out.append(pass_on(zo * 2 + c, 6, mate))
    for other in (z, fwd_from, fwd_to, zo):
        chunk_here(other * 2 + (1 - c))
    for copy in out:
        copy.wait_send()

    def sent_k(d, carry):
        pltpu.make_async_remote_copy(
            src_ref=rows(sendb, peer_k(d), SLOT), dst_ref=rows(recvb, me_k, SLOT),
            send_sem=xs_ss.at[d], recv_sem=xs_rs.at[d], device_id=(me_s, peer_k(d)), device_id_type=MESH,
        ).wait_send()
        return carry

    lax.fori_loop(1, NK, sent_k, 0)

    for at in range(0, KEYS, KC):
        kt[:, at:at + KC] = kb[at:at + KC, 0:IO].T
    loads[4].wait()
    loads[5].wait()
    c2 = ATTN_SCALE * LOG2E

    def attend(step, carry):
        at = pl.ds(pl.multiple_of(step * R, R), R)
        q = qv[at, :]
        do = dov[at, :]
        top = jnp.full((8, R), -jnp.inf, F32)
        for k in range(0, KEYS, KC):
            s = dot_nt(kb[k:k + KC, 0:KD], q)
            sv[k:k + KC, :] = s
            top = jnp.maximum(top, jnp.max(s.reshape(KC // 8, 8, R), axis=0))
        top = jnp.max(top, axis=0, keepdims=True) * c2
        total = jnp.zeros((8, R), F32)
        dotted = jnp.zeros((8, R), F32)
        for k in range(0, KEYS, KC):
            dp = dot_nt(kb[k:k + KC, 0:LAT], do)
            e = jnp.exp2(sv[k:k + KC, :] * c2 - top)
            sv[k:k + KC, :] = e
            dpv[k:k + KC, :] = dp
            total = total + jnp.sum(e.reshape(KC // 8, 8, R), axis=0)
            dotted = dotted + jnp.sum((e * dp).reshape(KC // 8, 8, R), axis=0)
        scale = 1.0 / jnp.sum(total, axis=0, keepdims=True)
        rowdot = jnp.sum(dotted, axis=0, keepdims=True) * scale
        for k in range(0, KEYS, KC):
            p = sv[k:k + KC, :] * scale
            pt[k:k + KC, at] = p.astype(BF16)
            dst[k:k + KC, at] = (p * (dpv[k:k + KC, :] - rowdot)).astype(BF16)
        dq = dot(kt[...], dst[:, at]) * ATTN_SCALE
        dqv[at, :] = dq.T[:, 0:KD].astype(BF16)
        pltpu.make_async_copy(dqv.at[at], dq_out.at[at], dq_sem.at[step]).start()
        return carry

    lax.fori_loop(0, ROWS // R, attend, 0)

    same_query = lax.div(lax.broadcasted_iota(jnp.int32, (QT, ROWS), 1), HL) == lax.broadcasted_iota(
        jnp.int32, (QT, ROWS), 0
    )
    pool = jnp.where(same_query, 1.0, 0.0).astype(BF16)
    for k in range(0, KEYS, KC):
        massv[:, k:k + KC] = dot_nt(pool, pt[k:k + KC, :])

    def mass_pair(i, carry):
        send(rows(massv, 2 * i + (1 - c), QL), mcr.at[i], m_ss.at[i], m_rs.at[i], me_k, mate)
        return carry

    lax.fori_loop(0, NZ, mass_pair, 0)

    def mass_sum(d):
        there = lax.rem(z + d, NZ)
        arrived(mcr.at[there], m_ss.at[there], m_rs.at[there])
        return massv[pl.ds(pl.multiple_of((2 * there + c) * QL, QL), QL), :] + mcr[there]

    for d in (2, 1, 3):
        mzs[d] = mass_sum(d)
        send(mzs.at[d], mzr.at[d], mz_ss.at[d], mz_rs.at[d], me_k, lax.rem(z + d, NZ) * 2 + c)
    mzs[0] = mass_sum(0)

    def key_grad(chunk):
        at = pl.ds(pl.multiple_of(chunk * CH, CH), CH)
        both = dot(dst[at, :], qv[...]) * ATTN_SCALE
        value = dot(pt[at, :], dov[...])
        return both[:, 0:LAT] + value, both[:, LAT:KD]

    def pair_chunk(i, carry):
        there = lax.rem(z + 2 + i, NZ)
        main, rope = key_grad(2 * there + (1 - c))
        gs[there, :, 0:LAT] = main.astype(BF16)
        gs[there, :, LAT:KD] = rope.astype(BF16)
        send(gs.at[there], gcr.at[there], g_ss.at[there], g_rs.at[there], me_k, mate)
        return carry

    lax.fori_loop(0, NZ, pair_chunk, 0)

    def own_chunk(i, carry):
        there = lax.rem(z + 2 + i, NZ)
        main, rope = key_grad(2 * there + c)
        arrived(gcr.at[there], g_ss.at[there], g_rs.at[there])
        gown[:, 0:LAT] = main + gcr[there, :, 0:LAT].astype(F32)
        gown[:, LAT:KD] = rope + gcr[there, :, LAT:KD].astype(F32)

        @pl.when(i != 2)
        def _():
            gzs[there] = gown[...].astype(BF16)
            send(gzs.at[there], gzr.at[z], gz_ss.at[there], gz_rs.at[z], me_k, there * 2 + c)

        @pl.when(i == 2)
        def _():
            hown[...] = gown[...]

        return carry

    lax.fori_loop(0, NZ, own_chunk, 0)

    loads[2].wait()
    loads[3].wait()

    def iq_here(d, carry):
        arrived(iqr.at[from_s(d)], iq_ss.at[d], iq_rs.at[d])
        arrived(iwr.at[from_s(d)], iw_ss.at[d], iw_rs.at[d])
        return carry

    lax.fori_loop(1, NS, iq_here, 0)
    eye = lax.broadcasted_iota(jnp.int32, (JL, 128), 0) == lax.broadcasted_iota(jnp.int32, (JL, 128), 1)
    eye8 = lax.broadcasted_iota(jnp.int32, (JL, JL), 0) == lax.broadcasted_iota(jnp.int32, (JL, JL), 1)

    dlv[...] = jnp.zeros_like(dlv)

    def logit_part(src, carry):
        weight = jnp.where(eye8[None], iwr[src][:, None, :], 0.0)
        weight = jnp.sum(weight, axis=2, keepdims=True).reshape(QL * JL, 1)
        wv[src] = jnp.broadcast_to(weight, (QL * JL, 128))
        sim = dot_nt(iqr[src], kb[:, IO:W])
        dlv[...] += jnp.maximum(sim, 0.0) * weight
        iqt[:, pl.ds(pl.multiple_of(src * 128, 128), 128)] = iqr[src].T
        return carry

    lax.fori_loop(0, NS, logit_part, 0)
    logits = INDEX_SCALE * jnp.sum(dlv[...].reshape(QL, JL, KEYS), axis=1)
    e = jnp.exp(logits - jnp.max(logits, axis=1, keepdims=True))
    guess = e / jnp.sum(e, axis=1, keepdims=True)
    mass = mzs[0]
    for d in (1, 2, 3):
        arrived(mzr.at[d], mz_ss.at[d], mz_rs.at[d])
        mass = mass + mzr[d]
    dlogit = INDEX_SCALE * (guess - mass * (1.0 / H))
    dlv[...] = jnp.broadcast_to(dlogit[:, None, :], (QL, JL, KEYS)).reshape(QL * JL, KEYS)

    def index_part(src, carry):
        sim = dot_nt(iqr[src], kb[:, IO:W])
        dl = dlv[...]
        ds = jnp.where(sim > 0, dl * wv[src][:, 0:1], 0.0).astype(BF16)
        dsv[pl.ds(pl.multiple_of(src * 128, 128), 128), :] = ds
        dw = jnp.sum(dl * jnp.maximum(sim, 0.0), axis=1, keepdims=True).reshape(QL, JL, 1)
        diws[src] = jnp.sum(jnp.where(eye[None], dw, 0.0), axis=1)[:, 0:JL]
        diqs[src] = dot(ds, kb[:, IO:W])
        return carry

    lax.fori_loop(0, NS, index_part, 0)

    def ship_grads(d, carry):
        there = peer_s(d)
        send(diqs.at[there], rows(diq_out, me_s, QL * JL), b_ss.at[d], b_rs.at[d], me_k, there)
        send(diws.at[there], rows(diw_out, me_s, QL), v_ss.at[d], v_rs.at[d], me_k, there)
        return carry

    lax.fori_loop(1, NS, ship_grads, 0)
    here_iq = pltpu.make_async_copy(diqs.at[me_s], rows(diq_out, me_s, QL * JL), fin_sem.at[0])
    here_iw = pltpu.make_async_copy(diws.at[me_s], rows(diw_out, me_s, QL), fin_sem.at[1])
    here_iq.start()
    here_iw.start()

    expand = onehot(pick_row[...], (NK * SLOT, CH), 0)
    home = onehot(slot_row[...], (CH, NK * SLOT), 0)

    def ship_home(buf, got, ss, rs):
        def one(d, carry):
            send(rows(buf, peer_k(d), SLOT), rows(got, me_k, SLOT), ss.at[d], rs.at[d], peer_k(d), me_s)
            return carry

        lax.fori_loop(1, NK, one, 0)
        got[own, :] = buf[own, :]

    def all_home(got, ss, rs):
        def one(d, carry):
            arrived(rows(got, from_k(d), SLOT), ss.at[d], rs.at[d])
            return carry

        lax.fori_loop(1, NK, one, 0)

    def all_sent(buf, got, ss, rs):
        def one(d, carry):
            pltpu.make_async_remote_copy(
                src_ref=rows(buf, peer_k(d), SLOT), dst_ref=rows(got, me_k, SLOT),
                send_sem=ss.at[d], recv_sem=rs.at[d], device_id=(me_s, peer_k(d)), device_id_type=MESH,
            ).wait_send()
            return carry

        lax.fori_loop(1, NK, one, 0)

    acc = hown[...]
    for other in (zp, zm, zo):
        arrived(gzr.at[other], gz_ss.at[other], gz_rs.at[other])
        acc = acc + gzr[other].astype(F32)
    ob[...] = dot(expand, acc.astype(BF16)).astype(BF16)
    ship_home(ob, orx, o_ss, o_rs)

    for k in range(0, KEYS, KC):
        part = dot(iqt[...], dsv[:, k:k + KC])
        sv[k:k + KC, 0:ID] = part.T

    def pair_index(i, carry):
        there = lax.rem(z + 2 + i, NZ)
        at = pl.ds(pl.multiple_of((2 * there + (1 - c)) * CH, CH), CH)
        hs[there] = sv[at, 0:ID].astype(BF16)
        send(hs.at[there], hcr.at[there], h_ss.at[there], h_rs.at[there], me_k, mate)
        return carry

    lax.fori_loop(0, NZ, pair_index, 0)

    def index_sum(there):
        at = pl.ds(pl.multiple_of((2 * there + c) * CH, CH), CH)
        arrived(hcr.at[there], h_ss.at[there], h_rs.at[there])
        return sv[at, 0:ID] + hcr[there].astype(F32)

    for there in (zo, zp, zm):
        hzs[there] = index_sum(there).astype(BF16)
        send(hzs.at[there], hzr.at[z], hz_ss.at[there], hz_rs.at[z], me_k, there * 2 + c)
    acc = index_sum(z)
    for other in (zp, zm, zo):
        arrived(hzr.at[other], hz_ss.at[other], hz_rs.at[other])
        acc = acc + hzr[other].astype(F32)
    hb[...] = dot(expand, acc.astype(BF16)).astype(BF16)
    ship_home(hb, hrx, p_ss, p_rs)

    all_home(orx, o_ss, o_rs)
    dlat_v[...] = dot(home, orx[...]).reshape(NK, SUB, KD)
    out_lat = pltpu.make_async_copy(dlat_v, dlat_out, fin_sem.at[2])
    out_lat.start()
    all_home(hrx, p_ss, p_rs)
    didx_v[...] = dot(home, hrx[...]).reshape(NK, SUB, ID)
    out_idx = pltpu.make_async_copy(didx_v, didx_out, fin_sem.at[3])
    out_idx.start()

    def grads_here(d, carry):
        arrived(rows(diq_out, from_s(d), QL * JL), b_ss.at[d], b_rs.at[d])
        arrived(rows(diw_out, from_s(d), QL), v_ss.at[d], v_rs.at[d])
        return carry

    lax.fori_loop(1, NS, grads_here, 0)

    def sent_s(d, carry):
        def gone(src, dst_ref, ss, rs):
            pltpu.make_async_remote_copy(
                src_ref=src, dst_ref=dst_ref, send_sem=ss.at[d], recv_sem=rs.at[d],
                device_id=(peer_s(d), me_k), device_id_type=MESH,
            ).wait_send()

        gone(rows(iq_hbm, peer_s(d), QL * JL), iqr.at[me_s], iq_ss, iq_rs)
        gone(rows(iw_hbm, peer_s(d), QL), iwr.at[me_s], iw_ss, iw_rs)
        gone(diqs.at[peer_s(d)], rows(diq_out, me_s, QL * JL), b_ss, b_rs)
        gone(diws.at[peer_s(d)], rows(diw_out, me_s, QL), v_ss, v_rs)
        return carry

    lax.fori_loop(1, NS, sent_s, 0)

    def gone(src, dst_ref, ss, rs):
        pltpu.make_async_remote_copy(
            src_ref=src, dst_ref=dst_ref, send_sem=ss, recv_sem=rs,
            device_id=(mate, me_k), device_id_type=MESH,
        ).wait_send()

    def sent_z(i, carry):
        gone(rows(massv, 2 * i + (1 - c), QL), mcr.at[i], m_ss.at[i], m_rs.at[i])
        gone(gs.at[i], gcr.at[i], g_ss.at[i], g_rs.at[i])
        gone(hs.at[i], hcr.at[i], h_ss.at[i], h_rs.at[i])
        return carry

    lax.fori_loop(0, NZ, sent_z, 0)
    for d in (1, 2, 3):
        there = lax.rem(z + d, NZ)
        gone(mzs.at[d], mzr.at[d], mz_ss.at[d], mz_rs.at[d])
        gone(gzs.at[there], gzr.at[z], gz_ss.at[there], gz_rs.at[z])
        gone(hzs.at[there], hzr.at[z], hz_ss.at[there], hz_rs.at[z])
    all_sent(ob, orx, o_ss, o_rs)
    all_sent(hb, hrx, p_ss, p_rs)

    def dq_done(step, carry):
        at = pl.ds(pl.multiple_of(step * R, R), R)
        pltpu.make_async_copy(dqv.at[at], dq_out.at[at], dq_sem.at[step]).wait()
        return carry

    lax.fori_loop(0, ROWS // R, dq_done, 0)
    here_iq.wait()
    here_iw.wait()
    out_lat.wait()
    out_idx.wait()


def body(queries, out_grad, latent_keys, index_queries, index_weights, index_keys, picks):
    my_column = lax.axis_index("sk")
    owner = picks // NK
    local = picks % NK
    place = jnp.arange(PICKS, dtype=jnp.int32)
    rank = jnp.sum((owner[:, :, None] == owner[:, None, :]) & (place[None, :] < place[:, None])[None], axis=2)
    slot = owner * CAP + rank
    mine = lax.dynamic_index_in_dim(slot, my_column, 0, keepdims=False)
    row = jnp.arange(SUB, dtype=jnp.int32)
    pick_at = (mine[:, None] * SUB + row).reshape(-1)
    hit = slot[:, None, :] == (my_column * CAP + jnp.arange(CAP, dtype=jnp.int32))[None, :, None]
    block = jnp.sum(jnp.where(hit, local[:, None, :] + 1, 0), axis=2) - 1
    slot_at = jnp.where(block[:, :, None] >= 0, block[:, :, None] * SUB + row, -1).reshape(-1)

    hbm = pl.BlockSpec(memory_space=pl.ANY)
    vmem = pl.BlockSpec(memory_space=pltpu.VMEM)
    dma = pltpu.SemaphoreType.DMA
    v = pltpu.VMEM
    outs = pl.pallas_call(
        kernel,
        out_shape=[
            jax.ShapeDtypeStruct((ROWS, KD), BF16),
            jax.ShapeDtypeStruct((NK, SUB, KD), F32),
            jax.ShapeDtypeStruct((QT * JL, ID), F32),
            jax.ShapeDtypeStruct((QT, JL), F32),
            jax.ShapeDtypeStruct((NK, SUB, ID), F32),
        ],
        in_specs=[hbm] * 6 + [vmem] * 4,
        out_specs=[hbm] * 5,
        scratch_shapes=[
            v((ROWS, KD), BF16), v((ROWS, LAT), BF16),
            v((NK, SUB, KD), BF16), v((NK, SUB, ID), BF16),
            v((NK * SLOT, W), BF16), v((NK * SLOT, W), BF16), v((KEYS, W), BF16),
            v((IO, KEYS), BF16), v((KEYS, ROWS), BF16), v((KEYS, ROWS), BF16),
            v((KEYS, R), F32), v((KEYS, R), F32), v((ROWS, KD), BF16),
            v((NS, QL * JL, ID), BF16), v((NS, QL, JL), F32),
            v((QT, KEYS), F32), v((NZ, QL, KEYS), F32), v((NZ, QL, KEYS), F32), v((NZ, QL, KEYS), F32),
            v((QL * JL, KEYS), F32), v((NS, QL * JL, 128), F32),
            v((NS * QL * JL, KEYS), BF16), v((ID, NS * QL * JL), BF16),
            v((NS, QL * JL, ID), F32), v((NS, QL, JL), F32),
            v((NZ, CH, KD), BF16), v((CH, KD), F32), v((NZ, CH, KD), BF16),
            v((NZ, CH, KD), BF16), v((NZ, CH, KD), BF16),
            v((NZ, CH, ID), BF16), v((CH, KD), F32), v((NZ, CH, ID), BF16),
            v((NZ, CH, ID), BF16), v((NZ, CH, ID), BF16),
            v((NK * SLOT, KD), BF16), v((NK * SLOT, KD), BF16),
            v((NK * SLOT, ID), BF16), v((NK * SLOT, ID), BF16),
            v((NK, SUB, KD), F32), v((NK, SUB, ID), F32),
            dma((6,)), dma((NS,)), dma((NS,)), dma((NS,)), dma((NS,)),
            dma((NK,)), dma((NK,)), dma((NS,)), dma((NS,)), dma((NS,)),
            dma((NZ,)), dma((NZ,)), dma((NZ,)), dma((NZ,)),
            dma((NZ,)), dma((NZ,)), dma((NZ,)), dma((NZ,)),
            dma((NZ,)), dma((NZ,)), dma((NZ,)), dma((NZ,)),
            dma((NK,)), dma((NK,)), dma((NK,)), dma((NK,)),
            dma((NS,)), dma((NS,)), dma((NS,)), dma((NS,)), dma((4,)),
        ],
        compiler_params=pltpu.CompilerParams(
            collective_id=0, has_side_effects=True, vmem_limit_bytes=63 * 1024 * 1024
        ),
        name="sparse_attention_backward",
    )(
        queries.reshape(ROWS, KD),
        out_grad.reshape(ROWS, LAT),
        latent_keys,
        index_queries.reshape(QT * JL, ID),
        index_weights,
        index_keys,
        slot_at[:, None],
        slot_at[None, :],
        pick_at[:, None],
        pick_at[None, :],
    )
    dq, dlat, diq, diw, didx = outs
    return (dq.reshape(QT, HL, KD), dlat, diq.reshape(QT, JL, ID), diw, didx)


def solution(mesh):
    placed = (
        P("sk", "sq", None),
        P("sk", "sq", None),
        P("sk", None, None),
        P("sk", "sq", None),
        P("sk", "sq"),
        P("sk", None, None),
        P(),
    )
    return jax.shard_map(
        body,
        mesh=mesh,
        in_specs=placed,
        out_specs=(
            P("sk", "sq", None),
            P("sk", "sq", None),
            P("sk", "sq", None),
            P("sk", "sq"),
            P("sk", "sq", None),
        ),
        check_vma=False,
    )
```

```python
import math

import jax
import jax.numpy as jnp
from jax import lax
from jax.experimental import pallas as pl
from jax.experimental.pallas import tpu as pltpu
from jax.sharding import PartitionSpec as P

H = 128
HI = 64
ID = 128
CAP = 2
LAT = 512
KD = 576
ATTN_SCALE = 0.1353
INDEX_SCALE = 1.0 / math.sqrt(ID * HI)
LOG2E = 1.4426950408889634

MESH = pl.DeviceIdType.MESH
F32 = jnp.float32
BF16 = jnp.bfloat16

NK = 16
NS = 8
NZ = 4
SUB = 16
PICKS = 16
CH = PICKS * SUB
KEYS = NS * CH
QT = 128
HL = 16
ROWS = HL * QT
JL = 8
QL = 16
QJ = QL * JL
SLOTS = NK * CAP
W = 768
IO = 640
GW = 256
GROUPS = 3
R = 256
KC = 256


def dot(a, b):
    return jnp.dot(a, b, preferred_element_type=F32)


def dot_nt(a, b):
    return lax.dot_general(a, b, (((1,), (1,)), ((), ())), preferred_element_type=F32)


def dot_tn(a, b):
    return lax.dot_general(a, b, (((0,), (0,)), ((), ())), preferred_element_type=F32)


def iota(shape, axis):
    return lax.broadcasted_iota(jnp.int32, shape, axis)


def ones_where(hit):
    return jnp.where(hit, 1.0, 0.0).astype(BF16)


def kernel(
    q_hbm, do_hbm, lat_hbm, iq_hbm, iw_hbm, idx_hbm, picks,
    dq_out, dlat_out, diq_out, diw_out, didx_out,
    qt, dov, xi, xs, sendb, recvb, kb, to_slot, to_block, sv, pt, dst, dqv, topv, totv, dotv,
    iqr, iwr, wv, lgv, masst, mcr, mzs, mzr, iqt, diws, diwr,
    gs, gcr, gzs, gzr, ob, orx, dlat_v, didx_v, diw_v, found,
    ld_sem, q_sem, lat_sem, iq_ss, iq_rs, iw_ss, iw_rs, xs_ss, xs_rs, ag_ss, ag_rs, dq_sem,
    m_ss, m_rs, mz_ss, mz_rs, g_ss, g_rs, gz_ss, gz_rs, o_ss, o_rs, b_ss, b_rs, v_ss, v_rs, fin_sem,
):
    massq = sv.at[0:QT]
    dlv = sv.at[QT:QT + QJ]
    ikt = sv.at[256:256 + ID]
    gown = sv.at[512:512 + GROUPS * 512, 0:NZ * GW]
    diqs = sv.at[512:512 + NS * QJ, NZ * GW:NZ * GW + ID]

    me_k = lax.axis_index("sk")
    me_s = lax.axis_index("sq")
    z = lax.div(me_s, 2)
    c = lax.rem(me_s, 2)
    zp = lax.rem(z + 1, NZ)
    zo = lax.rem(z + 2, NZ)
    zm = lax.rem(z + 3, NZ)
    mate = z * 2 + (1 - c)

    def remote(src, dst_ref, ss, rs, sk, sq):
        return pltpu.make_async_remote_copy(
            src_ref=src, dst_ref=dst_ref, send_sem=ss, recv_sem=rs,
            device_id=(sq, sk), device_id_type=MESH,
        )

    def send(*what):
        remote(*what).start()

    def gone(src, dst_ref, ss, rs):
        remote(src, dst_ref, ss, rs, me_k, mate).wait_send()

    def arrived(dst_ref, ss, rs):
        remote(dst_ref, dst_ref, ss, rs, me_k, mate).wait_recv()

    def peer_k(d):
        return lax.rem(me_k + d, NK)

    def from_k(d):
        return lax.rem(me_k + NK - d, NK)

    def peer_s(d):
        return lax.rem(me_s + d, NS)

    def from_s(d):
        return lax.rem(me_s + NS - d, NS)

    def span(at, count):
        return pl.ds(pl.multiple_of(at * count, count), count)

    def rows(ref, at, count):
        return ref.at[span(at, count)]

    def loop(lo, hi, step):
        def one(i, carry):
            step(i)
            return carry

        lax.fori_loop(lo, hi, one, 0)

    load_idx = pltpu.make_async_copy(idx_hbm.at[:, span(me_s, SUB), :], xi, ld_sem.at[0])
    load_iq = pltpu.make_async_copy(rows(iq_hbm, me_s, QJ), iqr.at[me_s], ld_sem.at[1])
    load_iw = pltpu.make_async_copy(iw_hbm, iwr.at[me_s], ld_sem.at[2])
    load_do = pltpu.make_async_copy(do_hbm, pt.at[:, 0:LAT], ld_sem.at[3])
    load_lat = [
        pltpu.make_async_copy(lat_hbm.at[b], dst.at[0:KD, b * 128:(b + 1) * 128], lat_sem.at[b]) for b in range(NK)
    ]
    load_q = [pltpu.make_async_copy(q_hbm.at[h], qt.at[:, h * QT:(h + 1) * QT], q_sem.at[h]) for h in range(HL)]
    for load in load_lat + [load_idx]:
        load.start()

    barrier = pltpu.get_barrier_semaphore()

    def greet_k(d):
        pl.semaphore_signal(barrier, inc=1, device_id=(me_s, peer_k(d)), device_id_type=MESH)

    def greet_s(d):
        pl.semaphore_signal(barrier, inc=1, device_id=(peer_s(d), me_k), device_id_type=MESH)

    loop(1, NK, greet_k)
    loop(1, NS, greet_s)

    def picked(t):
        first = jnp.int32(-1)
        second = jnp.int32(-1)
        for p in range(PICKS):
            block = picks[t, p]
            local = block & (NK - 1)
            here = lax.shift_right_logical(block, 4) == me_k
            second = jnp.where(here & (first >= 0), local, second)
            first = jnp.where(here & (first < 0), local, first)
        found[t, 0] = first
        found[t, 1] = second

    loop(0, NK, picked)

    pick_rows = ones_where(iota((SUB, 128), 1) == me_s * SUB + iota((SUB, 128), 0))
    load_idx.wait()
    for b in range(NK):
        load_lat[b].wait()
        xs[b, :, 0:KD] = dot_nt(pick_rows, dst[0:KD, b * 128:(b + 1) * 128]).astype(BF16)
        xs[b, :, KD:IO] = jnp.zeros((SUB, IO - KD), BF16)
        xs[b, :, IO:W] = xi[b]
    cell = iota((SUB, CH), 1) - iota((SUB, CH), 0)

    for load in [load_do] + load_q + [load_iq, load_iw]:
        load.start()

    def pack(t):
        sendb[2 * t] = xs[jnp.maximum(found[t, 0], 0)]
        sendb[2 * t + 1] = xs[jnp.maximum(found[t, 1], 0)]

    loop(0, NK, pack)
    pl.semaphore_wait(barrier, NK - 1 + NS - 1)

    def slots(ref, k):
        return ref.at[pl.ds(2 * k, 2)]

    loop(1, NK, lambda d: send(
        slots(sendb, peer_k(d)), slots(recvb, me_k), xs_ss.at[d], xs_rs.at[d], peer_k(d), me_s))
    recvb[pl.ds(2 * me_k, 2)] = sendb[pl.ds(2 * me_k, 2)]

    def ship_iq(d):
        send(rows(iq_hbm, peer_s(d), QJ), iqr.at[me_s], iq_ss.at[d], iq_rs.at[d], me_k, peer_s(d))
        send(iw_hbm, iwr.at[me_s], iw_ss.at[d], iw_rs.at[d], me_k, peer_s(d))

    loop(1, NS, ship_iq)

    def place(t):
        to_block[span(2 * t, SUB), :] = ones_where(cell == found[t, 0] * SUB)
        to_block[span(2 * t + 1, SUB), :] = ones_where(cell == found[t, 1] * SUB)

    mine = [picks[me_k, p] for p in range(PICKS)]
    owner = [lax.shift_right_logical(block, 4) for block in mine]
    slot = []
    for p in range(PICKS):
        rank = jnp.int32(0)
        for before in range(p):
            rank = rank + jnp.where(owner[before] == owner[p], 1, 0)
        slot.append(owner[p] * CAP + rank)

    def unpick(s):
        pick = jnp.int32(-1)
        for p in range(PICKS):
            pick = jnp.where(slot[p] == s, p, pick)
        to_slot[span(s, SUB), :] = ones_where(cell == pick * SUB)

    loop(0, SLOTS, unpick)
    loop(0, NK, place)
    i0, i1 = iota((CH, CH), 0), iota((CH, CH), 1)
    swap = ones_where(i1 == lax.rem(i0, 16) * 16 + lax.div(i0, 16))
    load_do.wait()
    for g in range(QT // 16):
        turned = dot(swap, pt[g * CH:(g + 1) * CH, 0:LAT]).astype(BF16)
        for h in range(HL):
            dov[h * QT + g * 16:h * QT + (g + 1) * 16, :] = turned[h * 16:(h + 1) * 16]
    for load in load_q:
        load.wait()
    topv[...] = jnp.full(topv.shape, -jnp.inf, F32)
    totv[...] = jnp.zeros_like(totv)
    dotv[...] = jnp.zeros_like(dotv)
    masst[...] = jnp.zeros_like(masst)

    load_iq.wait()
    load_iw.wait()

    def iq_here(d):
        arrived(iqr.at[from_s(d)], iq_ss.at[d], iq_rs.at[d])
        arrived(iwr.at[from_s(d)], iw_ss.at[d], iw_rs.at[d])

    loop(1, NS, iq_here)
    my_query = iota((QL, JL, 128), 2) == me_s * QL + iota((QL, JL, 128), 0)

    def weigh(src):
        weight = jnp.where(my_query, iwr[src][None], 0.0)
        weight = jnp.sum(weight, axis=2, keepdims=True).reshape(QJ, 1)
        wv[src] = jnp.broadcast_to(weight, (QJ, 128))
        iqt[:, span(src, 128)] = iqr[src].T

    loop(0, NS, weigh)

    fwd_from = jnp.where(c == 0, zm, zp)
    fwd_to = jnp.where(c == 0, zp, zm)
    lanes = {}
    c2 = ATTN_SCALE * LOG2E

    def pass_on(chunk, lane, sq):
        lanes[lane] = chunk
        send(rows(kb, chunk, CH), rows(kb, chunk, CH), ag_ss.at[lane], ag_rs.at[chunk], me_k, sq)

    def chunk_here(chunk):
        arrived(rows(kb, chunk, CH), ag_ss.at[0], ag_rs.at[chunk])

    def meet(chunk):
        at = span(chunk, CH)

        for lo in range(0, ROWS, 512):
            lane = slice(lo, lo + 512)
            s = dot(kb[at, 0:KD], qt[:, lane]) * c2
            dp = dot_nt(kb[at, 0:LAT], dov[lane, :])
            sv[at, lane] = s
            s = s.reshape(CH // 8, 8, 512)
            old = topv[:, lane]
            top = jnp.maximum(old, jnp.max(s, axis=0))
            e = jnp.exp2(s - top[None])
            fade = jnp.exp2(old - top)
            topv[:, lane] = top
            totv[:, lane] = totv[:, lane] * fade + jnp.sum(e, axis=0)
            dotv[:, lane] = dotv[:, lane] * fade + jnp.sum(e * dp.reshape(CH // 8, 8, 512), axis=0)

        keys = kb[at, IO:W]
        acc = jnp.zeros((QJ, CH), F32)
        for src in range(NS):
            acc = acc + jnp.maximum(dot_nt(iqr[src], keys), 0.0) * jnp.tile(wv[src], (1, CH // 128))
        lgv[:, at] = INDEX_SCALE * jnp.sum(acc.reshape(QL, JL, CH), axis=1)

    def meet_mate(zz):
        chunk_here(zz * 2 + (1 - c))
        meet(zz * 2 + (1 - c))

    loop(1, NK, lambda d: arrived(slots(recvb, from_k(d)), xs_ss.at[d], xs_rs.at[d]))
    for p in range(PICKS):
        kb[pl.ds(pl.multiple_of(me_s * CH + p * SUB, SUB), SUB), :] = recvb[slot[p]]
    pass_on(me_s, 0, mate)
    pass_on(me_s, 1, fwd_to * 2 + c)
    meet(me_s)
    pass_on(me_s, 2, fwd_from * 2 + c)
    chunk_here(fwd_from * 2 + c)
    pass_on(fwd_from * 2 + c, 3, fwd_to * 2 + c)
    pass_on(fwd_from * 2 + c, 4, mate)
    meet_mate(z)
    meet(fwd_from * 2 + c)
    chunk_here(fwd_to * 2 + c)
    pass_on(fwd_to * 2 + c, 5, mate)
    meet_mate(fwd_to)
    meet(fwd_to * 2 + c)
    chunk_here(zo * 2 + c)
    pass_on(zo * 2 + c, 6, mate)
    meet_mate(fwd_from)
    meet(zo * 2 + c)
    meet_mate(zo)

    def attend(step):
        at = span(step, R)
        do = dov[at, :]
        top = jnp.max(topv[:, at], axis=0, keepdims=True)
        fade = jnp.exp2(topv[:, at] - top)
        total = jnp.sum(totv[:, at] * fade, axis=0, keepdims=True)
        rowdot = jnp.sum(dotv[:, at] * fade, axis=0, keepdims=True) / total
        top = top + jnp.log2(total)
        for k in range(0, KEYS, KC):
            dp = dot_nt(kb[k:k + KC, 0:LAT], do)
            p = jnp.exp2(sv[k:k + KC, at] - top)
            pt[k:k + KC, at] = p.astype(BF16)
            dst[k:k + KC, at] = (p * (dp - rowdot)).astype(BF16)
            heads = p[:, 0:QT]
            for h in range(QT, R, QT):
                heads = heads + p[:, h:h + QT]
            masst[k:k + KC, :] += heads

    loop(0, ROWS // R, attend)

    for k in range(0, KEYS, KC):
        massq[:, k:k + KC] = masst[k:k + KC, :].T

    def mass_pair(i):
        send(rows(massq, 2 * i + (1 - c), QL), mcr.at[i], m_ss.at[i], m_rs.at[i], me_k, mate)

    loop(0, NZ, mass_pair)

    def at_step(i):
        return lax.rem(z + jnp.where(i == 0, 2, jnp.where(i == 1, 1, jnp.where(i == 2, 3, 0))), NZ)

    def key_group(g):
        base = g * 512
        lo = g * GW

        def finish(i):
            there = at_step(i)
            arrived(gcr.at[g, there], g_ss.at[g, there], g_rs.at[g, there])
            own_half = gown[pl.ds(pl.multiple_of(base + c * CH, CH), CH), span(i, GW)]
            gzs[g, there] = (own_half + gcr[g, there].astype(F32)).astype(BF16)
            send(gzs.at[g, there], gzr.at[g, z], gz_ss.at[g, there], gz_rs.at[g, z], me_k, there * 2 + c)

        def step(i):
            there = at_step(i)
            at = span(there, 2 * CH)
            lane = span(i, GW)
            if g < 2:
                gown[base:base + 512, lane] = (
                    dot_nt(dst[at, :], qt[lo:lo + GW, :]) * ATTN_SCALE + dot(pt[at, :], dov[:, lo:lo + GW])
                )
            else:
                rope = dot_nt(dst[at, :], qt[LAT:KD, :]) * ATTN_SCALE
                gown[base:base + 512, lane] = jnp.concatenate(
                    [rope, jnp.zeros((2 * CH, 128 - KD + LAT), F32), masst[at, :]], axis=1
                )
            gs[g, there] = gown[pl.ds(pl.multiple_of(base + (1 - c) * CH, CH), CH), lane].astype(BF16)
            send(gs.at[g, there], gcr.at[g, there], g_ss.at[g, there], g_rs.at[g, there], me_k, mate)

            @pl.when(i >= 1)
            def _():
                finish(i - 1)

        loop(0, NZ, step)

    def ship_home(g):
        arrived(gcr.at[g, z], g_ss.at[g, z], g_rs.at[g, z])
        acc = gown[pl.ds(pl.multiple_of(g * 512 + c * CH, CH), CH), 3 * GW:4 * GW] + gcr[g, z].astype(F32)
        for other in (zp, zm, zo):
            arrived(gzr.at[g, other], gz_ss.at[g, other], gz_rs.at[g, other])
            acc = acc + gzr[g, other].astype(F32)
        ob[g] = dot(to_slot[...], acc.astype(BF16)).astype(BF16)
        loop(1, NK, lambda d: send(
            home_part(ob, g, peer_k(d)), home_part(orx, g, me_k), o_ss.at[g, d], o_rs.at[g, d], peer_k(d), me_s))
        own = span(me_k, CAP * SUB)
        orx[g, own, :] = ob[g, own, :]

    def home_part(ref, g, k):
        return ref.at[g, span(k, CAP * SUB), :]

    key_group(0)
    def mass_sum(d):
        there = lax.rem(z + d, NZ)
        arrived(mcr.at[there], m_ss.at[there], m_rs.at[there])
        return massq[span(2 * there + c, QL), :] + mcr[there]

    for d in (2, 1, 3):
        mzs[d] = mass_sum(d)
        send(mzs.at[d], mzr.at[d], mz_ss.at[d], mz_rs.at[d], me_k, lax.rem(z + d, NZ) * 2 + c)
    mzs[0] = mass_sum(0)

    key_group(1)
    ship_home(0)

    logits = lgv[...]
    e = jnp.exp(logits - jnp.max(logits, axis=1, keepdims=True))
    guess = e / jnp.sum(e, axis=1, keepdims=True)
    mass = mzs[0]
    for d in (1, 2, 3):
        arrived(mzr.at[d], mz_ss.at[d], mz_rs.at[d])
        mass = mass + mzr[d]
    dlogit = INDEX_SCALE * (guess - mass * (1.0 / H))
    dlv[...] = jnp.broadcast_to(dlogit[:, None, :], (QL, JL, KEYS)).reshape(QJ, KEYS)
    ikt[...] = jnp.zeros(ikt.shape, F32)

    def index_part(src):
        sim = dot_nt(iqr[src], kb[:, IO:W])
        dl = dlv[...]
        ds = jnp.where(sim > 0, dl * jnp.tile(wv[src], (1, KEYS // 128)), 0.0).astype(BF16)
        dw = jnp.sum(dl * jnp.maximum(sim, 0.0), axis=1, keepdims=True).reshape(QL, JL, 1)
        diws[src] = jnp.sum(jnp.where(my_query, dw, 0.0), axis=0)
        diqs[span(src, QJ), :] = dot(ds, kb[:, IO:W])
        ikt[...] += dot(iqt[:, span(src, 128)], ds)

    loop(0, NS, index_part)

    def ship_grads(d):
        there = peer_s(d)
        send(rows(diqs, there, QJ), rows(diq_out, me_s, QJ), b_ss.at[d], b_rs.at[d], me_k, there)
        send(diws.at[there], diwr.at[me_s], v_ss.at[d], v_rs.at[d], me_k, there)

    loop(1, NS, ship_grads)
    diwr[me_s] = diws[me_s]
    here_iq = pltpu.make_async_copy(rows(diqs, me_s, QJ), rows(diq_out, me_s, QJ), fin_sem.at[0])
    here_iq.start()

    for k in range(0, KEYS, KC):
        masst[k:k + KC, :] = ikt[:, k:k + KC].T

    ship_home(1)
    key_group(2)

    def dq_copy(head):
        step = lax.div(head, 4)
        lane = span(lax.rem(head, 4), QT)
        return pltpu.make_async_copy(dqv.at[lax.rem(step, 2), :, lane], dq_out.at[head], dq_sem.at[head])

    def query_grad(step):
        at = span(step, 512)
        grad = (dot_tn(kb[:, 0:KD], dst[:, at]) * ATTN_SCALE).astype(BF16)

        @pl.when(step >= 2)
        def _():
            for h in range(4):
                dq_copy((step - 2) * 4 + h).wait()

        dqv[lax.rem(step, 2)] = grad
        for h in range(4):
            dq_copy(step * 4 + h).start()

    loop(0, 2, query_grad)
    ship_home(2)
    loop(2, 4, query_grad)

    def grads_here(d):
        arrived(rows(diq_out, from_s(d), QJ), b_ss.at[d], b_rs.at[d])
        arrived(diwr.at[from_s(d)], v_ss.at[d], v_rs.at[d])

    loop(1, NS, grads_here)
    weight_grad = diwr[0]
    for src in range(1, NS):
        weight_grad = weight_grad + diwr[src]
    diw_v[...] = weight_grad
    out_iw = pltpu.make_async_copy(diw_v, diw_out, fin_sem.at[1])
    out_iw.start()

    def sent_s(d):
        gone(rows(iq_hbm, peer_s(d), QJ), iqr.at[me_s], iq_ss.at[d], iq_rs.at[d])
        gone(iw_hbm, iwr.at[me_s], iw_ss.at[d], iw_rs.at[d])
        gone(rows(diqs, peer_s(d), QJ), rows(diq_out, me_s, QJ), b_ss.at[d], b_rs.at[d])
        gone(diws.at[peer_s(d)], diwr.at[me_s], v_ss.at[d], v_rs.at[d])

    loop(1, NS, sent_s)
    for lane, chunk in lanes.items():
        gone(rows(kb, chunk, CH), rows(kb, chunk, CH), ag_ss.at[lane], ag_rs.at[0])
    loop(1, NK, lambda d: gone(slots(sendb, peer_k(d)), slots(recvb, me_k), xs_ss.at[d], xs_rs.at[d]))

    def sent_pair(i):
        gone(rows(massq, 2 * i + (1 - c), QL), mcr.at[i], m_ss.at[i], m_rs.at[i])
        for g in range(GROUPS):
            gone(gs.at[g, i], gcr.at[g, i], g_ss.at[g, i], g_rs.at[g, i])

    loop(0, NZ, sent_pair)
    for d in (1, 2, 3):
        there = lax.rem(z + d, NZ)
        gone(mzs.at[d], mzr.at[d], mz_ss.at[d], mz_rs.at[d])
        for g in range(GROUPS):
            gone(gzs.at[g, there], gzr.at[g, z], gz_ss.at[g, there], gz_rs.at[g, z])

    loop(HL // 2, HL, lambda h: dq_copy(h).wait())
    here_iq.wait()
    out_iw.wait()

    for g in range(GROUPS):
        loop(1, NK, lambda d: arrived(home_part(orx, g, from_k(d)), o_ss.at[g, d], o_rs.at[g, d]))
        grads = dot_tn(to_block[...], orx[g])
        if g < 2:
            dlat_v[:, :, g * GW:(g + 1) * GW] = grads.reshape(NK, SUB, GW)
        else:
            dlat_v[:, :, LAT:KD] = grads[:, 0:KD - LAT].reshape(NK, SUB, KD - LAT)
            didx_v[...] = grads[:, GW - ID:GW].reshape(NK, SUB, ID)
    out_lat = pltpu.make_async_copy(dlat_v, dlat_out, fin_sem.at[2])
    out_lat.start()
    out_idx = pltpu.make_async_copy(didx_v, didx_out, fin_sem.at[3])
    out_idx.start()
    for g in range(GROUPS):
        loop(1, NK, lambda d: gone(
            home_part(ob, g, peer_k(d)), home_part(orx, g, me_k), o_ss.at[g, d], o_rs.at[g, d]))
    out_lat.wait()
    out_idx.wait()


def body(queries, out_grad, latent_keys, index_queries, index_weights, index_keys, picks):
    hbm = pl.BlockSpec(memory_space=pl.ANY)
    dma = pltpu.SemaphoreType.DMA
    v = pltpu.VMEM
    outs = pl.pallas_call(
        kernel,
        out_shape=[
            jax.ShapeDtypeStruct((HL, KD, QT), BF16),
            jax.ShapeDtypeStruct((NK, SUB, KD), F32),
            jax.ShapeDtypeStruct((QT * JL, ID), F32),
            jax.ShapeDtypeStruct((JL, QT), F32),
            jax.ShapeDtypeStruct((NK, SUB, ID), F32),
        ],
        in_specs=[hbm] * 6 + [pl.BlockSpec(memory_space=pltpu.SMEM)],
        out_specs=[hbm] * 5,
        scratch_shapes=[
            v((KD, ROWS), BF16), v((ROWS, LAT), BF16),
            v((NK, SUB, ID), BF16), v((NK, SUB, W), BF16),
            v((SLOTS, SUB, W), BF16), v((SLOTS, SUB, W), BF16), v((KEYS, W), BF16),
            v((SLOTS * SUB, CH), BF16), v((SLOTS * SUB, CH), BF16),
            v((KEYS, ROWS), F32),
            v((KEYS, ROWS), BF16), v((KEYS, ROWS), BF16), v((2, KD, 512), BF16), v((8, ROWS), F32),
            v((8, ROWS), F32), v((8, ROWS), F32),
            v((NS, QJ, ID), BF16), v((NS, JL, QT), F32), v((NS, QJ, 128), F32), v((QL, KEYS), F32),
            v((KEYS, QT), F32),
            v((NZ, QL, KEYS), F32), v((NZ, QL, KEYS), F32), v((NZ, QL, KEYS), F32),
            v((ID, NS * QJ), BF16), v((NS, JL, QT), F32), v((NS, JL, QT), F32),
            v((GROUPS, NZ, CH, GW), BF16), v((GROUPS, NZ, CH, GW), BF16),
            v((GROUPS, NZ, CH, GW), BF16), v((GROUPS, NZ, CH, GW), BF16),
            v((GROUPS, SLOTS * SUB, GW), BF16), v((GROUPS, SLOTS * SUB, GW), BF16),
            v((NK, SUB, KD), F32), v((NK, SUB, ID), F32), v((JL, QT), F32),
            pltpu.SMEM((NK, CAP), jnp.int32),
            dma((4,)), dma((HL,)), dma((NK,)), dma((NS,)), dma((NS,)), dma((NS,)), dma((NS,)),
            dma((NK,)), dma((NK,)), dma((NS,)), dma((NS,)), dma((HL,)),
            dma((NZ,)), dma((NZ,)), dma((NZ,)), dma((NZ,)),
            dma((GROUPS, NZ)), dma((GROUPS, NZ)), dma((GROUPS, NZ)), dma((GROUPS, NZ)),
            dma((GROUPS, NK)), dma((GROUPS, NK)), dma((NS,)), dma((NS,)), dma((NS,)), dma((NS,)), dma((4,)),
        ],
        compiler_params=pltpu.CompilerParams(
            collective_id=0, has_side_effects=True, vmem_limit_bytes=64 * 1024 * 1024
        ),
        name="sparse_attention_backward",
    )(
        queries.transpose(1, 2, 0),
        out_grad.reshape(ROWS, LAT),
        latent_keys.transpose(0, 2, 1),
        index_queries.reshape(QT * JL, ID),
        index_weights.T,
        index_keys,
        picks,
    )
    def hand_over(*refs):
        given, made, held, sems = refs[:5], refs[5:10], refs[10:15], refs[15]
        parts = []
        for i in range(5):
            count = 4 if i == 0 else 1
            size = given[i].shape[0] // count
            parts += [(i, pl.ds(n * size, size)) for n in range(count)]
        loads = [pltpu.make_async_copy(given[i].at[at], held[i].at[at], sems.at[n]) for n, (i, at) in enumerate(parts)]
        stores = [pltpu.make_async_copy(held[i].at[at], made[i].at[at], sems.at[n]) for n, (i, at) in enumerate(parts)]
        for load in loads:
            load.start()
        for load, store in zip(loads, stores):
            load.wait()
            store.start()
        for store in stores:
            store.wait()

    dq, dlat, diq, diw, didx = pl.pallas_call(
        hand_over,
        out_shape=[jax.ShapeDtypeStruct(o.shape, o.dtype) for o in outs],
        in_specs=[hbm] * 5,
        out_specs=[hbm] * 5,
        scratch_shapes=[v(o.shape, o.dtype) for o in outs] + [dma((8,))],
        compiler_params=pltpu.CompilerParams(vmem_limit_bytes=64 * 1024 * 1024),
        name="hand_over",
    )(*outs)
    return (dq.transpose(2, 0, 1), dlat, diq.reshape(QT, JL, ID), diw.T, didx)


def solution(mesh):
    placed = (
        P("sk", "sq", None),
        P("sk", "sq", None),
        P("sk", None, None),
        P("sk", "sq", None),
        P("sk", "sq"),
        P("sk", None, None),
        P(),
    )
    return jax.shard_map(
        body,
        mesh=mesh,
        in_specs=placed,
        out_specs=(
            P("sk", "sq", None),
            P("sk", "sq", None),
            P("sk", "sq", None),
            P("sk", "sq"),
            P("sk", "sq", None),
        ),
        check_vma=False,
    )
```

```python
import math

import jax
import jax.numpy as jnp
from jax import lax
from jax.experimental import pallas as pl
from jax.experimental.pallas import tpu as pltpu
from jax.sharding import PartitionSpec as P

H = 128
HI = 64
ID = 128
CAP = 2
LAT = 512
KD = 576
ATTN_SCALE = 0.1353
INDEX_SCALE = 1.0 / math.sqrt(ID * HI)
LOG2E = 1.4426950408889634

MESH = pl.DeviceIdType.MESH
F32 = jnp.float32
BF16 = jnp.bfloat16

NK = 16
NS = 8
NZ = 4
SUB = 16
PICKS = 16
CH = PICKS * SUB
KEYS = NS * CH
QT = 128
HL = 16
ROWS = HL * QT
JL = 8
QL = 16
QJ = QL * JL
SLOTS = NK * CAP
W = 768
IO = 640
HALF = W // 2
GW = 256
GROUPS = 3
R = 256
KC = 256


def dot(a, b):
    return jnp.dot(a, b, preferred_element_type=F32)


def dot_nt(a, b):
    return lax.dot_general(a, b, (((1,), (1,)), ((), ())), preferred_element_type=F32)


def dot_tn(a, b):
    return lax.dot_general(a, b, (((0,), (0,)), ((), ())), preferred_element_type=F32)


def iota(shape, axis):
    return lax.broadcasted_iota(jnp.int32, shape, axis)


def ones_where(hit):
    return jnp.where(hit, 1.0, 0.0).astype(BF16)


def kernel(
    q_hbm, do_hbm, lat_hbm, iq_hbm, iw_hbm, idx_hbm, picks,
    dq_out, dlat_out, diq_out, diw_out, didx_out,
    qt, dov, xi, xs, sendb, recv0, recv1, kb, to_slot, to_block, sv, pt, dst, dqv, topv, totv, dotv,
    iqr, iwr, wv, lgv, masst, mcr, mzs, mzr, iqt, diws, diwr,
    gs, gcr, gzs, gzr, ob, orx, dlat_v, didx_v, diw_v, found,
    ld_sem, q_sem, lat_sem, iq_ss, iq_rs, iw_ss, iw_rs, xs_ss, xs_rs, ag_ss, ag_rs, dq_sem,
    m_ss, m_rs, mz_ss, mz_rs, g_ss, g_rs, gz_ss, gz_rs, o_ss, o_rs, b_ss, b_rs, v_ss, v_rs, fin_sem,
):
    massq = sv.at[0:QT]
    dlv = sv.at[QT:QT + QJ]
    ikt = sv.at[256:256 + ID]
    gown = sv.at[512:512 + GROUPS * 512, 0:NZ * GW]
    diqs = sv.at[512:512 + NS * QJ, NZ * GW:NZ * GW + ID]

    me_k = lax.axis_index("sk")
    me_s = lax.axis_index("sq")
    z = lax.div(me_s, 2)
    c = lax.rem(me_s, 2)
    zp = lax.rem(z + 1, NZ)
    zo = lax.rem(z + 2, NZ)
    zm = lax.rem(z + 3, NZ)
    mate = z * 2 + (1 - c)

    def remote(src, dst_ref, ss, rs, sk, sq):
        return pltpu.make_async_remote_copy(
            src_ref=src, dst_ref=dst_ref, send_sem=ss, recv_sem=rs,
            device_id=(sq, sk), device_id_type=MESH,
        )

    def send(*what):
        remote(*what).start()

    def gone(src, dst_ref, ss, rs):
        remote(src, dst_ref, ss, rs, me_k, mate).wait_send()

    def arrived(dst_ref, ss, rs):
        remote(dst_ref, dst_ref, ss, rs, me_k, mate).wait_recv()

    def peer_k(d):
        return lax.rem(me_k + d, NK)

    def from_k(d):
        return lax.rem(me_k + NK - d, NK)

    def peer_s(d):
        return lax.rem(me_s + d, NS)

    def from_s(d):
        return lax.rem(me_s + NS - d, NS)

    def span(at, count):
        return pl.ds(pl.multiple_of(at * count, count), count)

    def rows(ref, at, count):
        return ref.at[span(at, count)]

    def loop(lo, hi, step):
        def one(i, carry):
            step(i)
            return carry

        lax.fori_loop(lo, hi, one, 0)

    load_idx = pltpu.make_async_copy(idx_hbm.at[:, span(me_s, SUB), :], xi, ld_sem.at[0])
    load_iq = pltpu.make_async_copy(rows(iq_hbm, me_s, QJ), iqr.at[me_s], ld_sem.at[1])
    load_iw = pltpu.make_async_copy(iw_hbm, iwr.at[me_s], ld_sem.at[2])
    load_do = pltpu.make_async_copy(do_hbm, pt.at[:, 0:LAT], ld_sem.at[3])
    load_lat = [
        pltpu.make_async_copy(lat_hbm.at[b], dst.at[0:KD, b * 128:(b + 1) * 128], lat_sem.at[b]) for b in range(NK)
    ]
    load_q = [pltpu.make_async_copy(q_hbm.at[h], qt.at[:, h * QT:(h + 1) * QT], q_sem.at[h]) for h in range(HL)]
    for load in load_lat + [load_idx]:
        load.start()

    barrier = pltpu.get_barrier_semaphore()

    def greet_k(d):
        pl.semaphore_signal(barrier, inc=1, device_id=(me_s, peer_k(d)), device_id_type=MESH)

    def greet_s(d):
        pl.semaphore_signal(barrier, inc=1, device_id=(peer_s(d), me_k), device_id_type=MESH)

    loop(1, NK, greet_k)
    loop(1, NS, greet_s)

    def picked(t):
        first = jnp.int32(-1)
        second = jnp.int32(-1)
        for p in range(PICKS):
            block = picks[t, p]
            local = block & (NK - 1)
            here = lax.shift_right_logical(block, 4) == me_k
            second = jnp.where(here & (first >= 0), local, second)
            first = jnp.where(here & (first < 0), local, first)
        found[t, 0] = first
        found[t, 1] = second

    loop(0, NK, picked)

    pick_rows = ones_where(iota((SUB, 128), 1) == me_s * SUB + iota((SUB, 128), 0))
    load_idx.wait()
    for b in range(NK):
        load_lat[b].wait()
        xs[b, :, 0:KD] = dot_nt(pick_rows, dst[0:KD, b * 128:(b + 1) * 128]).astype(BF16)
        xs[b, :, KD:IO] = jnp.zeros((SUB, IO - KD), BF16)
        xs[b, :, IO:W] = xi[b]
    cell = iota((SUB, CH), 1) - iota((SUB, CH), 0)

    for load in [load_do] + load_q + [load_iq, load_iw]:
        load.start()

    def pack(t):
        for i in range(CAP):
            block = xs[jnp.maximum(found[t, i], 0)]
            for f in range(2):
                sendb[f, 2 * t + i] = block[:, f * HALF:(f + 1) * HALF]

    loop(0, NK, pack)
    pl.semaphore_wait(barrier, NK - 1 + NS - 1)

    recvb = (recv0, recv1)

    def slots(ref, k):
        return ref.at[pl.ds(2 * k, 2)]

    def fetch(f, d):
        return remote(
            slots(sendb.at[f], peer_k(d)), slots(recvb[f], me_k), xs_ss.at[f, d], xs_rs.at[f, d], peer_k(d), me_s)

    for f in range(2):
        loop(1, NK, lambda d: fetch(f, d).start())
        recvb[f][pl.ds(2 * me_k, 2)] = sendb[f, pl.ds(2 * me_k, 2)]

    def ship_iq(d):
        send(rows(iq_hbm, peer_s(d), QJ), iqr.at[me_s], iq_ss.at[d], iq_rs.at[d], me_k, peer_s(d))
        send(iw_hbm, iwr.at[me_s], iw_ss.at[d], iw_rs.at[d], me_k, peer_s(d))

    loop(1, NS, ship_iq)

    def place(t):
        to_block[span(2 * t, SUB), :] = ones_where(cell == found[t, 0] * SUB)
        to_block[span(2 * t + 1, SUB), :] = ones_where(cell == found[t, 1] * SUB)

    mine = [picks[me_k, p] for p in range(PICKS)]
    owner = [lax.shift_right_logical(block, 4) for block in mine]
    slot = []
    for p in range(PICKS):
        rank = jnp.int32(0)
        for before in range(p):
            rank = rank + jnp.where(owner[before] == owner[p], 1, 0)
        slot.append(owner[p] * CAP + rank)

    def unpick(s):
        pick = jnp.int32(-1)
        for p in range(PICKS):
            pick = jnp.where(slot[p] == s, p, pick)
        to_slot[span(s, SUB), :] = ones_where(cell == pick * SUB)

    loop(0, SLOTS, unpick)
    loop(0, NK, place)
    i0, i1 = iota((CH, CH), 0), iota((CH, CH), 1)
    swap = ones_where(i1 == lax.rem(i0, 16) * 16 + lax.div(i0, 16))
    load_do.wait()
    for g in range(QT // 16):
        turned = dot(swap, pt[g * CH:(g + 1) * CH, 0:LAT]).astype(BF16)
        for h in range(HL):
            dov[h * QT + g * 16:h * QT + (g + 1) * 16, :] = turned[h * 16:(h + 1) * 16]
    for load in load_q:
        load.wait()
    topv[...] = jnp.full(topv.shape, -jnp.inf, F32)
    totv[...] = jnp.zeros_like(totv)
    dotv[...] = jnp.zeros_like(dotv)
    masst[...] = jnp.zeros_like(masst)

    load_iq.wait()
    load_iw.wait()

    def iq_here(d):
        arrived(iqr.at[from_s(d)], iq_ss.at[d], iq_rs.at[d])
        arrived(iwr.at[from_s(d)], iw_ss.at[d], iw_rs.at[d])

    loop(1, NS, iq_here)
    my_query = iota((QL, JL, 128), 2) == me_s * QL + iota((QL, JL, 128), 0)

    def weigh(src):
        weight = jnp.where(my_query, iwr[src][None], 0.0)
        weight = jnp.sum(weight, axis=2, keepdims=True).reshape(QJ, 1)
        wv[src] = jnp.broadcast_to(weight, (QJ, 128))
        iqt[:, span(src, 128)] = iqr[src].T

    loop(0, NS, weigh)

    fwd_from = jnp.where(c == 0, zm, zp)
    fwd_to = jnp.where(c == 0, zp, zm)
    c2 = ATTN_SCALE * LOG2E

    def chunk_ref(chunk, f):
        return kb.at[span(chunk, CH), f * HALF:(f + 1) * HALF]

    routes = (
        (me_s, mate),
        (me_s, fwd_to * 2 + c),
        (me_s, fwd_from * 2 + c),
        (fwd_from * 2 + c, fwd_to * 2 + c),
        (fwd_from * 2 + c, mate),
        (fwd_to * 2 + c, mate),
        (zo * 2 + c, mate),
    )

    def pass_on(f, *which):
        for lane in which:
            chunk, sq = routes[lane]
            send(chunk_ref(chunk, f), chunk_ref(chunk, f), ag_ss.at[f, lane], ag_rs.at[f, chunk], me_k, sq)

    def chunk_here(f, chunk):
        arrived(chunk_ref(chunk, f), ag_ss.at[f, 0], ag_rs.at[f, chunk])

    def meet(chunk):
        at = span(chunk, CH)

        for lo in range(0, ROWS, 512):
            lane = slice(lo, lo + 512)
            s = dot(kb[at, 0:KD], qt[:, lane]) * c2
            dp = dot_nt(kb[at, 0:LAT], dov[lane, :])
            sv[at, lane] = s
            s = s.reshape(CH // 8, 8, 512)
            old = topv[:, lane]
            top = jnp.maximum(old, jnp.max(s, axis=0))
            e = jnp.exp2(s - top[None])
            fade = jnp.exp2(old - top)
            topv[:, lane] = top
            totv[:, lane] = totv[:, lane] * fade + jnp.sum(e, axis=0)
            dotv[:, lane] = dotv[:, lane] * fade + jnp.sum(e * dp.reshape(CH // 8, 8, 512), axis=0)

        keys = kb[at, IO:W]
        acc = jnp.zeros((QJ, CH), F32)
        for src in range(NS):
            acc = acc + jnp.maximum(dot_nt(iqr[src], keys), 0.0) * jnp.tile(wv[src], (1, CH // 128))
        lgv[:, at] = INDEX_SCALE * jnp.sum(acc.reshape(QL, JL, CH), axis=1)

    for f in range(2):
        loop(1, NK, lambda d: fetch(f, d).wait_recv())
        for p in range(PICKS):
            kb[pl.ds(pl.multiple_of(me_s * CH + p * SUB, SUB), SUB), f * HALF:(f + 1) * HALF] = recvb[f][slot[p]]
        pass_on(f, 0, 1, 2)

    def via_from(f):
        chunk_here(f, fwd_from * 2 + c)
        pass_on(f, 3, 4)

    def via_to(f):
        chunk_here(f, fwd_to * 2 + c)
        pass_on(f, 5)

    def via_far(f):
        chunk_here(f, zo * 2 + c)
        pass_on(f, 6)

    def gather_step(i):
        side = jnp.where(
            i < 2, z, jnp.where((i == 2) | (i == 5), fwd_from, jnp.where((i == 3) | (i == 4), fwd_to, zo))
        )
        own_core = lax.rem(i, 2) == 0

        @pl.when(i == 1)
        def _():
            via_from(0)
            via_to(0)

        @pl.when(i == 2)
        def _():
            via_from(1)

        @pl.when(i == 4)
        def _():
            via_to(1)
            via_far(0)

        @pl.when(i == 6)
        def _():
            via_far(1)

        @pl.when(jnp.logical_not(own_core))
        def _():
            for f in range(2):
                chunk_here(f, side * 2 + 1 - c)

        meet(side * 2 + jnp.where(own_core, c, 1 - c))

    loop(0, NS, gather_step)

    def attend(step):
        at = span(step, R)
        do = dov[at, :]
        top = jnp.max(topv[:, at], axis=0, keepdims=True)
        fade = jnp.exp2(topv[:, at] - top)
        total = jnp.sum(totv[:, at] * fade, axis=0, keepdims=True)
        rowdot = jnp.sum(dotv[:, at] * fade, axis=0, keepdims=True) / total
        top = top + jnp.log2(total)
        for k in range(0, KEYS, KC):
            dp = dot_nt(kb[k:k + KC, 0:LAT], do)
            p = jnp.exp2(sv[k:k + KC, at] - top)
            pt[k:k + KC, at] = p.astype(BF16)
            dst[k:k + KC, at] = (p * (dp - rowdot)).astype(BF16)
            heads = p[:, 0:QT]
            for h in range(QT, R, QT):
                heads = heads + p[:, h:h + QT]
            masst[k:k + KC, :] += heads

    loop(0, ROWS // R, attend)

    for k in range(0, KEYS, KC):
        massq[:, k:k + KC] = masst[k:k + KC, :].T

    def mass_pair(i):
        send(rows(massq, 2 * i + (1 - c), QL), mcr.at[i], m_ss.at[i], m_rs.at[i], me_k, mate)

    loop(0, NZ, mass_pair)

    def at_step(i):
        return jnp.where(i == 0, zo, jnp.where(i == 1, fwd_from, jnp.where(i == 2, fwd_to, z)))

    to_sq = fwd_to * 2 + c
    from_sq = fwd_from * 2 + c

    def key_group(g, then=None):
        base = g * 512
        lo = g * GW

        def finish(i):
            there = at_step(i)
            arrived(gcr.at[g, there], g_ss.at[g, there], g_rs.at[g, there])
            own_half = gown[pl.ds(pl.multiple_of(base + c * CH, CH), CH), span(i, GW)]
            return own_half + gcr[g, there].astype(F32)

        def relay():
            gzs[g, 0] = finish(0).astype(BF16)
            send(gzs.at[g, 0], gzr.at[g, 0], gz_ss.at[g, 0], gz_rs.at[g, 0], me_k, to_sq)

        def back():
            gzs[g, 1] = finish(1).astype(BF16)
            send(gzs.at[g, 1], gzr.at[g, 1], gz_ss.at[g, 1], gz_rs.at[g, 1], me_k, from_sq)

        def onward():
            arrived(gzr.at[g, 0], gz_ss.at[g, 0], gz_rs.at[g, 0])
            gzs[g, 2] = (finish(2) + gzr[g, 0].astype(F32)).astype(BF16)
            send(gzs.at[g, 2], gzr.at[g, 2], gz_ss.at[g, 2], gz_rs.at[g, 2], me_k, to_sq)

        def step(i):
            there = at_step(i)
            at = span(there, 2 * CH)
            lane = span(i, GW)
            if g < 2:
                gown[base:base + 512, lane] = (
                    dot_nt(dst[at, :], qt[lo:lo + GW, :]) * ATTN_SCALE + dot(pt[at, :], dov[:, lo:lo + GW])
                )
            else:
                rope = dot_nt(dst[at, :], qt[LAT:KD, :]) * ATTN_SCALE
                gown[base:base + 512, lane] = jnp.concatenate(
                    [rope, jnp.zeros((2 * CH, 128 - KD + LAT), F32), masst[at, :]], axis=1
                )
            gs[g, there] = gown[pl.ds(pl.multiple_of(base + (1 - c) * CH, CH), CH), lane].astype(BF16)
            send(gs.at[g, there], gcr.at[g, there], g_ss.at[g, there], g_rs.at[g, there], me_k, mate)

            for n, act in ((1, relay), (2, back), (3, onward)):
                pl.when(i == n)(act)
            if then is not None:
                pl.when(i == 1)(then)

        loop(0, NZ, step)

    def ship_home(g):
        arrived(gcr.at[g, z], g_ss.at[g, z], g_rs.at[g, z])
        acc = gown[pl.ds(pl.multiple_of(g * 512 + c * CH, CH), CH), 3 * GW:4 * GW] + gcr[g, z].astype(F32)
        for way in (1, 2):
            arrived(gzr.at[g, way], gz_ss.at[g, way], gz_rs.at[g, way])
            acc = acc + gzr[g, way].astype(F32)
        ob[g] = dot(to_slot[...], acc.astype(BF16)).astype(BF16)
        loop(1, NK, lambda d: send(
            home_part(ob, g, peer_k(d)), home_part(orx, g, me_k), o_ss.at[g, d], o_rs.at[g, d], peer_k(d), me_s))
        own = span(me_k, CAP * SUB)
        orx[g, own, :] = ob[g, own, :]

    def home_part(ref, g, k):
        return ref.at[g, span(k, CAP * SUB), :]

    def mass_sum(there):
        arrived(mcr.at[there], m_ss.at[there], m_rs.at[there])
        return massq[span(2 * there + c, QL), :] + mcr[there]

    def mass_first():
        mzs[0] = mass_sum(zo)
        send(mzs.at[0], mzr.at[0], mz_ss.at[0], mz_rs.at[0], me_k, to_sq)
        mzs[1] = mass_sum(fwd_from)
        send(mzs.at[1], mzr.at[1], mz_ss.at[1], mz_rs.at[1], me_k, from_sq)

    key_group(0, mass_first)
    arrived(mzr.at[0], mz_ss.at[0], mz_rs.at[0])
    mzs[2] = mass_sum(fwd_to) + mzr[0]
    send(mzs.at[2], mzr.at[2], mz_ss.at[2], mz_rs.at[2], me_k, to_sq)
    mzs[3] = mass_sum(z)
    key_group(1)
    ship_home(0)

    logits = lgv[...]
    e = jnp.exp(logits - jnp.max(logits, axis=1, keepdims=True))
    guess = e / jnp.sum(e, axis=1, keepdims=True)
    mass = mzs[3]
    for way in (1, 2):
        arrived(mzr.at[way], mz_ss.at[way], mz_rs.at[way])
        mass = mass + mzr[way]
    dlogit = INDEX_SCALE * (guess - mass * (1.0 / H))
    dlv[...] = jnp.broadcast_to(dlogit[:, None, :], (QL, JL, KEYS)).reshape(QJ, KEYS)
    ikt[...] = jnp.zeros(ikt.shape, F32)

    def index_part(src):
        sim = dot_nt(iqr[src], kb[:, IO:W])
        dl = dlv[...]
        ds = jnp.where(sim > 0, dl * jnp.tile(wv[src], (1, KEYS // 128)), 0.0).astype(BF16)
        dw = jnp.sum(dl * jnp.maximum(sim, 0.0), axis=1, keepdims=True).reshape(QL, JL, 1)
        diws[src] = jnp.sum(jnp.where(my_query, dw, 0.0), axis=0)
        diqs[span(src, QJ), :] = dot(ds, kb[:, IO:W])
        ikt[...] += dot(iqt[:, span(src, 128)], ds)

    loop(0, NS, index_part)

    def ship_grads(d):
        there = peer_s(d)
        send(rows(diqs, there, QJ), rows(diq_out, me_s, QJ), b_ss.at[d], b_rs.at[d], me_k, there)
        send(diws.at[there], diwr.at[me_s], v_ss.at[d], v_rs.at[d], me_k, there)

    loop(1, NS, ship_grads)
    diwr[me_s] = diws[me_s]
    here_iq = pltpu.make_async_copy(rows(diqs, me_s, QJ), rows(diq_out, me_s, QJ), fin_sem.at[0])
    here_iq.start()

    for k in range(0, KEYS, KC):
        masst[k:k + KC, :] = ikt[:, k:k + KC].T

    ship_home(1)
    key_group(2)

    def dq_copy(head):
        step = lax.div(head, 4)
        lane = span(lax.rem(head, 4), QT)
        return pltpu.make_async_copy(dqv.at[lax.rem(step, 2), :, lane], dq_out.at[head], dq_sem.at[head])

    def query_grad(step):
        at = span(step, 512)
        grad = (dot_tn(kb[:, 0:KD], dst[:, at]) * ATTN_SCALE).astype(BF16)

        @pl.when(step >= 2)
        def _():
            for h in range(4):
                dq_copy((step - 2) * 4 + h).wait()

        dqv[lax.rem(step, 2)] = grad
        for h in range(4):
            dq_copy(step * 4 + h).start()

    loop(0, 2, query_grad)
    ship_home(2)
    loop(2, 4, query_grad)

    def grads_here(d):
        arrived(rows(diq_out, from_s(d), QJ), b_ss.at[d], b_rs.at[d])
        arrived(diwr.at[from_s(d)], v_ss.at[d], v_rs.at[d])

    loop(1, NS, grads_here)
    weight_grad = diwr[0]
    for src in range(1, NS):
        weight_grad = weight_grad + diwr[src]
    diw_v[...] = weight_grad
    out_iw = pltpu.make_async_copy(diw_v, diw_out, fin_sem.at[1])
    out_iw.start()

    def sent_s(d):
        gone(rows(iq_hbm, peer_s(d), QJ), iqr.at[me_s], iq_ss.at[d], iq_rs.at[d])
        gone(iw_hbm, iwr.at[me_s], iw_ss.at[d], iw_rs.at[d])
        gone(rows(diqs, peer_s(d), QJ), rows(diq_out, me_s, QJ), b_ss.at[d], b_rs.at[d])
        gone(diws.at[peer_s(d)], diwr.at[me_s], v_ss.at[d], v_rs.at[d])

    loop(1, NS, sent_s)
    for f in range(2):
        for lane, (chunk, _) in enumerate(routes):
            gone(chunk_ref(chunk, f), chunk_ref(chunk, f), ag_ss.at[f, lane], ag_rs.at[f, 0])
        loop(1, NK, lambda d: fetch(f, d).wait_send())

    def sent_pair(i):
        gone(rows(massq, 2 * i + (1 - c), QL), mcr.at[i], m_ss.at[i], m_rs.at[i])
        for g in range(GROUPS):
            gone(gs.at[g, i], gcr.at[g, i], g_ss.at[g, i], g_rs.at[g, i])

    loop(0, NZ, sent_pair)
    for way in range(3):
        gone(mzs.at[way], mzr.at[way], mz_ss.at[way], mz_rs.at[way])
        for g in range(GROUPS):
            gone(gzs.at[g, way], gzr.at[g, way], gz_ss.at[g, way], gz_rs.at[g, way])

    loop(HL // 2, HL, lambda h: dq_copy(h).wait())
    here_iq.wait()
    out_iw.wait()

    for g in range(GROUPS):
        loop(1, NK, lambda d: arrived(home_part(orx, g, from_k(d)), o_ss.at[g, d], o_rs.at[g, d]))
        grads = dot_tn(to_block[...], orx[g])
        if g < 2:
            dlat_v[:, :, g * GW:(g + 1) * GW] = grads.reshape(NK, SUB, GW)
        else:
            dlat_v[:, :, LAT:KD] = grads[:, 0:KD - LAT].reshape(NK, SUB, KD - LAT)
            didx_v[...] = grads[:, GW - ID:GW].reshape(NK, SUB, ID)
    out_lat = pltpu.make_async_copy(dlat_v, dlat_out, fin_sem.at[2])
    out_lat.start()
    out_idx = pltpu.make_async_copy(didx_v, didx_out, fin_sem.at[3])
    out_idx.start()
    for g in range(GROUPS):
        loop(1, NK, lambda d: gone(
            home_part(ob, g, peer_k(d)), home_part(orx, g, me_k), o_ss.at[g, d], o_rs.at[g, d]))
    out_lat.wait()
    out_idx.wait()


def body(queries, out_grad, latent_keys, index_queries, index_weights, index_keys, picks):
    hbm = pl.BlockSpec(memory_space=pl.ANY)
    dma = pltpu.SemaphoreType.DMA
    v = pltpu.VMEM
    outs = pl.pallas_call(
        kernel,
        out_shape=[
            jax.ShapeDtypeStruct((HL, KD, QT), BF16),
            jax.ShapeDtypeStruct((NK, SUB, KD), F32),
            jax.ShapeDtypeStruct((QT * JL, ID), F32),
            jax.ShapeDtypeStruct((JL, QT), F32),
            jax.ShapeDtypeStruct((NK, SUB, ID), F32),
        ],
        in_specs=[hbm] * 6 + [pl.BlockSpec(memory_space=pltpu.SMEM)],
        out_specs=[hbm] * 5,
        scratch_shapes=[
            v((KD, ROWS), BF16), v((ROWS, LAT), BF16),
            v((NK, SUB, ID), BF16), v((NK, SUB, W), BF16),
            v((2, SLOTS, SUB, HALF), BF16), v((SLOTS, SUB, HALF), BF16), v((SLOTS, SUB, HALF), BF16),
            v((KEYS, W), BF16),
            v((SLOTS * SUB, CH), BF16), v((SLOTS * SUB, CH), BF16),
            v((KEYS, ROWS), F32),
            v((KEYS, ROWS), BF16), v((KEYS, ROWS), BF16), v((2, KD, 512), BF16), v((8, ROWS), F32),
            v((8, ROWS), F32), v((8, ROWS), F32),
            v((NS, QJ, ID), BF16), v((NS, JL, QT), F32), v((NS, QJ, 128), F32), v((QL, KEYS), F32),
            v((KEYS, QT), F32),
            v((NZ, QL, KEYS), F32), v((NZ, QL, KEYS), F32), v((NZ, QL, KEYS), F32),
            v((ID, NS * QJ), BF16), v((NS, JL, QT), F32), v((NS, JL, QT), F32),
            v((GROUPS, NZ, CH, GW), BF16), v((GROUPS, NZ, CH, GW), BF16),
            v((GROUPS, NZ, CH, GW), BF16), v((GROUPS, NZ, CH, GW), BF16),
            v((GROUPS, SLOTS * SUB, GW), BF16), v((GROUPS, SLOTS * SUB, GW), BF16),
            v((NK, SUB, KD), F32), v((NK, SUB, ID), F32), v((JL, QT), F32),
            pltpu.SMEM((NK, CAP), jnp.int32),
            dma((4,)), dma((HL,)), dma((NK,)), dma((NS,)), dma((NS,)), dma((NS,)), dma((NS,)),
            dma((2, NK)), dma((2, NK)), dma((2, NS)), dma((2, NS)), dma((HL,)),
            dma((NZ,)), dma((NZ,)), dma((NZ,)), dma((NZ,)),
            dma((GROUPS, NZ)), dma((GROUPS, NZ)), dma((GROUPS, NZ)), dma((GROUPS, NZ)),
            dma((GROUPS, NK)), dma((GROUPS, NK)), dma((NS,)), dma((NS,)), dma((NS,)), dma((NS,)), dma((4,)),
        ],
        compiler_params=pltpu.CompilerParams(
            collective_id=0, has_side_effects=True, vmem_limit_bytes=64 * 1024 * 1024
        ),
        name="sparse_attention_backward",
    )(
        queries.transpose(1, 2, 0),
        out_grad.reshape(ROWS, LAT),
        latent_keys.transpose(0, 2, 1),
        index_queries.reshape(QT * JL, ID),
        index_weights.T,
        index_keys,
        picks,
    )
    def hand_over(*refs):
        given, made, held, sems = refs[:5], refs[5:10], refs[10:15], refs[15]
        parts = []
        for i in range(5):
            count = 4 if i == 0 else 1
            size = given[i].shape[0] // count
            parts += [(i, pl.ds(n * size, size)) for n in range(count)]
        loads = [pltpu.make_async_copy(given[i].at[at], held[i].at[at], sems.at[n]) for n, (i, at) in enumerate(parts)]
        stores = [pltpu.make_async_copy(held[i].at[at], made[i].at[at], sems.at[n]) for n, (i, at) in enumerate(parts)]
        for load in loads:
            load.start()
        for load, store in zip(loads, stores):
            load.wait()
            store.start()
        for store in stores:
            store.wait()

    dq, dlat, diq, diw, didx = pl.pallas_call(
        hand_over,
        out_shape=[jax.ShapeDtypeStruct(o.shape, o.dtype) for o in outs],
        in_specs=[hbm] * 5,
        out_specs=[hbm] * 5,
        scratch_shapes=[v(o.shape, o.dtype) for o in outs] + [dma((8,))],
        compiler_params=pltpu.CompilerParams(vmem_limit_bytes=64 * 1024 * 1024),
        name="hand_over",
    )(*outs)
    return (dq.transpose(2, 0, 1), dlat, diq.reshape(QT, JL, ID), diw.T, didx)


def solution(mesh):
    placed = (
        P("sk", "sq", None),
        P("sk", "sq", None),
        P("sk", None, None),
        P("sk", "sq", None),
        P("sk", "sq"),
        P("sk", None, None),
        P(),
    )
    return jax.shard_map(
        body,
        mesh=mesh,
        in_specs=placed,
        out_specs=(
            P("sk", "sq", None),
            P("sk", "sq", None),
            P("sk", "sq", None),
            P("sk", "sq"),
            P("sk", "sq", None),
        ),
        check_vma=False,
    )
```

```python
import math

import jax
import jax.numpy as jnp
from jax import lax
from jax.experimental import pallas as pl
from jax.experimental.pallas import tpu as pltpu
from jax.sharding import PartitionSpec as P

H = 128
HI = 64
ID = 128
CAP = 2
LAT = 512
KD = 576
ATTN_SCALE = 0.1353
INDEX_SCALE = 1.0 / math.sqrt(ID * HI)
LOG2E = 1.4426950408889634

MESH = pl.DeviceIdType.MESH
F32 = jnp.float32
BF16 = jnp.bfloat16

NK = 16
NS = 8
NZ = 4
SUB = 16
PICKS = 16
CH = PICKS * SUB
KEYS = NS * CH
QT = 128
HL = 16
ROWS = HL * QT
JL = 8
QL = 16
QJ = QL * JL
SLOTS = NK * CAP
W = 768
IO = 640
HALF = W // 2
GW = 256
GROUPS = 3
R = 256
KC = 256


def dot(a, b):
    return jnp.dot(a, b, preferred_element_type=F32)


def dot_nt(a, b):
    return lax.dot_general(a, b, (((1,), (1,)), ((), ())), preferred_element_type=F32)


def dot_tn(a, b):
    return lax.dot_general(a, b, (((0,), (0,)), ((), ())), preferred_element_type=F32)


def iota(shape, axis):
    return lax.broadcasted_iota(jnp.int32, shape, axis)


def ones_where(hit):
    return jnp.where(hit, 1.0, 0.0).astype(BF16)


def kernel(
    q_hbm, do_hbm, lat_hbm, iq_hbm, iw_hbm, idx_hbm, picks,
    dq_out, dlat_out, diq_out, diw_out, didx_out,
    qt, dov, xi, xs, sendb, recv0, recv1, kb, to_slot, to_block, home, sv, pt, dst, dqv, topv, totv, dotv,
    iqr, iwr, wv, lgv, masst, mcr, mzs, mzr, iqt, diws, diwr,
    gs, gcr, gzs, gzr, ob, orx, dlat_v, didx_v, diw_v, found,
    ld_sem, q_sem, lat_sem, iq_ss, iq_rs, iw_ss, iw_rs, xs_ss, xs_rs, ag_ss, ag_rs, dq_sem,
    m_ss, m_rs, mz_ss, mz_rs, g_ss, g_rs, gz_ss, gz_rs, o_ss, o_rs, b_ss, b_rs, v_ss, v_rs, fin_sem,
):
    massq = sv.at[0:QT]
    dlv = sv.at[QT:QT + QJ]
    ikt = sv.at[256:256 + ID]
    gown = sv.at[512:512 + GROUPS * 512, 0:NZ * GW]
    diqs = sv.at[512:512 + NS * QJ, NZ * GW:NZ * GW + ID]

    me_k = lax.axis_index("sk")
    me_s = lax.axis_index("sq")
    z = lax.div(me_s, 2)
    c = lax.rem(me_s, 2)
    zp = lax.rem(z + 1, NZ)
    zo = lax.rem(z + 2, NZ)
    zm = lax.rem(z + 3, NZ)
    mate = z * 2 + (1 - c)

    def remote(src, dst_ref, ss, rs, sk, sq):
        return pltpu.make_async_remote_copy(
            src_ref=src, dst_ref=dst_ref, send_sem=ss, recv_sem=rs,
            device_id=(sq, sk), device_id_type=MESH,
        )

    def send(*what):
        remote(*what).start()

    def gone(src, dst_ref, ss, rs):
        remote(src, dst_ref, ss, rs, me_k, mate).wait_send()

    def arrived(dst_ref, ss, rs):
        remote(dst_ref, dst_ref, ss, rs, me_k, mate).wait_recv()

    def peer_k(d):
        return lax.rem(me_k + d, NK)

    def from_k(d):
        return lax.rem(me_k + NK - d, NK)

    def peer_s(d):
        return lax.rem(me_s + d, NS)

    def from_s(d):
        return lax.rem(me_s + NS - d, NS)

    def span(at, count):
        return pl.ds(pl.multiple_of(at * count, count), count)

    def rows(ref, at, count):
        return ref.at[span(at, count)]

    def loop(lo, hi, step):
        def one(i, carry):
            step(i)
            return carry

        lax.fori_loop(lo, hi, one, 0)

    load_idx = pltpu.make_async_copy(idx_hbm.at[:, span(me_s, SUB), :], xi, ld_sem.at[0])
    load_iq = pltpu.make_async_copy(rows(iq_hbm, me_s, QJ), iqr.at[me_s], ld_sem.at[1])
    load_iw = pltpu.make_async_copy(iw_hbm, iwr.at[me_s], ld_sem.at[2])
    load_do = pltpu.make_async_copy(do_hbm, pt.at[:, 0:LAT], ld_sem.at[3])
    load_lat = [
        pltpu.make_async_copy(lat_hbm.at[b], dst.at[0:KD, b * 128:(b + 1) * 128], lat_sem.at[b]) for b in range(NK)
    ]
    load_q = [pltpu.make_async_copy(q_hbm.at[h], qt.at[:, h * QT:(h + 1) * QT], q_sem.at[h]) for h in range(HL)]
    for load in load_lat + [load_idx]:
        load.start()

    barrier = pltpu.get_barrier_semaphore()

    def greet_k(d):
        pl.semaphore_signal(barrier, inc=1, device_id=(me_s, peer_k(d)), device_id_type=MESH)

    def greet_s(d):
        pl.semaphore_signal(barrier, inc=1, device_id=(peer_s(d), me_k), device_id_type=MESH)

    loop(1, NK, greet_k)
    loop(1, NS, greet_s)

    def picked(t):
        first = jnp.int32(-1)
        second = jnp.int32(-1)
        for p in range(PICKS):
            block = picks[t, p]
            local = block & (NK - 1)
            here = lax.shift_right_logical(block, 4) == me_k
            second = jnp.where(here & (first >= 0), local, second)
            first = jnp.where(here & (first < 0), local, first)
        found[t, 0] = first
        found[t, 1] = second

    loop(0, NK, picked)

    pick_rows = ones_where(iota((SUB, 128), 1) == me_s * SUB + iota((SUB, 128), 0))
    load_idx.wait()
    for b in range(NK):
        load_lat[b].wait()
        xs[b, :, 0:KD] = dot_nt(pick_rows, dst[0:KD, b * 128:(b + 1) * 128]).astype(BF16)
        xs[b, :, KD:IO] = jnp.zeros((SUB, IO - KD), BF16)
        xs[b, :, IO:W] = xi[b]
    cell = iota((SUB, CH), 1) - iota((SUB, CH), 0)

    for load in [load_do] + load_q + [load_iq, load_iw]:
        load.start()

    def pack(t):
        for i in range(CAP):
            block = xs[jnp.maximum(found[t, i], 0)]
            for f in range(2):
                sendb[f, 2 * t + i] = block[:, f * HALF:(f + 1) * HALF]

    loop(0, NK, pack)
    pl.semaphore_wait(barrier, NK - 1 + NS - 1)

    recvb = (recv0, recv1)

    def slots(ref, k):
        return ref.at[pl.ds(2 * k, 2)]

    def fetch(f, d):
        return remote(
            slots(sendb.at[f], peer_k(d)), slots(recvb[f], me_k), xs_ss.at[f, d], xs_rs.at[f, d], peer_k(d), me_s)

    for f in range(2):
        loop(1, NK, lambda d: fetch(f, d).start())
        recvb[f][pl.ds(2 * me_k, 2)] = sendb[f, pl.ds(2 * me_k, 2)]

    def ship_iq(d):
        send(rows(iq_hbm, peer_s(d), QJ), iqr.at[me_s], iq_ss.at[d], iq_rs.at[d], me_k, peer_s(d))
        send(iw_hbm, iwr.at[me_s], iw_ss.at[d], iw_rs.at[d], me_k, peer_s(d))

    loop(1, NS, ship_iq)

    def place(t):
        to_block[span(2 * t, SUB), :] = ones_where(cell == found[t, 0] * SUB)
        to_block[span(2 * t + 1, SUB), :] = ones_where(cell == found[t, 1] * SUB)

    mine = [picks[me_k, p] for p in range(PICKS)]
    owner = [lax.shift_right_logical(block, 4) for block in mine]
    slot = []
    for p in range(PICKS):
        rank = jnp.int32(0)
        for before in range(p):
            rank = rank + jnp.where(owner[before] == owner[p], 1, 0)
        slot.append(owner[p] * CAP + rank)

    def unpick(s):
        pick = jnp.int32(-1)
        for p in range(PICKS):
            pick = jnp.where(slot[p] == s, p, pick)
        to_slot[span(s, SUB), :] = ones_where(cell == pick * SUB)

    loop(0, SLOTS, unpick)
    loop(0, NK, place)
    home[...] = to_block[...].T
    i0, i1 = iota((CH, CH), 0), iota((CH, CH), 1)
    swap = ones_where(i1 == lax.rem(i0, 16) * 16 + lax.div(i0, 16))
    load_do.wait()
    for g in range(QT // 16):
        turned = dot(swap, pt[g * CH:(g + 1) * CH, 0:LAT]).astype(BF16)
        for h in range(HL):
            dov[h * QT + g * 16:h * QT + (g + 1) * 16, :] = turned[h * 16:(h + 1) * 16]
    for load in load_q:
        load.wait()
    topv[...] = jnp.full(topv.shape, -jnp.inf, F32)
    totv[...] = jnp.zeros_like(totv)
    dotv[...] = jnp.zeros_like(dotv)
    masst[...] = jnp.zeros_like(masst)

    load_iq.wait()
    load_iw.wait()

    def iq_here(d):
        arrived(iqr.at[from_s(d)], iq_ss.at[d], iq_rs.at[d])
        arrived(iwr.at[from_s(d)], iw_ss.at[d], iw_rs.at[d])

    loop(1, NS, iq_here)
    my_query = iota((QL, JL, 128), 2) == me_s * QL + iota((QL, JL, 128), 0)

    def weigh(src):
        weight = jnp.where(my_query, iwr[src][None], 0.0)
        weight = jnp.sum(weight, axis=2, keepdims=True).reshape(QJ, 1)
        wv[src] = jnp.broadcast_to(weight, (QJ, 128))
        iqt[:, span(src, 128)] = iqr[src].T

    loop(0, NS, weigh)

    fwd_from = jnp.where(c == 0, zm, zp)
    fwd_to = jnp.where(c == 0, zp, zm)
    c2 = ATTN_SCALE * LOG2E

    def chunk_ref(chunk, f):
        return kb.at[span(chunk, CH), f * HALF:(f + 1) * HALF]

    routes = (
        (me_s, mate),
        (me_s, fwd_to * 2 + c),
        (me_s, fwd_from * 2 + c),
        (fwd_from * 2 + c, fwd_to * 2 + c),
        (fwd_from * 2 + c, mate),
        (fwd_to * 2 + c, mate),
        (zo * 2 + c, mate),
    )

    def pass_on(f, *which):
        for lane in which:
            chunk, sq = routes[lane]
            send(chunk_ref(chunk, f), chunk_ref(chunk, f), ag_ss.at[f, lane], ag_rs.at[f, chunk], me_k, sq)

    def chunk_here(f, chunk):
        arrived(chunk_ref(chunk, f), ag_ss.at[f, 0], ag_rs.at[f, chunk])

    def meet(chunk):
        at = span(chunk, CH)

        for lo in range(0, ROWS, 512):
            lane = slice(lo, lo + 512)
            s = dot(kb[at, 0:KD], qt[:, lane]) * c2
            dp = dot_nt(kb[at, 0:LAT], dov[lane, :])
            sv[at, lane] = s
            s = s.reshape(CH // 8, 8, 512)
            old = topv[:, lane]
            top = jnp.maximum(old, jnp.max(s, axis=0))
            e = jnp.exp2(s - top[None])
            fade = jnp.exp2(old - top)
            topv[:, lane] = top
            totv[:, lane] = totv[:, lane] * fade + jnp.sum(e, axis=0)
            dotv[:, lane] = dotv[:, lane] * fade + jnp.sum(e * dp.reshape(CH // 8, 8, 512), axis=0)

        keys = kb[at, IO:W]
        acc = jnp.zeros((QJ, CH), F32)
        for src in range(NS):
            acc = acc + jnp.maximum(dot_nt(iqr[src], keys), 0.0) * jnp.tile(wv[src], (1, CH // 128))
        lgv[:, at] = INDEX_SCALE * jnp.sum(acc.reshape(QL, JL, CH), axis=1)

    for f in range(2):
        loop(1, NK, lambda d: fetch(f, d).wait_recv())
        for p in range(PICKS):
            kb[pl.ds(pl.multiple_of(me_s * CH + p * SUB, SUB), SUB), f * HALF:(f + 1) * HALF] = recvb[f][slot[p]]
        pass_on(f, 0, 1, 2)

    def via_from(f):
        chunk_here(f, fwd_from * 2 + c)
        pass_on(f, 3, 4)

    def via_to(f):
        chunk_here(f, fwd_to * 2 + c)
        pass_on(f, 5)

    def via_far(f):
        chunk_here(f, zo * 2 + c)
        pass_on(f, 6)

    def gather_step(i):
        side = jnp.where(
            i < 2, z, jnp.where((i == 2) | (i == 5), fwd_from, jnp.where((i == 3) | (i == 4), fwd_to, zo))
        )
        own_core = lax.rem(i, 2) == 0

        @pl.when(i == 1)
        def _():
            via_from(0)
            via_to(0)

        @pl.when(i == 2)
        def _():
            via_from(1)

        @pl.when(i == 4)
        def _():
            via_to(1)
            via_far(0)

        @pl.when(i == 6)
        def _():
            via_far(1)

        @pl.when(jnp.logical_not(own_core))
        def _():
            for f in range(2):
                chunk_here(f, side * 2 + 1 - c)

        meet(side * 2 + jnp.where(own_core, c, 1 - c))

    loop(0, NS, gather_step)

    def attend(step):
        at = span(step, R)
        do = dov[at, :]
        top = jnp.max(topv[:, at], axis=0, keepdims=True)
        fade = jnp.exp2(topv[:, at] - top)
        total = jnp.sum(totv[:, at] * fade, axis=0, keepdims=True)
        rowdot = jnp.sum(dotv[:, at] * fade, axis=0, keepdims=True) / total
        top = top + jnp.log2(total)
        for k in range(0, KEYS, KC):
            dp = dot_nt(kb[k:k + KC, 0:LAT], do)
            p = jnp.exp2(sv[k:k + KC, at] - top)
            pt[k:k + KC, at] = p.astype(BF16)
            dst[k:k + KC, at] = (p * (dp - rowdot)).astype(BF16)
            heads = p[:, 0:QT]
            for h in range(QT, R, QT):
                heads = heads + p[:, h:h + QT]
            masst[k:k + KC, :] += heads

    loop(0, ROWS // R, attend)

    for k in range(0, KEYS, KC):
        massq[:, k:k + KC] = masst[k:k + KC, :].T

    def mass_pair(i):
        send(rows(massq, 2 * i + (1 - c), QL), mcr.at[i], m_ss.at[i], m_rs.at[i], me_k, mate)

    loop(0, NZ, mass_pair)

    def at_step(i):
        return jnp.where(i == 0, zo, jnp.where(i == 1, fwd_from, jnp.where(i == 2, fwd_to, z)))

    to_sq = fwd_to * 2 + c
    from_sq = fwd_from * 2 + c

    def group_rows(g):
        return span(g, 2 * CH)

    def to_mate(g, i, grads):
        there = at_step(i)
        gown[group_rows(g), span(i, GW)] = grads
        gs[g, there] = gown[span(2 * g + 1 - c, CH), span(i, GW)].astype(BF16)
        send(gs.at[g, there], gcr.at[g, there], g_ss.at[g, there], g_rs.at[g, there], me_k, mate)

    def key_part(n):
        g, i = lax.div(n, NZ), lax.rem(n, NZ)
        at = span(at_step(i), 2 * CH)
        part = span(g, GW)
        to_mate(g, i, dot_nt(dst[at, :], qt[part, :]) * ATTN_SCALE + dot(pt[at, :], dov[:, part]))

    def rope_part(i):
        at = span(at_step(i), 2 * CH)
        rope = dot_nt(dst[at, :], qt[LAT:KD, :]) * ATTN_SCALE
        empty = jnp.zeros((2 * CH, GW - ID - KD + LAT), F32)
        to_mate(2, i, jnp.concatenate([rope, empty, masst[at, :]], axis=1))

    def of_chip(g, i):
        there = at_step(i)
        arrived(gcr.at[g, there], g_ss.at[g, there], g_rs.at[g, there])
        return gown[span(2 * g + c, CH), span(i, GW)] + gcr[g, there].astype(F32)

    def along(g, way, sq):
        send(gzs.at[g, way], gzr.at[g, way], gz_ss.at[g, way], gz_rs.at[g, way], me_k, sq)

    def relay(g):
        gzs[g, 0] = of_chip(g, 0).astype(BF16)
        along(g, 0, to_sq)

    def back(g):
        gzs[g, 1] = of_chip(g, 1).astype(BF16)
        along(g, 1, from_sq)

    def onward(g):
        arrived(gzr.at[g, 0], gz_ss.at[g, 0], gz_rs.at[g, 0])
        gzs[g, 2] = (of_chip(g, 2) + gzr[g, 0].astype(F32)).astype(BF16)
        along(g, 2, to_sq)

    def ship_home(g):
        acc = of_chip(g, 3)
        for way in (1, 2):
            arrived(gzr.at[g, way], gz_ss.at[g, way], gz_rs.at[g, way])
            acc = acc + gzr[g, way].astype(F32)
        ob[g] = dot(to_slot[...], acc.astype(BF16)).astype(BF16)
        loop(1, NK, lambda d: send(
            home_part(ob, g, peer_k(d)), home_part(orx, g, me_k), o_ss.at[g, d], o_rs.at[g, d], peer_k(d), me_s))
        own = span(me_k, CAP * SUB)
        orx[g, own, :] = ob[g, own, :]

    def home_part(ref, g, k):
        return ref.at[g, span(k, CAP * SUB), :]

    def mass_sum(there):
        arrived(mcr.at[there], m_ss.at[there], m_rs.at[there])
        return massq[span(2 * there + c, QL), :] + mcr[there]

    def mass_first():
        mzs[0] = mass_sum(zo)
        send(mzs.at[0], mzr.at[0], mz_ss.at[0], mz_rs.at[0], me_k, to_sq)
        mzs[1] = mass_sum(fwd_from)
        send(mzs.at[1], mzr.at[1], mz_ss.at[1], mz_rs.at[1], me_k, from_sq)

    def mass_onward():
        arrived(mzr.at[0], mz_ss.at[0], mz_rs.at[0])
        mzs[2] = mass_sum(fwd_to) + mzr[0]
        send(mzs.at[2], mzr.at[2], mz_ss.at[2], mz_rs.at[2], me_k, to_sq)
        mzs[3] = mass_sum(z)

    def key_step(n):
        key_part(n)
        pl.when(n == 2)(mass_first)
        for g in range(2):
            for i, act in enumerate((relay, back, onward)):
                pl.when(n == g * NZ + i + 2)(lambda g=g, act=act: act(g))
        pl.when(n == 6)(mass_onward)

    loop(0, 2 * NZ, key_step)
    onward(1)
    ship_home(0)

    logits = lgv[...]
    e = jnp.exp(logits - jnp.max(logits, axis=1, keepdims=True))
    guess = e / jnp.sum(e, axis=1, keepdims=True)
    mass = mzs[3]
    for way in (1, 2):
        arrived(mzr.at[way], mz_ss.at[way], mz_rs.at[way])
        mass = mass + mzr[way]
    dlogit = INDEX_SCALE * (guess - mass * (1.0 / H))
    dlv[...] = jnp.broadcast_to(dlogit[:, None, :], (QL, JL, KEYS)).reshape(QJ, KEYS)
    ikt[...] = jnp.zeros(ikt.shape, F32)

    def index_part(src):
        sim = dot_nt(iqr[src], kb[:, IO:W])
        dl = dlv[...]
        ds = jnp.where(sim > 0, dl * jnp.tile(wv[src], (1, KEYS // 128)), 0.0).astype(BF16)
        dw = jnp.sum(dl * jnp.maximum(sim, 0.0), axis=1, keepdims=True).reshape(QL, JL, 1)
        diws[src] = jnp.sum(jnp.where(my_query, dw, 0.0), axis=0)
        diqs[span(src, QJ), :] = dot(ds, kb[:, IO:W])
        ikt[...] += dot(iqt[:, span(src, 128)], ds)

    loop(0, NS, index_part)

    def ship_grads(d):
        there = peer_s(d)
        send(rows(diqs, there, QJ), rows(diq_out, me_s, QJ), b_ss.at[d], b_rs.at[d], me_k, there)
        send(diws.at[there], diwr.at[me_s], v_ss.at[d], v_rs.at[d], me_k, there)

    loop(1, NS, ship_grads)
    diwr[me_s] = diws[me_s]
    here_iq = pltpu.make_async_copy(rows(diqs, me_s, QJ), rows(diq_out, me_s, QJ), fin_sem.at[0])
    here_iq.start()

    for k in range(0, KEYS, KC):
        masst[k:k + KC, :] = ikt[:, k:k + KC].T

    ship_home(1)
    loop(0, NZ, rope_part)

    def dq_copy(head):
        step = lax.div(head, 4)
        lane = span(lax.rem(head, 4), QT)
        return pltpu.make_async_copy(dqv.at[lax.rem(step, 2), :, lane], dq_out.at[head], dq_sem.at[head])

    def query_grad(step):
        at = span(step, 512)
        grad = (dot_tn(kb[:, 0:KD], dst[:, at]) * ATTN_SCALE).astype(BF16)

        @pl.when(step >= 2)
        def _():
            for h in range(4):
                dq_copy((step - 2) * 4 + h).wait()

        dqv[lax.rem(step, 2)] = grad
        for h in range(4):
            dq_copy(step * 4 + h).start()

    def last_step(i):
        query_grad(i)

        @pl.when(i == 0)
        def _():
            relay(2)
            back(2)

        pl.when(i == 1)(lambda: onward(2))
        pl.when(i == 2)(lambda: ship_home(2))

    loop(0, 4, last_step)

    def grads_here(d):
        arrived(rows(diq_out, from_s(d), QJ), b_ss.at[d], b_rs.at[d])
        arrived(diwr.at[from_s(d)], v_ss.at[d], v_rs.at[d])

    loop(1, NS, grads_here)
    weight_grad = diwr[0]
    for src in range(1, NS):
        weight_grad = weight_grad + diwr[src]
    diw_v[...] = weight_grad
    out_iw = pltpu.make_async_copy(diw_v, diw_out, fin_sem.at[1])
    out_iw.start()

    def sent_s(d):
        gone(rows(iq_hbm, peer_s(d), QJ), iqr.at[me_s], iq_ss.at[d], iq_rs.at[d])
        gone(iw_hbm, iwr.at[me_s], iw_ss.at[d], iw_rs.at[d])
        gone(rows(diqs, peer_s(d), QJ), rows(diq_out, me_s, QJ), b_ss.at[d], b_rs.at[d])
        gone(diws.at[peer_s(d)], diwr.at[me_s], v_ss.at[d], v_rs.at[d])

    loop(1, NS, sent_s)
    for f in range(2):
        for lane, (chunk, _) in enumerate(routes):
            gone(chunk_ref(chunk, f), chunk_ref(chunk, f), ag_ss.at[f, lane], ag_rs.at[f, 0])
        loop(1, NK, lambda d: fetch(f, d).wait_send())

    def sent_pair(i):
        gone(rows(massq, 2 * i + (1 - c), QL), mcr.at[i], m_ss.at[i], m_rs.at[i])
        for g in range(GROUPS):
            gone(gs.at[g, i], gcr.at[g, i], g_ss.at[g, i], g_rs.at[g, i])

    loop(0, NZ, sent_pair)
    for way in range(3):
        gone(mzs.at[way], mzr.at[way], mz_ss.at[way], mz_rs.at[way])
        for g in range(GROUPS):
            gone(gzs.at[g, way], gzr.at[g, way], gz_ss.at[g, way], gz_rs.at[g, way])

    loop(HL // 2, HL, lambda h: dq_copy(h).wait())
    here_iq.wait()
    out_iw.wait()

    for g in range(GROUPS):
        loop(1, NK, lambda d: arrived(home_part(orx, g, from_k(d)), o_ss.at[g, d], o_rs.at[g, d]))
        grads = dot(home[...], orx[g])
        if g < 2:
            dlat_v[:, :, g * GW:(g + 1) * GW] = grads.reshape(NK, SUB, GW)
        else:
            dlat_v[:, :, LAT:KD] = grads[:, 0:KD - LAT].reshape(NK, SUB, KD - LAT)
            didx_v[...] = grads[:, GW - ID:GW].reshape(NK, SUB, ID)
    out_lat = pltpu.make_async_copy(dlat_v, dlat_out, fin_sem.at[2])
    out_lat.start()
    out_idx = pltpu.make_async_copy(didx_v, didx_out, fin_sem.at[3])
    out_idx.start()
    for g in range(GROUPS):
        loop(1, NK, lambda d: gone(
            home_part(ob, g, peer_k(d)), home_part(orx, g, me_k), o_ss.at[g, d], o_rs.at[g, d]))
    out_lat.wait()
    out_idx.wait()


def body(queries, out_grad, latent_keys, index_queries, index_weights, index_keys, picks):
    hbm = pl.BlockSpec(memory_space=pl.ANY)
    dma = pltpu.SemaphoreType.DMA
    v = pltpu.VMEM
    outs = pl.pallas_call(
        kernel,
        out_shape=[
            jax.ShapeDtypeStruct((HL, KD, QT), BF16),
            jax.ShapeDtypeStruct((NK, SUB, KD), F32),
            jax.ShapeDtypeStruct((QT * JL, ID), F32),
            jax.ShapeDtypeStruct((JL, QT), F32),
            jax.ShapeDtypeStruct((NK, SUB, ID), F32),
        ],
        in_specs=[hbm] * 6 + [pl.BlockSpec(memory_space=pltpu.SMEM)],
        out_specs=[hbm] * 5,
        scratch_shapes=[
            v((KD, ROWS), BF16), v((ROWS, LAT), BF16),
            v((NK, SUB, ID), BF16), v((NK, SUB, W), BF16),
            v((2, SLOTS, SUB, HALF), BF16), v((SLOTS, SUB, HALF), BF16), v((SLOTS, SUB, HALF), BF16),
            v((KEYS, W), BF16),
            v((SLOTS * SUB, CH), BF16), v((SLOTS * SUB, CH), BF16), v((CH, SLOTS * SUB), BF16),
            v((KEYS, ROWS), F32),
            v((KEYS, ROWS), BF16), v((KEYS, ROWS), BF16), v((2, KD, 512), BF16), v((8, ROWS), F32),
            v((8, ROWS), F32), v((8, ROWS), F32),
            v((NS, QJ, ID), BF16), v((NS, JL, QT), F32), v((NS, QJ, 128), F32), v((QL, KEYS), F32),
            v((KEYS, QT), F32),
            v((NZ, QL, KEYS), F32), v((NZ, QL, KEYS), F32), v((NZ, QL, KEYS), F32),
            v((ID, NS * QJ), BF16), v((NS, JL, QT), F32), v((NS, JL, QT), F32),
            v((GROUPS, NZ, CH, GW), BF16), v((GROUPS, NZ, CH, GW), BF16),
            v((GROUPS, NZ, CH, GW), BF16), v((GROUPS, NZ, CH, GW), BF16),
            v((GROUPS, SLOTS * SUB, GW), BF16), v((GROUPS, SLOTS * SUB, GW), BF16),
            v((NK, SUB, KD), F32), v((NK, SUB, ID), F32), v((JL, QT), F32),
            pltpu.SMEM((NK, CAP), jnp.int32),
            dma((4,)), dma((HL,)), dma((NK,)), dma((NS,)), dma((NS,)), dma((NS,)), dma((NS,)),
            dma((2, NK)), dma((2, NK)), dma((2, NS)), dma((2, NS)), dma((HL,)),
            dma((NZ,)), dma((NZ,)), dma((NZ,)), dma((NZ,)),
            dma((GROUPS, NZ)), dma((GROUPS, NZ)), dma((GROUPS, NZ)), dma((GROUPS, NZ)),
            dma((GROUPS, NK)), dma((GROUPS, NK)), dma((NS,)), dma((NS,)), dma((NS,)), dma((NS,)), dma((4,)),
        ],
        compiler_params=pltpu.CompilerParams(
            collective_id=0, has_side_effects=True, vmem_limit_bytes=64 * 1024 * 1024
        ),
        name="sparse_attention_backward",
    )(
        queries.transpose(1, 2, 0),
        out_grad.reshape(ROWS, LAT),
        latent_keys.transpose(0, 2, 1),
        index_queries.reshape(QT * JL, ID),
        index_weights.T,
        index_keys,
        picks,
    )
    def hand_over(*refs):
        given, made, held, sems = refs[:5], refs[5:10], refs[10:15], refs[15]
        parts = []
        for i in range(5):
            count = 4 if i == 0 else 1
            size = given[i].shape[0] // count
            parts += [(i, pl.ds(n * size, size)) for n in range(count)]
        loads = [pltpu.make_async_copy(given[i].at[at], held[i].at[at], sems.at[n]) for n, (i, at) in enumerate(parts)]
        stores = [pltpu.make_async_copy(held[i].at[at], made[i].at[at], sems.at[n]) for n, (i, at) in enumerate(parts)]
        for load in loads:
            load.start()
        for load, store in zip(loads, stores):
            load.wait()
            store.start()
        for store in stores:
            store.wait()

    dq, dlat, diq, diw, didx = pl.pallas_call(
        hand_over,
        out_shape=[jax.ShapeDtypeStruct(o.shape, o.dtype) for o in outs],
        in_specs=[hbm] * 5,
        out_specs=[hbm] * 5,
        scratch_shapes=[v(o.shape, o.dtype) for o in outs] + [dma((8,))],
        compiler_params=pltpu.CompilerParams(vmem_limit_bytes=64 * 1024 * 1024),
        name="hand_over",
    )(*outs)
    return (dq.transpose(2, 0, 1), dlat, diq.reshape(QT, JL, ID), diw.T, didx)


def solution(mesh):
    placed = (
        P("sk", "sq", None),
        P("sk", "sq", None),
        P("sk", None, None),
        P("sk", "sq", None),
        P("sk", "sq"),
        P("sk", None, None),
        P(),
    )
    return jax.shard_map(
        body,
        mesh=mesh,
        in_specs=placed,
        out_specs=(
            P("sk", "sq", None),
            P("sk", "sq", None),
            P("sk", "sq", None),
            P("sk", "sq"),
            P("sk", "sq", None),
        ),
        check_vma=False,
    )
```

```python
import math

import jax
import jax.numpy as jnp
from jax import lax
from jax.experimental import pallas as pl
from jax.experimental.pallas import tpu as pltpu
from jax.sharding import PartitionSpec as P

H = 128
HI = 64
ID = 128
CAP = 2
LAT = 512
KD = 576
ATTN_SCALE = 0.1353
INDEX_SCALE = 1.0 / math.sqrt(ID * HI)
LOG2E = 1.4426950408889634

MESH = pl.DeviceIdType.MESH
F32 = jnp.float32
BF16 = jnp.bfloat16

NK = 16
NS = 8
NZ = 4
SUB = 16
PICKS = 16
CH = PICKS * SUB
KEYS = NS * CH
QT = 128
HL = 16
ROWS = HL * QT
JL = 8
QL = 16
QJ = QL * JL
SLOTS = NK * CAP
W = 768
IO = 640
HALF = W // 2
GW = 256
GROUPS = 3
R = 256
KC = 256


def dot(a, b):
    return jnp.dot(a, b, preferred_element_type=F32)


def dot_nt(a, b):
    return lax.dot_general(a, b, (((1,), (1,)), ((), ())), preferred_element_type=F32)


def dot_tn(a, b):
    return lax.dot_general(a, b, (((0,), (0,)), ((), ())), preferred_element_type=F32)


def iota(shape, axis):
    return lax.broadcasted_iota(jnp.int32, shape, axis)


def ones_where(hit):
    return jnp.where(hit, 1.0, 0.0).astype(BF16)


def kernel(
    q_hbm, do_hbm, lat_hbm, iq_hbm, iw_hbm, idx_hbm, picks,
    dq_out, dlat_out, diq_out, diw_out, didx_out,
    qt, dov, xi, xs, sendb, recv0, recv1, kb, to_slot, to_block, home, sv, pt, dst, dqv, topv, totv, dotv,
    iqr, iwr, wv, lgv, masst, mcr, mzs, mzr, iqt, diws, diwr,
    gs, gcr, gzs, gzr, ob, orx, dlat_v, didx_v, diw_v, found,
    ld_sem, q_sem, lat_sem, iq_ss, iq_rs, iw_ss, iw_rs, xs_ss, xs_rs, ag_ss, ag_rs, dq_sem,
    m_ss, m_rs, mz_ss, mz_rs, g_ss, g_rs, gz_ss, gz_rs, o_ss, o_rs, b_ss, b_rs, v_ss, v_rs, fin_sem,
):
    massq = sv.at[0:QT]
    dlv = sv.at[QT:QT + QJ]
    ikt = sv.at[256:256 + ID]
    gown = sv.at[512:512 + GROUPS * 512, 0:NZ * GW]
    diqs = sv.at[512:512 + NS * QJ, NZ * GW:NZ * GW + ID]

    me_k = lax.axis_index("sk")
    me_s = lax.axis_index("sq")
    z = lax.div(me_s, 2)
    c = lax.rem(me_s, 2)
    zp = lax.rem(z + 1, NZ)
    zo = lax.rem(z + 2, NZ)
    zm = lax.rem(z + 3, NZ)
    mate = z * 2 + (1 - c)

    def remote(src, dst_ref, ss, rs, sk, sq):
        return pltpu.make_async_remote_copy(
            src_ref=src, dst_ref=dst_ref, send_sem=ss, recv_sem=rs,
            device_id=(sq, sk), device_id_type=MESH,
        )

    def send(*what):
        remote(*what).start()

    def gone(src, dst_ref, ss, rs):
        remote(src, dst_ref, ss, rs, me_k, mate).wait_send()

    def arrived(dst_ref, ss, rs):
        remote(dst_ref, dst_ref, ss, rs, me_k, mate).wait_recv()

    def peer_k(d):
        return lax.rem(me_k + d, NK)

    def from_k(d):
        return lax.rem(me_k + NK - d, NK)

    def peer_s(d):
        return lax.rem(me_s + d, NS)

    def from_s(d):
        return lax.rem(me_s + NS - d, NS)

    def span(at, count):
        return pl.ds(pl.multiple_of(at * count, count), count)

    def rows(ref, at, count):
        return ref.at[span(at, count)]

    def loop(lo, hi, step):
        def one(i, carry):
            step(i)
            return carry

        lax.fori_loop(lo, hi, one, 0)

    load_idx = pltpu.make_async_copy(idx_hbm.at[:, span(me_s, SUB), :], xi, ld_sem.at[0])
    load_iq = pltpu.make_async_copy(rows(iq_hbm, me_s, QJ), iqr.at[me_s], ld_sem.at[1])
    load_iw = pltpu.make_async_copy(iw_hbm, iwr.at[me_s], ld_sem.at[2])
    load_do = pltpu.make_async_copy(do_hbm, pt.at[:, 0:LAT], ld_sem.at[3])
    load_lat = [
        pltpu.make_async_copy(lat_hbm.at[b], dst.at[0:KD, b * 128:(b + 1) * 128], lat_sem.at[b]) for b in range(NK)
    ]
    load_q = [pltpu.make_async_copy(q_hbm.at[h], qt.at[:, h * QT:(h + 1) * QT], q_sem.at[h]) for h in range(HL)]
    for load in load_lat + [load_idx]:
        load.start()

    barrier = pltpu.get_barrier_semaphore()

    def greet_k(d):
        pl.semaphore_signal(barrier, inc=1, device_id=(me_s, peer_k(d)), device_id_type=MESH)

    def greet_s(d):
        pl.semaphore_signal(barrier, inc=1, device_id=(peer_s(d), me_k), device_id_type=MESH)

    loop(1, NK, greet_k)
    loop(1, NS, greet_s)

    def picked(t):
        first = jnp.int32(-1)
        second = jnp.int32(-1)
        for p in range(PICKS):
            block = picks[t, p]
            local = block & (NK - 1)
            here = lax.shift_right_logical(block, 4) == me_k
            second = jnp.where(here & (first >= 0), local, second)
            first = jnp.where(here & (first < 0), local, first)
        found[t, 0] = first
        found[t, 1] = second

    loop(0, NK, picked)

    pick_rows = ones_where(iota((SUB, 128), 1) == me_s * SUB + iota((SUB, 128), 0))
    load_idx.wait()
    for b in range(NK):
        load_lat[b].wait()
        xs[b, :, 0:KD] = dot_nt(pick_rows, dst[0:KD, b * 128:(b + 1) * 128]).astype(BF16)
        xs[b, :, KD:IO] = jnp.zeros((SUB, IO - KD), BF16)
        xs[b, :, IO:W] = xi[b]
    cell = iota((SUB, CH), 1) - iota((SUB, CH), 0)

    for load in [load_do] + load_q + [load_iq, load_iw]:
        load.start()

    def pack(t):
        for i in range(CAP):
            block = xs[jnp.maximum(found[t, i], 0)]
            for f in range(2):
                sendb[f, 2 * t + i] = block[:, f * HALF:(f + 1) * HALF]

    loop(0, NK, pack)
    pl.semaphore_wait(barrier, NK - 1 + NS - 1)

    recvb = (recv0, recv1)

    def slots(ref, k):
        return ref.at[pl.ds(2 * k, 2)]

    def fetch(f, d):
        return remote(
            slots(sendb.at[f], peer_k(d)), slots(recvb[f], me_k), xs_ss.at[f, d], xs_rs.at[f, d], peer_k(d), me_s)

    for f in range(2):
        loop(1, NK, lambda d: fetch(f, d).start())
        recvb[f][pl.ds(2 * me_k, 2)] = sendb[f, pl.ds(2 * me_k, 2)]

    def ship_iq(d):
        send(rows(iq_hbm, peer_s(d), QJ), iqr.at[me_s], iq_ss.at[d], iq_rs.at[d], me_k, peer_s(d))
        send(iw_hbm, iwr.at[me_s], iw_ss.at[d], iw_rs.at[d], me_k, peer_s(d))

    loop(1, NS, ship_iq)

    def place(t):
        to_block[span(2 * t, SUB), :] = ones_where(cell == found[t, 0] * SUB)
        to_block[span(2 * t + 1, SUB), :] = ones_where(cell == found[t, 1] * SUB)

    mine = [picks[me_k, p] for p in range(PICKS)]
    owner = [lax.shift_right_logical(block, 4) for block in mine]
    slot = []
    for p in range(PICKS):
        rank = jnp.int32(0)
        for before in range(p):
            rank = rank + jnp.where(owner[before] == owner[p], 1, 0)
        slot.append(owner[p] * CAP + rank)

    def unpick(s):
        pick = jnp.int32(-1)
        for p in range(PICKS):
            pick = jnp.where(slot[p] == s, p, pick)
        to_slot[span(s, SUB), :] = ones_where(cell == pick * SUB)

    loop(0, SLOTS, unpick)
    loop(0, NK, place)
    home[...] = to_block[...].T
    i0, i1 = iota((CH, CH), 0), iota((CH, CH), 1)
    swap = ones_where(i1 == lax.rem(i0, 16) * 16 + lax.div(i0, 16))
    load_do.wait()
    for g in range(QT // 16):
        turned = dot(swap, pt[g * CH:(g + 1) * CH, 0:LAT]).astype(BF16)
        for h in range(HL):
            dov[h * QT + g * 16:h * QT + (g + 1) * 16, :] = turned[h * 16:(h + 1) * 16]
    for load in load_q:
        load.wait()
    topv[...] = jnp.full(topv.shape, -jnp.inf, F32)
    totv[...] = jnp.zeros_like(totv)
    dotv[...] = jnp.zeros_like(dotv)
    masst[...] = jnp.zeros_like(masst)

    load_iq.wait()
    load_iw.wait()

    def iq_here(d):
        arrived(iqr.at[from_s(d)], iq_ss.at[d], iq_rs.at[d])
        arrived(iwr.at[from_s(d)], iw_ss.at[d], iw_rs.at[d])

    loop(1, NS, iq_here)
    my_query = iota((QL, JL, 128), 2) == me_s * QL + iota((QL, JL, 128), 0)

    def weigh(src):
        weight = jnp.where(my_query, iwr[src][None], 0.0)
        weight = jnp.sum(weight, axis=2, keepdims=True).reshape(QJ, 1)
        wv[src] = jnp.broadcast_to(weight, (QJ, 128))
        iqt[:, span(src, 128)] = iqr[src].T

    loop(0, NS, weigh)

    fwd_from = jnp.where(c == 0, zm, zp)
    fwd_to = jnp.where(c == 0, zp, zm)
    c2 = ATTN_SCALE * LOG2E

    def chunk_ref(chunk, f):
        return kb.at[span(chunk, CH), f * HALF:(f + 1) * HALF]

    routes = (
        (me_s, mate),
        (me_s, fwd_to * 2 + c),
        (me_s, fwd_from * 2 + c),
        (fwd_from * 2 + c, fwd_to * 2 + c),
        (fwd_from * 2 + c, mate),
        (fwd_to * 2 + c, mate),
        (zo * 2 + c, mate),
    )

    def pass_on(f, *which):
        for lane in which:
            chunk, sq = routes[lane]
            send(chunk_ref(chunk, f), chunk_ref(chunk, f), ag_ss.at[f, lane], ag_rs.at[f, chunk], me_k, sq)

    def chunk_here(f, chunk):
        arrived(chunk_ref(chunk, f), ag_ss.at[f, 0], ag_rs.at[f, chunk])

    def meet(chunk):
        at = span(chunk, CH)

        for lo in range(0, ROWS, 512):
            lane = slice(lo, lo + 512)
            s = dot(kb[at, 0:KD], qt[:, lane]) * c2
            dp = dot_nt(kb[at, 0:LAT], dov[lane, :])
            sv[at, lane] = s
            s = s.reshape(CH // 8, 8, 512)
            old = topv[:, lane]
            top = jnp.maximum(old, jnp.max(s, axis=0))
            e = jnp.exp2(s - top[None])
            fade = jnp.exp2(old - top)
            topv[:, lane] = top
            totv[:, lane] = totv[:, lane] * fade + jnp.sum(e, axis=0)
            dotv[:, lane] = dotv[:, lane] * fade + jnp.sum(e * dp.reshape(CH // 8, 8, 512), axis=0)

        keys = kb[at, IO:W]
        acc = jnp.zeros((QJ, CH), F32)
        for src in range(NS):
            acc = acc + jnp.maximum(dot_nt(iqr[src], keys), 0.0) * jnp.tile(wv[src], (1, CH // 128))
        lgv[:, at] = INDEX_SCALE * jnp.sum(acc.reshape(QL, JL, CH), axis=1)

    for f in range(2):
        loop(1, NK, lambda d: fetch(f, d).wait_recv())
        for p in range(PICKS):
            kb[pl.ds(pl.multiple_of(me_s * CH + p * SUB, SUB), SUB), f * HALF:(f + 1) * HALF] = recvb[f][slot[p]]
        pass_on(f, 0, 1, 2)

    def via_from(f):
        chunk_here(f, fwd_from * 2 + c)
        pass_on(f, 3, 4)

    def via_to(f):
        chunk_here(f, fwd_to * 2 + c)
        pass_on(f, 5)

    def via_far(f):
        chunk_here(f, zo * 2 + c)
        pass_on(f, 6)

    def gather_step(i):
        side = jnp.where(
            i < 2, z, jnp.where((i == 2) | (i == 5), fwd_from, jnp.where((i == 3) | (i == 4), fwd_to, zo))
        )
        own_core = lax.rem(i, 2) == 0

        @pl.when(i == 1)
        def _():
            via_from(0)
            via_to(0)

        @pl.when(i == 2)
        def _():
            via_from(1)

        @pl.when(i == 4)
        def _():
            via_to(1)
            via_far(0)

        @pl.when(i == 6)
        def _():
            via_far(1)

        @pl.when(jnp.logical_not(own_core))
        def _():
            for f in range(2):
                chunk_here(f, side * 2 + 1 - c)

        meet(side * 2 + jnp.where(own_core, c, 1 - c))

    loop(0, NS, gather_step)

    def attend(step):
        at = span(step, R)
        do = dov[at, :]
        top = jnp.max(topv[:, at], axis=0, keepdims=True)
        fade = jnp.exp2(topv[:, at] - top)
        total = jnp.sum(totv[:, at] * fade, axis=0, keepdims=True)
        rowdot = jnp.sum(dotv[:, at] * fade, axis=0, keepdims=True) / total
        top = top + jnp.log2(total)
        for k in range(0, KEYS, KC):
            dp = dot_nt(kb[k:k + KC, 0:LAT], do)
            p = jnp.exp2(sv[k:k + KC, at] - top)
            pt[k:k + KC, at] = p.astype(BF16)
            dst[k:k + KC, at] = (p * (dp - rowdot)).astype(BF16)
            heads = p[:, 0:QT]
            for h in range(QT, R, QT):
                heads = heads + p[:, h:h + QT]
            masst[k:k + KC, :] += heads

    loop(0, ROWS // R, attend)

    for k in range(0, KEYS, KC):
        massq[:, k:k + KC] = masst[k:k + KC, :].T

    def mass_pair(i):
        send(rows(massq, 2 * i + (1 - c), QL), mcr.at[i], m_ss.at[i], m_rs.at[i], me_k, mate)

    loop(0, NZ, mass_pair)

    def at_step(i):
        return jnp.where(i == 0, zo, jnp.where(i == 1, fwd_from, jnp.where(i == 2, fwd_to, z)))

    to_sq = fwd_to * 2 + c
    from_sq = fwd_from * 2 + c

    def of_chip(g, i):
        there = at_step(i)
        arrived(gcr.at[g, there], g_ss.at[g, there], g_rs.at[g, there])
        return gown[span(2 * g + c, CH), span(i, GW)] + gcr[g, there].astype(F32)

    def to_mate(g, i):
        there = at_step(i)
        gs[g, there] = gown[span(2 * g + 1 - c, CH), span(i, GW)].astype(BF16)
        send(gs.at[g, there], gcr.at[g, there], g_ss.at[g, there], g_rs.at[g, there], me_k, mate)

    def along(g, way, sq):
        send(gzs.at[g, way], gzr.at[g, way], gz_ss.at[g, way], gz_rs.at[g, way], me_k, sq)

    def relay(g):
        gzs[g, 0] = of_chip(g, 0).astype(BF16)
        along(g, 0, to_sq)

    def back(g):
        gzs[g, 1] = of_chip(g, 1).astype(BF16)
        along(g, 1, from_sq)

    def onward(g):
        arrived(gzr.at[g, 0], gz_ss.at[g, 0], gz_rs.at[g, 0])
        gzs[g, 2] = (of_chip(g, 2) + gzr[g, 0].astype(F32)).astype(BF16)
        along(g, 2, to_sq)

    def key_group(g, acts):
        lo = g * GW

        def step(i):
            at = span(at_step(i), 2 * CH)
            gown[g * 512:(g + 1) * 512, span(i, GW)] = (
                dot_nt(dst[at, :], qt[lo:lo + GW, :]) * ATTN_SCALE + dot(pt[at, :], dov[:, lo:lo + GW])
            )
            to_mate(g, i)
            for n, act in acts:
                pl.when(i == n)(act)

        loop(0, NZ, step)

    def rope_part(i):
        at = span(at_step(i), 2 * CH)
        rope = dot_nt(dst[at, :], qt[LAT:KD, :]) * ATTN_SCALE
        lane = pl.ds(pl.multiple_of(i * GW, 128), 128)
        gown[1024:1536, lane] = jnp.concatenate([rope, jnp.zeros((2 * CH, 128 - KD + LAT), F32)], axis=1)

    def index_pair(i):
        lane = pl.ds(pl.multiple_of(i * GW + 128, 128), 128)
        gown[1024:1536, lane] = masst[span(at_step(i), 2 * CH), :]
        to_mate(2, i)

    def ship_home(g):
        acc = of_chip(g, 3)
        for way in (1, 2) if g < 2 else (0, 1, 2):
            arrived(gzr.at[g, way], gz_ss.at[g, way], gz_rs.at[g, way])
            acc = acc + gzr[g, way].astype(F32)
        ob[g] = dot(to_slot[...], acc.astype(BF16)).astype(BF16)
        loop(1, NK, lambda d: send(
            home_part(ob, g, peer_k(d)), home_part(orx, g, me_k), o_ss.at[g, d], o_rs.at[g, d], peer_k(d), me_s))
        own = span(me_k, CAP * SUB)
        orx[g, own, :] = ob[g, own, :]

    def home_part(ref, g, k):
        return ref.at[g, span(k, CAP * SUB), :]

    def mass_sum(there):
        arrived(mcr.at[there], m_ss.at[there], m_rs.at[there])
        return massq[span(2 * there + c, QL), :] + mcr[there]

    def mass_first():
        mzs[0] = mass_sum(zo)
        send(mzs.at[0], mzr.at[0], mz_ss.at[0], mz_rs.at[0], me_k, to_sq)
        mzs[1] = mass_sum(fwd_from)
        send(mzs.at[1], mzr.at[1], mz_ss.at[1], mz_rs.at[1], me_k, from_sq)

    def mass_onward():
        arrived(mzr.at[0], mz_ss.at[0], mz_rs.at[0])
        mzs[2] = mass_sum(fwd_to) + mzr[0]
        send(mzs.at[2], mzr.at[2], mz_ss.at[2], mz_rs.at[2], me_k, to_sq)
        mzs[3] = mass_sum(z)

    def dq_copy(head):
        step = lax.div(head, 4)
        lane = span(lax.rem(head, 4), QT)
        return pltpu.make_async_copy(dqv.at[lax.rem(step, 2), :, lane], dq_out.at[head], dq_sem.at[head])

    def query_grad(step):
        at = span(step, 512)
        grad = (dot_tn(kb[:, 0:KD], dst[:, at]) * ATTN_SCALE).astype(BF16)

        @pl.when(step >= 2)
        def _():
            for h in range(4):
                dq_copy((step - 2) * 4 + h).wait()

        dqv[lax.rem(step, 2)] = grad
        for h in range(4):
            dq_copy(step * 4 + h).start()

    key_group(0, ((1, lambda: relay(0)), (2, lambda: back(0)), (3, mass_first)))
    key_group(1, ((1, lambda: relay(1)), (1, lambda: onward(0)), (2, lambda: back(1)), (3, mass_onward)))
    loop(0, NZ, rope_part)
    onward(1)
    ship_home(0)
    loop(0, 1, query_grad)

    logits = lgv[...]
    e = jnp.exp(logits - jnp.max(logits, axis=1, keepdims=True))
    guess = e / jnp.sum(e, axis=1, keepdims=True)
    mass = mzs[3]
    for way in (1, 2):
        arrived(mzr.at[way], mz_ss.at[way], mz_rs.at[way])
        mass = mass + mzr[way]
    dlogit = INDEX_SCALE * (guess - mass * (1.0 / H))
    dlv[...] = jnp.broadcast_to(dlogit[:, None, :], (QL, JL, KEYS)).reshape(QJ, KEYS)
    ikt[...] = jnp.zeros(ikt.shape, F32)

    def index_part(src):
        sim = dot_nt(iqr[src], kb[:, IO:W])
        dl = dlv[...]
        ds = jnp.where(sim > 0, dl * jnp.tile(wv[src], (1, KEYS // 128)), 0.0).astype(BF16)
        dw = jnp.sum(dl * jnp.maximum(sim, 0.0), axis=1, keepdims=True).reshape(QL, JL, 1)
        diws[src] = jnp.sum(jnp.where(my_query, dw, 0.0), axis=0)
        diqs[span(src, QJ), :] = dot(ds, kb[:, IO:W])
        ikt[...] += dot(iqt[:, span(src, 128)], ds)

    loop(0, NS, index_part)

    def ship_grads(d):
        there = peer_s(d)
        send(rows(diqs, there, QJ), rows(diq_out, me_s, QJ), b_ss.at[d], b_rs.at[d], me_k, there)
        send(diws.at[there], diwr.at[me_s], v_ss.at[d], v_rs.at[d], me_k, there)

    loop(1, NS, ship_grads)
    diwr[me_s] = diws[me_s]
    here_iq = pltpu.make_async_copy(rows(diqs, me_s, QJ), rows(diq_out, me_s, QJ), fin_sem.at[0])
    here_iq.start()

    for k in range(0, KEYS, KC):
        masst[k:k + KC, :] = ikt[:, k:k + KC].T

    loop(0, NZ, index_pair)
    ship_home(1)
    for way, sq in ((0, zo * 2 + c), (1, from_sq), (2, to_sq)):
        gzs[2, way] = of_chip(2, way).astype(BF16)
        along(2, way, sq)
    loop(1, 4, query_grad)
    ship_home(2)

    def grads_here(d):
        arrived(rows(diq_out, from_s(d), QJ), b_ss.at[d], b_rs.at[d])
        arrived(diwr.at[from_s(d)], v_ss.at[d], v_rs.at[d])

    loop(1, NS, grads_here)
    weight_grad = diwr[0]
    for src in range(1, NS):
        weight_grad = weight_grad + diwr[src]
    diw_v[...] = weight_grad
    out_iw = pltpu.make_async_copy(diw_v, diw_out, fin_sem.at[1])
    out_iw.start()

    def sent_s(d):
        gone(rows(iq_hbm, peer_s(d), QJ), iqr.at[me_s], iq_ss.at[d], iq_rs.at[d])
        gone(iw_hbm, iwr.at[me_s], iw_ss.at[d], iw_rs.at[d])
        gone(rows(diqs, peer_s(d), QJ), rows(diq_out, me_s, QJ), b_ss.at[d], b_rs.at[d])
        gone(diws.at[peer_s(d)], diwr.at[me_s], v_ss.at[d], v_rs.at[d])

    loop(1, NS, sent_s)
    for f in range(2):
        for lane, (chunk, _) in enumerate(routes):
            gone(chunk_ref(chunk, f), chunk_ref(chunk, f), ag_ss.at[f, lane], ag_rs.at[f, 0])
        loop(1, NK, lambda d: fetch(f, d).wait_send())

    def sent_pair(i):
        gone(rows(massq, 2 * i + (1 - c), QL), mcr.at[i], m_ss.at[i], m_rs.at[i])
        for g in range(GROUPS):
            gone(gs.at[g, i], gcr.at[g, i], g_ss.at[g, i], g_rs.at[g, i])

    loop(0, NZ, sent_pair)
    for way in range(3):
        gone(mzs.at[way], mzr.at[way], mz_ss.at[way], mz_rs.at[way])
        for g in range(GROUPS):
            gone(gzs.at[g, way], gzr.at[g, way], gz_ss.at[g, way], gz_rs.at[g, way])

    loop(HL // 2, HL, lambda h: dq_copy(h).wait())
    here_iq.wait()
    out_iw.wait()

    for g in range(GROUPS):
        loop(1, NK, lambda d: arrived(home_part(orx, g, from_k(d)), o_ss.at[g, d], o_rs.at[g, d]))
        grads = dot(home[...], orx[g])
        if g < 2:
            dlat_v[:, :, g * GW:(g + 1) * GW] = grads.reshape(NK, SUB, GW)
        else:
            dlat_v[:, :, LAT:KD] = grads[:, 0:KD - LAT].reshape(NK, SUB, KD - LAT)
            didx_v[...] = grads[:, GW - ID:GW].reshape(NK, SUB, ID)
    out_lat = pltpu.make_async_copy(dlat_v, dlat_out, fin_sem.at[2])
    out_lat.start()
    out_idx = pltpu.make_async_copy(didx_v, didx_out, fin_sem.at[3])
    out_idx.start()
    for g in range(GROUPS):
        loop(1, NK, lambda d: gone(
            home_part(ob, g, peer_k(d)), home_part(orx, g, me_k), o_ss.at[g, d], o_rs.at[g, d]))
    out_lat.wait()
    out_idx.wait()


def body(queries, out_grad, latent_keys, index_queries, index_weights, index_keys, picks):
    hbm = pl.BlockSpec(memory_space=pl.ANY)
    dma = pltpu.SemaphoreType.DMA
    v = pltpu.VMEM
    outs = pl.pallas_call(
        kernel,
        out_shape=[
            jax.ShapeDtypeStruct((HL, KD, QT), BF16),
            jax.ShapeDtypeStruct((NK, SUB, KD), F32),
            jax.ShapeDtypeStruct((QT * JL, ID), F32),
            jax.ShapeDtypeStruct((JL, QT), F32),
            jax.ShapeDtypeStruct((NK, SUB, ID), F32),
        ],
        in_specs=[hbm] * 6 + [pl.BlockSpec(memory_space=pltpu.SMEM)],
        out_specs=[hbm] * 5,
        scratch_shapes=[
            v((KD, ROWS), BF16), v((ROWS, LAT), BF16),
            v((NK, SUB, ID), BF16), v((NK, SUB, W), BF16),
            v((2, SLOTS, SUB, HALF), BF16), v((SLOTS, SUB, HALF), BF16), v((SLOTS, SUB, HALF), BF16),
            v((KEYS, W), BF16),
            v((SLOTS * SUB, CH), BF16), v((SLOTS * SUB, CH), BF16), v((CH, SLOTS * SUB), BF16),
            v((KEYS, ROWS), F32),
            v((KEYS, ROWS), BF16), v((KEYS, ROWS), BF16), v((2, KD, 512), BF16), v((8, ROWS), F32),
            v((8, ROWS), F32), v((8, ROWS), F32),
            v((NS, QJ, ID), BF16), v((NS, JL, QT), F32), v((NS, QJ, 128), F32), v((QL, KEYS), F32),
            v((KEYS, QT), F32),
            v((NZ, QL, KEYS), F32), v((NZ, QL, KEYS), F32), v((NZ, QL, KEYS), F32),
            v((ID, NS * QJ), BF16), v((NS, JL, QT), F32), v((NS, JL, QT), F32),
            v((GROUPS, NZ, CH, GW), BF16), v((GROUPS, NZ, CH, GW), BF16),
            v((GROUPS, NZ, CH, GW), BF16), v((GROUPS, NZ, CH, GW), BF16),
            v((GROUPS, SLOTS * SUB, GW), BF16), v((GROUPS, SLOTS * SUB, GW), BF16),
            v((NK, SUB, KD), F32), v((NK, SUB, ID), F32), v((JL, QT), F32),
            pltpu.SMEM((NK, CAP), jnp.int32),
            dma((4,)), dma((HL,)), dma((NK,)), dma((NS,)), dma((NS,)), dma((NS,)), dma((NS,)),
            dma((2, NK)), dma((2, NK)), dma((2, NS)), dma((2, NS)), dma((HL,)),
            dma((NZ,)), dma((NZ,)), dma((NZ,)), dma((NZ,)),
            dma((GROUPS, NZ)), dma((GROUPS, NZ)), dma((GROUPS, NZ)), dma((GROUPS, NZ)),
            dma((GROUPS, NK)), dma((GROUPS, NK)), dma((NS,)), dma((NS,)), dma((NS,)), dma((NS,)), dma((4,)),
        ],
        compiler_params=pltpu.CompilerParams(
            collective_id=0, has_side_effects=True, vmem_limit_bytes=64 * 1024 * 1024
        ),
        name="sparse_attention_backward",
    )(
        queries.transpose(1, 2, 0),
        out_grad.reshape(ROWS, LAT),
        latent_keys.transpose(0, 2, 1),
        index_queries.reshape(QT * JL, ID),
        index_weights.T,
        index_keys,
        picks,
    )
    def hand_over(*refs):
        given, made, held, sems = refs[:5], refs[5:10], refs[10:15], refs[15]
        parts = []
        for i in range(5):
            count = 4 if i == 0 else 1
            size = given[i].shape[0] // count
            parts += [(i, pl.ds(n * size, size)) for n in range(count)]
        loads = [pltpu.make_async_copy(given[i].at[at], held[i].at[at], sems.at[n]) for n, (i, at) in enumerate(parts)]
        stores = [pltpu.make_async_copy(held[i].at[at], made[i].at[at], sems.at[n]) for n, (i, at) in enumerate(parts)]
        for load in loads:
            load.start()
        for load, store in zip(loads, stores):
            load.wait()
            store.start()
        for store in stores:
            store.wait()

    dq, dlat, diq, diw, didx = pl.pallas_call(
        hand_over,
        out_shape=[jax.ShapeDtypeStruct(o.shape, o.dtype) for o in outs],
        in_specs=[hbm] * 5,
        out_specs=[hbm] * 5,
        scratch_shapes=[v(o.shape, o.dtype) for o in outs] + [dma((8,))],
        compiler_params=pltpu.CompilerParams(vmem_limit_bytes=64 * 1024 * 1024),
        name="hand_over",
    )(*outs)
    return (dq.transpose(2, 0, 1), dlat, diq.reshape(QT, JL, ID), diw.T, didx)


def solution(mesh):
    placed = (
        P("sk", "sq", None),
        P("sk", "sq", None),
        P("sk", None, None),
        P("sk", "sq", None),
        P("sk", "sq"),
        P("sk", None, None),
        P(),
    )
    return jax.shard_map(
        body,
        mesh=mesh,
        in_specs=placed,
        out_specs=(
            P("sk", "sq", None),
            P("sk", "sq", None),
            P("sk", "sq", None),
            P("sk", "sq"),
            P("sk", "sq", None),
        ),
        check_vma=False,
    )
```

```python
import math

import jax
import jax.numpy as jnp
from jax import lax
from jax.experimental import pallas as pl
from jax.experimental.pallas import tpu as pltpu
from jax.sharding import PartitionSpec as P

H = 128
HI = 64
ID = 128
CAP = 2
LAT = 512
KD = 576
ATTN_SCALE = 0.1353
INDEX_SCALE = 1.0 / math.sqrt(ID * HI)
LOG2E = 1.4426950408889634

MESH = pl.DeviceIdType.MESH
F32 = jnp.float32
BF16 = jnp.bfloat16

NK = 16
NS = 8
NZ = 4
SUB = 16
PICKS = 16
CH = PICKS * SUB
KEYS = NS * CH
QT = 128
HL = 16
ROWS = HL * QT
JL = 8
QL = 16
QJ = QL * JL
SLOTS = NK * CAP
W = 768
IO = 640
HALF = W // 2
GW = 256
WIDTHS = (256, 256, 128, 128)
GROUPS = len(WIDTHS)
R = 256
KC = 256


def dot(a, b):
    return jnp.dot(a, b, preferred_element_type=F32)


def dot_nt(a, b):
    return lax.dot_general(a, b, (((1,), (1,)), ((), ())), preferred_element_type=F32)


def dot_tn(a, b):
    return lax.dot_general(a, b, (((0,), (0,)), ((), ())), preferred_element_type=F32)


def iota(shape, axis):
    return lax.broadcasted_iota(jnp.int32, shape, axis)


def ones_where(hit):
    return jnp.where(hit, 1.0, 0.0).astype(BF16)


def kernel(
    q_hbm, do_hbm, lat_hbm, iq_hbm, iw_hbm, idx_hbm, picks,
    dq_out, dlat_out, diq_out, diw_out, didx_out,
    qt, dov, xi, xs, sendb, recv0, recv1, kb, to_slot, to_block, home, sv, pt, dst, dqv, topv, totv, dotv,
    iqr, iwr, wv, lgv, masst, mcr, mzs, mzr, iqt, diws, diwr,
    gs, gcr, gzs, gzr, ob, orx, dlat_v, didx_v, diw_v, found,
    ld_sem, q_sem, lat_sem, iq_ss, iq_rs, iw_ss, iw_rs, xs_ss, xs_rs, ag_ss, ag_rs, dq_sem,
    m_ss, m_rs, mz_ss, mz_rs, g_ss, g_rs, gz_ss, gz_rs, o_ss, o_rs, b_ss, b_rs, v_ss, v_rs, fin_sem,
):
    massq = sv.at[0:QT]
    dlv = sv.at[QT:QT + QJ]
    ikt = sv.at[256:256 + ID]
    gown = sv.at[512:512 + 3 * 512, 0:NZ * GW]
    diqs = sv.at[512:512 + NS * QJ, NZ * GW:NZ * GW + ID]

    me_k = lax.axis_index("sk")
    me_s = lax.axis_index("sq")
    z = lax.div(me_s, 2)
    c = lax.rem(me_s, 2)
    zp = lax.rem(z + 1, NZ)
    zo = lax.rem(z + 2, NZ)
    zm = lax.rem(z + 3, NZ)
    mate = z * 2 + (1 - c)

    def remote(src, dst_ref, ss, rs, sk, sq):
        return pltpu.make_async_remote_copy(
            src_ref=src, dst_ref=dst_ref, send_sem=ss, recv_sem=rs,
            device_id=(sq, sk), device_id_type=MESH,
        )

    def send(*what):
        remote(*what).start()

    def gone(src, dst_ref, ss, rs):
        remote(src, dst_ref, ss, rs, me_k, mate).wait_send()

    def arrived(dst_ref, ss, rs):
        remote(dst_ref, dst_ref, ss, rs, me_k, mate).wait_recv()

    def peer_k(d):
        return lax.rem(me_k + d, NK)

    def from_k(d):
        return lax.rem(me_k + NK - d, NK)

    def peer_s(d):
        return lax.rem(me_s + d, NS)

    def from_s(d):
        return lax.rem(me_s + NS - d, NS)

    def span(at, count):
        return pl.ds(pl.multiple_of(at * count, count), count)

    def rows(ref, at, count):
        return ref.at[span(at, count)]

    def loop(lo, hi, step):
        def one(i, carry):
            step(i)
            return carry

        lax.fori_loop(lo, hi, one, 0)

    load_idx = pltpu.make_async_copy(idx_hbm.at[:, span(me_s, SUB), :], xi, ld_sem.at[0])
    load_iq = pltpu.make_async_copy(rows(iq_hbm, me_s, QJ), iqr.at[me_s], ld_sem.at[1])
    load_iw = pltpu.make_async_copy(iw_hbm, iwr.at[me_s], ld_sem.at[2])
    load_do = pltpu.make_async_copy(do_hbm, pt.at[:, 0:LAT], ld_sem.at[3])
    load_lat = [
        pltpu.make_async_copy(lat_hbm.at[b], dst.at[0:KD, b * 128:(b + 1) * 128], lat_sem.at[b]) for b in range(NK)
    ]
    load_q = [pltpu.make_async_copy(q_hbm.at[h], qt.at[:, h * QT:(h + 1) * QT], q_sem.at[h]) for h in range(HL)]
    for load in load_lat + [load_idx]:
        load.start()

    barrier = pltpu.get_barrier_semaphore()

    def greet_k(d):
        pl.semaphore_signal(barrier, inc=1, device_id=(me_s, peer_k(d)), device_id_type=MESH)

    def greet_s(d):
        pl.semaphore_signal(barrier, inc=1, device_id=(peer_s(d), me_k), device_id_type=MESH)

    loop(1, NK, greet_k)
    loop(1, NS, greet_s)

    def picked(t):
        first = jnp.int32(-1)
        second = jnp.int32(-1)
        for p in range(PICKS):
            block = picks[t, p]
            local = block & (NK - 1)
            here = lax.shift_right_logical(block, 4) == me_k
            second = jnp.where(here & (first >= 0), local, second)
            first = jnp.where(here & (first < 0), local, first)
        found[t, 0] = first
        found[t, 1] = second

    loop(0, NK, picked)

    pick_rows = ones_where(iota((SUB, 128), 1) == me_s * SUB + iota((SUB, 128), 0))
    load_idx.wait()
    for b in range(NK):
        load_lat[b].wait()
        xs[b, :, 0:KD] = dot_nt(pick_rows, dst[0:KD, b * 128:(b + 1) * 128]).astype(BF16)
        xs[b, :, KD:IO] = jnp.zeros((SUB, IO - KD), BF16)
        xs[b, :, IO:W] = xi[b]
    cell = iota((SUB, CH), 1) - iota((SUB, CH), 0)

    for load in [load_do] + load_q + [load_iq, load_iw]:
        load.start()

    def pack(t):
        for i in range(CAP):
            block = xs[jnp.maximum(found[t, i], 0)]
            for f in range(2):
                sendb[f, 2 * t + i] = block[:, f * HALF:(f + 1) * HALF]

    loop(0, NK, pack)
    pl.semaphore_wait(barrier, NK - 1 + NS - 1)

    recvb = (recv0, recv1)

    def slots(ref, k):
        return ref.at[pl.ds(2 * k, 2)]

    def fetch(f, d):
        return remote(
            slots(sendb.at[f], peer_k(d)), slots(recvb[f], me_k), xs_ss.at[f, d], xs_rs.at[f, d], peer_k(d), me_s)

    for f in range(2):
        loop(1, NK, lambda d: fetch(f, d).start())
        recvb[f][pl.ds(2 * me_k, 2)] = sendb[f, pl.ds(2 * me_k, 2)]

    def ship_iq(d):
        send(rows(iq_hbm, peer_s(d), QJ), iqr.at[me_s], iq_ss.at[d], iq_rs.at[d], me_k, peer_s(d))
        send(iw_hbm, iwr.at[me_s], iw_ss.at[d], iw_rs.at[d], me_k, peer_s(d))

    loop(1, NS, ship_iq)

    def place(t):
        to_block[span(2 * t, SUB), :] = ones_where(cell == found[t, 0] * SUB)
        to_block[span(2 * t + 1, SUB), :] = ones_where(cell == found[t, 1] * SUB)

    mine = [picks[me_k, p] for p in range(PICKS)]
    owner = [lax.shift_right_logical(block, 4) for block in mine]
    slot = []
    for p in range(PICKS):
        rank = jnp.int32(0)
        for before in range(p):
            rank = rank + jnp.where(owner[before] == owner[p], 1, 0)
        slot.append(owner[p] * CAP + rank)

    def unpick(s):
        pick = jnp.int32(-1)
        for p in range(PICKS):
            pick = jnp.where(slot[p] == s, p, pick)
        to_slot[span(s, SUB), :] = ones_where(cell == pick * SUB)

    loop(0, SLOTS, unpick)
    loop(0, NK, place)
    home[...] = to_block[...].T
    i0, i1 = iota((CH, CH), 0), iota((CH, CH), 1)
    swap = ones_where(i1 == lax.rem(i0, 16) * 16 + lax.div(i0, 16))
    load_do.wait()
    for g in range(QT // 16):
        turned = dot(swap, pt[g * CH:(g + 1) * CH, 0:LAT]).astype(BF16)
        for h in range(HL):
            dov[h * QT + g * 16:h * QT + (g + 1) * 16, :] = turned[h * 16:(h + 1) * 16]
    for load in load_q:
        load.wait()
    topv[...] = jnp.full(topv.shape, -jnp.inf, F32)
    totv[...] = jnp.zeros_like(totv)
    dotv[...] = jnp.zeros_like(dotv)
    masst[...] = jnp.zeros_like(masst)

    load_iq.wait()
    load_iw.wait()

    def iq_here(d):
        arrived(iqr.at[from_s(d)], iq_ss.at[d], iq_rs.at[d])
        arrived(iwr.at[from_s(d)], iw_ss.at[d], iw_rs.at[d])

    loop(1, NS, iq_here)
    my_query = iota((QL, JL, 128), 2) == me_s * QL + iota((QL, JL, 128), 0)

    def weigh(src):
        weight = jnp.where(my_query, iwr[src][None], 0.0)
        weight = jnp.sum(weight, axis=2, keepdims=True).reshape(QJ, 1)
        wv[src] = jnp.broadcast_to(weight, (QJ, 128))
        iqt[:, span(src, 128)] = iqr[src].T

    loop(0, NS, weigh)

    fwd_from = jnp.where(c == 0, zm, zp)
    fwd_to = jnp.where(c == 0, zp, zm)
    c2 = ATTN_SCALE * LOG2E

    def chunk_ref(chunk, f):
        return kb.at[span(chunk, CH), f * HALF:(f + 1) * HALF]

    routes = (
        (me_s, mate),
        (me_s, fwd_to * 2 + c),
        (me_s, fwd_from * 2 + c),
        (fwd_from * 2 + c, fwd_to * 2 + c),
        (fwd_from * 2 + c, mate),
        (fwd_to * 2 + c, mate),
        (zo * 2 + c, mate),
    )

    def pass_on(f, *which):
        for lane in which:
            chunk, sq = routes[lane]
            send(chunk_ref(chunk, f), chunk_ref(chunk, f), ag_ss.at[f, lane], ag_rs.at[f, chunk], me_k, sq)

    def chunk_here(f, chunk):
        arrived(chunk_ref(chunk, f), ag_ss.at[f, 0], ag_rs.at[f, chunk])

    def meet(chunk):
        at = span(chunk, CH)

        for lo in range(0, ROWS, 512):
            lane = slice(lo, lo + 512)
            s = dot(kb[at, 0:KD], qt[:, lane]) * c2
            dp = dot_nt(kb[at, 0:LAT], dov[lane, :])
            sv[at, lane] = s
            s = s.reshape(CH // 8, 8, 512)
            old = topv[:, lane]
            top = jnp.maximum(old, jnp.max(s, axis=0))
            e = jnp.exp2(s - top[None])
            fade = jnp.exp2(old - top)
            topv[:, lane] = top
            totv[:, lane] = totv[:, lane] * fade + jnp.sum(e, axis=0)
            dotv[:, lane] = dotv[:, lane] * fade + jnp.sum(e * dp.reshape(CH // 8, 8, 512), axis=0)

        keys = kb[at, IO:W]
        acc = jnp.zeros((QJ, CH), F32)
        for src in range(NS):
            acc = acc + jnp.maximum(dot_nt(iqr[src], keys), 0.0) * jnp.tile(wv[src], (1, CH // 128))
        lgv[:, at] = INDEX_SCALE * jnp.sum(acc.reshape(QL, JL, CH), axis=1)

    for f in range(2):
        loop(1, NK, lambda d: fetch(f, d).wait_recv())
        for p in range(PICKS):
            kb[pl.ds(pl.multiple_of(me_s * CH + p * SUB, SUB), SUB), f * HALF:(f + 1) * HALF] = recvb[f][slot[p]]
        pass_on(f, 0, 1, 2)

    def via_from(f):
        chunk_here(f, fwd_from * 2 + c)
        pass_on(f, 3, 4)

    def via_to(f):
        chunk_here(f, fwd_to * 2 + c)
        pass_on(f, 5)

    def via_far(f):
        chunk_here(f, zo * 2 + c)
        pass_on(f, 6)

    def gather_step(i):
        side = jnp.where(
            i < 2, z, jnp.where((i == 2) | (i == 5), fwd_from, jnp.where((i == 3) | (i == 4), fwd_to, zo))
        )
        own_core = lax.rem(i, 2) == 0

        @pl.when(i == 1)
        def _():
            via_from(0)
            via_to(0)

        @pl.when(i == 2)
        def _():
            via_from(1)

        @pl.when(i == 4)
        def _():
            via_to(1)
            via_far(0)

        @pl.when(i == 6)
        def _():
            via_far(1)

        @pl.when(jnp.logical_not(own_core))
        def _():
            for f in range(2):
                chunk_here(f, side * 2 + 1 - c)

        meet(side * 2 + jnp.where(own_core, c, 1 - c))

    loop(0, NS, gather_step)

    def attend(step):
        at = span(step, R)
        do = dov[at, :]
        top = jnp.max(topv[:, at], axis=0, keepdims=True)
        fade = jnp.exp2(topv[:, at] - top)
        total = jnp.sum(totv[:, at] * fade, axis=0, keepdims=True)
        rowdot = jnp.sum(dotv[:, at] * fade, axis=0, keepdims=True) / total
        top = top + jnp.log2(total)
        for k in range(0, KEYS, KC):
            dp = dot_nt(kb[k:k + KC, 0:LAT], do)
            p = jnp.exp2(sv[k:k + KC, at] - top)
            pt[k:k + KC, at] = p.astype(BF16)
            dst[k:k + KC, at] = (p * (dp - rowdot)).astype(BF16)
            heads = p[:, 0:QT]
            for h in range(QT, R, QT):
                heads = heads + p[:, h:h + QT]
            masst[k:k + KC, :] += heads

    loop(0, ROWS // R, attend)

    for k in range(0, KEYS, KC):
        massq[:, k:k + KC] = masst[k:k + KC, :].T

    def mass_pair(i):
        send(rows(massq, 2 * i + (1 - c), QL), mcr.at[i], m_ss.at[i], m_rs.at[i], me_k, mate)

    loop(0, NZ, mass_pair)

    def at_step(i):
        return jnp.where(i == 0, zo, jnp.where(i == 1, fwd_from, jnp.where(i == 2, fwd_to, z)))

    to_sq = fwd_to * 2 + c
    from_sq = fwd_from * 2 + c

    def spot(g, core, i):
        rows_at = pl.ds(pl.multiple_of((2 * min(g, 2) + core) * CH, CH), CH)
        return rows_at, pl.ds(pl.multiple_of(i * GW + (128 if g == 3 else 0), 128), WIDTHS[g])

    def cut(ref, g, *at):
        return ref.at[(g, *at, slice(None), slice(0, WIDTHS[g]))]

    def of_chip(g, i):
        there = at_step(i)
        arrived(cut(gcr, g, there), g_ss.at[g, there], g_rs.at[g, there])
        return gown[spot(g, c, i)] + cut(gcr, g, there)[...].astype(F32)

    def to_mate(g, i):
        there = at_step(i)
        cut(gs, g, there)[...] = gown[spot(g, 1 - c, i)].astype(BF16)
        send(cut(gs, g, there), cut(gcr, g, there), g_ss.at[g, there], g_rs.at[g, there], me_k, mate)

    def along(g, way, sq):
        send(cut(gzs, g, way), cut(gzr, g, way), gz_ss.at[g, way], gz_rs.at[g, way], me_k, sq)

    def direct(g):
        for way, sq in ((0, zo * 2 + c), (1, from_sq), (2, to_sq)):
            cut(gzs, g, way)[...] = of_chip(g, way).astype(BF16)
            along(g, way, sq)

    def relay(g):
        gzs[g, 0] = of_chip(g, 0).astype(BF16)
        along(g, 0, to_sq)

    def back(g):
        gzs[g, 1] = of_chip(g, 1).astype(BF16)
        along(g, 1, from_sq)

    def onward(g):
        arrived(gzr.at[g, 0], gz_ss.at[g, 0], gz_rs.at[g, 0])
        gzs[g, 2] = (of_chip(g, 2) + gzr[g, 0].astype(F32)).astype(BF16)
        along(g, 2, to_sq)

    def key_group(g, acts):
        lo = g * GW

        def step(i):
            at = span(at_step(i), 2 * CH)
            gown[g * 512:(g + 1) * 512, span(i, GW)] = (
                dot_nt(dst[at, :], qt[lo:lo + GW, :]) * ATTN_SCALE + dot(pt[at, :], dov[:, lo:lo + GW])
            )
            to_mate(g, i)
            for n, act in acts:
                pl.when(i == n)(act)

        loop(0, NZ, step)

    def rope_part(i):
        at = span(at_step(i), 2 * CH)
        rope = dot_nt(dst[at, :], qt[LAT:KD, :]) * ATTN_SCALE
        lane = pl.ds(pl.multiple_of(i * GW, 128), 128)
        gown[1024:1536, lane] = jnp.concatenate([rope, jnp.zeros((2 * CH, 128 - KD + LAT), F32)], axis=1)
        to_mate(2, i)

    def index_pair(i):
        lane = pl.ds(pl.multiple_of(i * GW + 128, 128), 128)
        gown[1024:1536, lane] = masst[span(at_step(i), 2 * CH), :]
        to_mate(3, i)

    def ship_home(g):
        acc = of_chip(g, 3)
        for way in (1, 2) if g < 2 else (0, 1, 2):
            arrived(cut(gzr, g, way), gz_ss.at[g, way], gz_rs.at[g, way])
            acc = acc + cut(gzr, g, way)[...].astype(F32)
        lanes = slice(0, WIDTHS[g])
        ob[g, :, lanes] = dot(to_slot[...], acc.astype(BF16)).astype(BF16)
        loop(1, NK, lambda d: send(
            home_part(ob, g, peer_k(d)), home_part(orx, g, me_k), o_ss.at[g, d], o_rs.at[g, d], peer_k(d), me_s))
        own = span(me_k, CAP * SUB)
        orx[g, own, lanes] = ob[g, own, lanes]

    def home_part(ref, g, k):
        return ref.at[g, span(k, CAP * SUB), 0:WIDTHS[g]]

    def mass_sum(there):
        arrived(mcr.at[there], m_ss.at[there], m_rs.at[there])
        return massq[span(2 * there + c, QL), :] + mcr[there]

    def mass_first():
        mzs[0] = mass_sum(zo)
        send(mzs.at[0], mzr.at[0], mz_ss.at[0], mz_rs.at[0], me_k, to_sq)
        mzs[1] = mass_sum(fwd_from)
        send(mzs.at[1], mzr.at[1], mz_ss.at[1], mz_rs.at[1], me_k, from_sq)

    def mass_onward():
        arrived(mzr.at[0], mz_ss.at[0], mz_rs.at[0])
        mzs[2] = mass_sum(fwd_to) + mzr[0]
        send(mzs.at[2], mzr.at[2], mz_ss.at[2], mz_rs.at[2], me_k, to_sq)
        mzs[3] = mass_sum(z)

    def dq_copy(head):
        step = lax.div(head, 4)
        lane = span(lax.rem(head, 4), QT)
        return pltpu.make_async_copy(dqv.at[lax.rem(step, 2), :, lane], dq_out.at[head], dq_sem.at[head])

    def query_grad(step):
        at = span(step, 512)
        grad = (dot_tn(kb[:, 0:KD], dst[:, at]) * ATTN_SCALE).astype(BF16)

        @pl.when(step >= 2)
        def _():
            for h in range(4):
                dq_copy((step - 2) * 4 + h).wait()

        dqv[lax.rem(step, 2)] = grad
        for h in range(4):
            dq_copy(step * 4 + h).start()

    key_group(0, ((1, lambda: relay(0)), (2, lambda: back(0)), (3, mass_first)))
    key_group(1, ((1, lambda: relay(1)), (1, lambda: onward(0)), (2, lambda: back(1)), (3, mass_onward)))
    loop(0, NZ, rope_part)
    onward(1)
    ship_home(0)
    loop(0, 1, query_grad)
    direct(2)

    logits = lgv[...]
    e = jnp.exp(logits - jnp.max(logits, axis=1, keepdims=True))
    guess = e / jnp.sum(e, axis=1, keepdims=True)
    mass = mzs[3]
    for way in (1, 2):
        arrived(mzr.at[way], mz_ss.at[way], mz_rs.at[way])
        mass = mass + mzr[way]
    dlogit = INDEX_SCALE * (guess - mass * (1.0 / H))
    dlv[...] = jnp.broadcast_to(dlogit[:, None, :], (QL, JL, KEYS)).reshape(QJ, KEYS)
    ikt[...] = jnp.zeros(ikt.shape, F32)

    def index_part(src):
        sim = dot_nt(iqr[src], kb[:, IO:W])
        dl = dlv[...]
        ds = jnp.where(sim > 0, dl * jnp.tile(wv[src], (1, KEYS // 128)), 0.0).astype(BF16)
        dw = jnp.sum(dl * jnp.maximum(sim, 0.0), axis=1, keepdims=True).reshape(QL, JL, 1)
        diws[src] = jnp.sum(jnp.where(my_query, dw, 0.0), axis=0)
        diqs[span(src, QJ), :] = dot(ds, kb[:, IO:W])
        ikt[...] += dot(iqt[:, span(src, 128)], ds)
        pl.when(src == 3)(lambda: ship_home(1))
        pl.when(src == 6)(lambda: ship_home(2))

    loop(0, NS, index_part)

    def ship_grads(d):
        there = peer_s(d)
        send(rows(diqs, there, QJ), rows(diq_out, me_s, QJ), b_ss.at[d], b_rs.at[d], me_k, there)
        send(diws.at[there], diwr.at[me_s], v_ss.at[d], v_rs.at[d], me_k, there)

    loop(1, NS, ship_grads)
    diwr[me_s] = diws[me_s]
    here_iq = pltpu.make_async_copy(rows(diqs, me_s, QJ), rows(diq_out, me_s, QJ), fin_sem.at[0])
    here_iq.start()

    for k in range(0, KEYS, KC):
        masst[k:k + KC, :] = ikt[:, k:k + KC].T

    loop(0, NZ, index_pair)
    direct(3)
    loop(1, 4, query_grad)
    ship_home(3)

    def grads_here(d):
        arrived(rows(diq_out, from_s(d), QJ), b_ss.at[d], b_rs.at[d])
        arrived(diwr.at[from_s(d)], v_ss.at[d], v_rs.at[d])

    loop(1, NS, grads_here)
    weight_grad = diwr[0]
    for src in range(1, NS):
        weight_grad = weight_grad + diwr[src]
    diw_v[...] = weight_grad
    out_iw = pltpu.make_async_copy(diw_v, diw_out, fin_sem.at[1])
    out_iw.start()

    def sent_s(d):
        gone(rows(iq_hbm, peer_s(d), QJ), iqr.at[me_s], iq_ss.at[d], iq_rs.at[d])
        gone(iw_hbm, iwr.at[me_s], iw_ss.at[d], iw_rs.at[d])
        gone(rows(diqs, peer_s(d), QJ), rows(diq_out, me_s, QJ), b_ss.at[d], b_rs.at[d])
        gone(diws.at[peer_s(d)], diwr.at[me_s], v_ss.at[d], v_rs.at[d])

    loop(1, NS, sent_s)
    for f in range(2):
        for lane, (chunk, _) in enumerate(routes):
            gone(chunk_ref(chunk, f), chunk_ref(chunk, f), ag_ss.at[f, lane], ag_rs.at[f, 0])
        loop(1, NK, lambda d: fetch(f, d).wait_send())

    def sent_pair(i):
        gone(rows(massq, 2 * i + (1 - c), QL), mcr.at[i], m_ss.at[i], m_rs.at[i])
        for g in range(GROUPS):
            gone(cut(gs, g, i), cut(gcr, g, i), g_ss.at[g, i], g_rs.at[g, i])

    loop(0, NZ, sent_pair)
    for way in range(3):
        gone(mzs.at[way], mzr.at[way], mz_ss.at[way], mz_rs.at[way])
        for g in range(GROUPS):
            gone(cut(gzs, g, way), cut(gzr, g, way), gz_ss.at[g, way], gz_rs.at[g, way])

    loop(HL // 2, HL, lambda h: dq_copy(h).wait())
    here_iq.wait()
    out_iw.wait()

    for g in range(GROUPS):
        loop(1, NK, lambda d: arrived(home_part(orx, g, from_k(d)), o_ss.at[g, d], o_rs.at[g, d]))
        grads = dot(home[...], orx[g, :, 0:WIDTHS[g]])
        if g < 2:
            dlat_v[:, :, g * GW:(g + 1) * GW] = grads.reshape(NK, SUB, GW)
        elif g == 2:
            dlat_v[:, :, LAT:KD] = grads[:, 0:KD - LAT].reshape(NK, SUB, KD - LAT)
        else:
            didx_v[...] = grads.reshape(NK, SUB, ID)
    out_lat = pltpu.make_async_copy(dlat_v, dlat_out, fin_sem.at[2])
    out_lat.start()
    out_idx = pltpu.make_async_copy(didx_v, didx_out, fin_sem.at[3])
    out_idx.start()
    for g in range(GROUPS):
        loop(1, NK, lambda d: gone(
            home_part(ob, g, peer_k(d)), home_part(orx, g, me_k), o_ss.at[g, d], o_rs.at[g, d]))
    out_lat.wait()
    out_idx.wait()


def body(queries, out_grad, latent_keys, index_queries, index_weights, index_keys, picks):
    hbm = pl.BlockSpec(memory_space=pl.ANY)
    dma = pltpu.SemaphoreType.DMA
    v = pltpu.VMEM
    outs = pl.pallas_call(
        kernel,
        out_shape=[
            jax.ShapeDtypeStruct((HL, KD, QT), BF16),
            jax.ShapeDtypeStruct((NK, SUB, KD), F32),
            jax.ShapeDtypeStruct((QT * JL, ID), F32),
            jax.ShapeDtypeStruct((JL, QT), F32),
            jax.ShapeDtypeStruct((NK, SUB, ID), F32),
        ],
        in_specs=[hbm] * 6 + [pl.BlockSpec(memory_space=pltpu.SMEM)],
        out_specs=[hbm] * 5,
        scratch_shapes=[
            v((KD, ROWS), BF16), v((ROWS, LAT), BF16),
            v((NK, SUB, ID), BF16), v((NK, SUB, W), BF16),
            v((2, SLOTS, SUB, HALF), BF16), v((SLOTS, SUB, HALF), BF16), v((SLOTS, SUB, HALF), BF16),
            v((KEYS, W), BF16),
            v((SLOTS * SUB, CH), BF16), v((SLOTS * SUB, CH), BF16), v((CH, SLOTS * SUB), BF16),
            v((KEYS, ROWS), F32),
            v((KEYS, ROWS), BF16), v((KEYS, ROWS), BF16), v((2, KD, 512), BF16), v((8, ROWS), F32),
            v((8, ROWS), F32), v((8, ROWS), F32),
            v((NS, QJ, ID), BF16), v((NS, JL, QT), F32), v((NS, QJ, 128), F32), v((QL, KEYS), F32),
            v((KEYS, QT), F32),
            v((NZ, QL, KEYS), F32), v((NZ, QL, KEYS), F32), v((NZ, QL, KEYS), F32),
            v((ID, NS * QJ), BF16), v((NS, JL, QT), F32), v((NS, JL, QT), F32),
            v((GROUPS, NZ, CH, GW), BF16), v((GROUPS, NZ, CH, GW), BF16),
            v((GROUPS, NZ, CH, GW), BF16), v((GROUPS, NZ, CH, GW), BF16),
            v((GROUPS, SLOTS * SUB, GW), BF16), v((GROUPS, SLOTS * SUB, GW), BF16),
            v((NK, SUB, KD), F32), v((NK, SUB, ID), F32), v((JL, QT), F32),
            pltpu.SMEM((NK, CAP), jnp.int32),
            dma((4,)), dma((HL,)), dma((NK,)), dma((NS,)), dma((NS,)), dma((NS,)), dma((NS,)),
            dma((2, NK)), dma((2, NK)), dma((2, NS)), dma((2, NS)), dma((HL,)),
            dma((NZ,)), dma((NZ,)), dma((NZ,)), dma((NZ,)),
            dma((GROUPS, NZ)), dma((GROUPS, NZ)), dma((GROUPS, NZ)), dma((GROUPS, NZ)),
            dma((GROUPS, NK)), dma((GROUPS, NK)), dma((NS,)), dma((NS,)), dma((NS,)), dma((NS,)), dma((4,)),
        ],
        compiler_params=pltpu.CompilerParams(
            collective_id=0, has_side_effects=True, vmem_limit_bytes=64 * 1024 * 1024
        ),
        name="sparse_attention_backward",
    )(
        queries.transpose(1, 2, 0),
        out_grad.reshape(ROWS, LAT),
        latent_keys.transpose(0, 2, 1),
        index_queries.reshape(QT * JL, ID),
        index_weights.T,
        index_keys,
        picks,
    )
    def hand_over(*refs):
        given, made, held, sems = refs[:5], refs[5:10], refs[10:15], refs[15]
        parts = []
        for i in range(5):
            count = 4 if i == 0 else 1
            size = given[i].shape[0] // count
            parts += [(i, pl.ds(n * size, size)) for n in range(count)]
        loads = [pltpu.make_async_copy(given[i].at[at], held[i].at[at], sems.at[n]) for n, (i, at) in enumerate(parts)]
        stores = [pltpu.make_async_copy(held[i].at[at], made[i].at[at], sems.at[n]) for n, (i, at) in enumerate(parts)]
        for load in loads:
            load.start()
        for load, store in zip(loads, stores):
            load.wait()
            store.start()
        for store in stores:
            store.wait()

    dq, dlat, diq, diw, didx = pl.pallas_call(
        hand_over,
        out_shape=[jax.ShapeDtypeStruct(o.shape, o.dtype) for o in outs],
        in_specs=[hbm] * 5,
        out_specs=[hbm] * 5,
        scratch_shapes=[v(o.shape, o.dtype) for o in outs] + [dma((8,))],
        compiler_params=pltpu.CompilerParams(vmem_limit_bytes=64 * 1024 * 1024),
        name="hand_over",
    )(*outs)
    return (dq.transpose(2, 0, 1), dlat, diq.reshape(QT, JL, ID), diw.T, didx)


def solution(mesh):
    placed = (
        P("sk", "sq", None),
        P("sk", "sq", None),
        P("sk", None, None),
        P("sk", "sq", None),
        P("sk", "sq"),
        P("sk", None, None),
        P(),
    )
    return jax.shard_map(
        body,
        mesh=mesh,
        in_specs=placed,
        out_specs=(
            P("sk", "sq", None),
            P("sk", "sq", None),
            P("sk", "sq", None),
            P("sk", "sq"),
            P("sk", "sq", None),
        ),
        check_vma=False,
    )
```

```python
import math

import jax
import jax.numpy as jnp
from jax import lax
from jax.experimental import pallas as pl
from jax.experimental.pallas import tpu as pltpu
from jax.sharding import PartitionSpec as P

H = 128
HI = 64
ID = 128
CAP = 2
LAT = 512
KD = 576
ATTN_SCALE = 0.1353
INDEX_SCALE = 1.0 / math.sqrt(ID * HI)
LOG2E = 1.4426950408889634

MESH = pl.DeviceIdType.MESH
F32 = jnp.float32
BF16 = jnp.bfloat16

NK = 16
NS = 8
NZ = 4
SUB = 16
PICKS = 16
CH = PICKS * SUB
KEYS = NS * CH
QT = 128
HL = 16
ROWS = HL * QT
JL = 8
QL = 16
QJ = QL * JL
SLOTS = NK * CAP
W = 768
IO = 640
HALF = W // 2
GW = 256
WIDTHS = (256, 256, 128, 128)
GROUPS = len(WIDTHS)
R = 256
KC = 256


def dot(a, b):
    return jnp.dot(a, b, preferred_element_type=F32)


def dot_nt(a, b):
    return lax.dot_general(a, b, (((1,), (1,)), ((), ())), preferred_element_type=F32)


def dot_tn(a, b):
    return lax.dot_general(a, b, (((0,), (0,)), ((), ())), preferred_element_type=F32)


def iota(shape, axis):
    return lax.broadcasted_iota(jnp.int32, shape, axis)


def ones_where(hit):
    return jnp.where(hit, 1.0, 0.0).astype(BF16)


def kernel(
    q_hbm, do_hbm, lat_hbm, iq_hbm, iw_hbm, idx_hbm, picks,
    dq_out, dlat_out, diq_out, diw_out, didx_out,
    qt, dov, xi, xs, sendb, recv0, recv1, kb, to_slot, to_block, home, sv, pt, dst, dqv, topv, totv, dotv,
    iqr, iwr, wv, lgv, masst, mcr, mzs, mzr, iqt, diws, diwr,
    gs, gcr, gzs, gzr, ob, orx, dlat_v, didx_v, diw_v, found,
    ld_sem, q_sem, lat_sem, iq_ss, iq_rs, iw_ss, iw_rs, xs_ss, xs_rs, ag_ss, ag_rs, dq_sem,
    m_ss, m_rs, mz_ss, mz_rs, g_ss, g_rs, gz_ss, gz_rs, o_ss, o_rs, b_ss, b_rs, v_ss, v_rs, fin_sem,
):
    massq = sv.at[0:QT]
    dlv = sv.at[QT:QT + QJ]
    ikt = sv.at[256:256 + ID]
    gown = sv.at[512:512 + 3 * 512, 0:NZ * GW]
    diqs = sv.at[512:512 + NS * QJ, NZ * GW:NZ * GW + ID]

    me_k = lax.axis_index("sk")
    me_s = lax.axis_index("sq")
    z = lax.div(me_s, 2)
    c = lax.rem(me_s, 2)
    zp = lax.rem(z + 1, NZ)
    zo = lax.rem(z + 2, NZ)
    zm = lax.rem(z + 3, NZ)
    mate = z * 2 + (1 - c)

    def remote(src, dst_ref, ss, rs, sk, sq):
        return pltpu.make_async_remote_copy(
            src_ref=src, dst_ref=dst_ref, send_sem=ss, recv_sem=rs,
            device_id=(sq, sk), device_id_type=MESH,
        )

    def send(*what):
        remote(*what).start()

    def gone(src, dst_ref, ss, rs):
        remote(src, dst_ref, ss, rs, me_k, mate).wait_send()

    def arrived(dst_ref, ss, rs):
        remote(dst_ref, dst_ref, ss, rs, me_k, mate).wait_recv()

    def peer_k(d):
        return lax.rem(me_k + d, NK)

    def from_k(d):
        return lax.rem(me_k + NK - d, NK)

    def peer_s(d):
        return lax.rem(me_s + d, NS)

    def from_s(d):
        return lax.rem(me_s + NS - d, NS)

    def span(at, count):
        return pl.ds(pl.multiple_of(at * count, count), count)

    def rows(ref, at, count):
        return ref.at[span(at, count)]

    def loop(lo, hi, step):
        def one(i, carry):
            step(i)
            return carry

        lax.fori_loop(lo, hi, one, 0)

    load_idx = pltpu.make_async_copy(idx_hbm.at[:, span(me_s, SUB), :], xi, ld_sem.at[0])
    load_iq = pltpu.make_async_copy(rows(iq_hbm, me_s, QJ), iqr.at[me_s], ld_sem.at[1])
    load_iw = pltpu.make_async_copy(iw_hbm, iwr.at[me_s], ld_sem.at[2])
    load_do = pltpu.make_async_copy(do_hbm, pt.at[:, 0:LAT], ld_sem.at[3])
    load_lat = [
        pltpu.make_async_copy(lat_hbm.at[b], dst.at[0:KD, b * 128:(b + 1) * 128], lat_sem.at[b]) for b in range(NK)
    ]
    load_q = [pltpu.make_async_copy(q_hbm.at[h], qt.at[:, h * QT:(h + 1) * QT], q_sem.at[h]) for h in range(HL)]
    for load in load_lat + [load_idx]:
        load.start()

    barrier = pltpu.get_barrier_semaphore()

    def greet_k(d):
        pl.semaphore_signal(barrier, inc=1, device_id=(me_s, peer_k(d)), device_id_type=MESH)

    def greet_s(d):
        pl.semaphore_signal(barrier, inc=1, device_id=(peer_s(d), me_k), device_id_type=MESH)

    loop(1, NK, greet_k)
    loop(1, NS, greet_s)

    def picked(t):
        first = jnp.int32(-1)
        second = jnp.int32(-1)
        for p in range(PICKS):
            block = picks[t, p]
            local = block & (NK - 1)
            here = lax.shift_right_logical(block, 4) == me_k
            second = jnp.where(here & (first >= 0), local, second)
            first = jnp.where(here & (first < 0), local, first)
        found[t, 0] = first
        found[t, 1] = second

    loop(0, NK, picked)

    pick_rows = ones_where(iota((SUB, 128), 1) == me_s * SUB + iota((SUB, 128), 0))
    load_idx.wait()
    for b in range(NK):
        load_lat[b].wait()
        xs[b, :, 0:KD] = dot_nt(pick_rows, dst[0:KD, b * 128:(b + 1) * 128]).astype(BF16)
        xs[b, :, KD:IO] = jnp.zeros((SUB, IO - KD), BF16)
        xs[b, :, IO:W] = xi[b]
    cell = iota((SUB, CH), 1) - iota((SUB, CH), 0)

    for load in [load_do] + load_q + [load_iq, load_iw]:
        load.start()

    def pack(t):
        for i in range(CAP):
            block = xs[jnp.maximum(found[t, i], 0)]
            for f in range(2):
                sendb[f, 2 * t + i] = block[:, f * HALF:(f + 1) * HALF]

    loop(0, NK, pack)
    pl.semaphore_wait(barrier, NK - 1 + NS - 1)

    recvb = (recv0, recv1)

    def slots(ref, k):
        return ref.at[pl.ds(2 * k, 2)]

    def fetch(f, d):
        return remote(
            slots(sendb.at[f], peer_k(d)), slots(recvb[f], me_k), xs_ss.at[f, d], xs_rs.at[f, d], peer_k(d), me_s)

    for f in range(2):
        loop(1, NK, lambda d: fetch(f, d).start())
        recvb[f][pl.ds(2 * me_k, 2)] = sendb[f, pl.ds(2 * me_k, 2)]

    def ship_iq(d):
        send(rows(iq_hbm, peer_s(d), QJ), iqr.at[me_s], iq_ss.at[d], iq_rs.at[d], me_k, peer_s(d))
        send(iw_hbm, iwr.at[me_s], iw_ss.at[d], iw_rs.at[d], me_k, peer_s(d))

    loop(1, NS, ship_iq)

    def place(t):
        to_block[span(2 * t, SUB), :] = ones_where(cell == found[t, 0] * SUB)
        to_block[span(2 * t + 1, SUB), :] = ones_where(cell == found[t, 1] * SUB)

    mine = [picks[me_k, p] for p in range(PICKS)]
    owner = [lax.shift_right_logical(block, 4) for block in mine]
    slot = []
    for p in range(PICKS):
        rank = jnp.int32(0)
        for before in range(p):
            rank = rank + jnp.where(owner[before] == owner[p], 1, 0)
        slot.append(owner[p] * CAP + rank)

    def unpick(s):
        pick = jnp.int32(-1)
        for p in range(PICKS):
            pick = jnp.where(slot[p] == s, p, pick)
        to_slot[span(s, SUB), :] = ones_where(cell == pick * SUB)

    loop(0, SLOTS, unpick)
    loop(0, NK, place)
    home[...] = to_block[...].T
    i0, i1 = iota((CH, CH), 0), iota((CH, CH), 1)
    swap = ones_where(i1 == lax.rem(i0, 16) * 16 + lax.div(i0, 16))
    load_do.wait()
    for g in range(QT // 16):
        turned = dot(swap, pt[g * CH:(g + 1) * CH, 0:LAT]).astype(BF16)
        for h in range(HL):
            dov[h * QT + g * 16:h * QT + (g + 1) * 16, :] = turned[h * 16:(h + 1) * 16]
    for load in load_q:
        load.wait()
    topv[...] = jnp.full(topv.shape, -jnp.inf, F32)
    totv[...] = jnp.zeros_like(totv)
    dotv[...] = jnp.zeros_like(dotv)
    masst[...] = jnp.zeros_like(masst)

    load_iq.wait()
    load_iw.wait()

    def iq_here(d):
        arrived(iqr.at[from_s(d)], iq_ss.at[d], iq_rs.at[d])
        arrived(iwr.at[from_s(d)], iw_ss.at[d], iw_rs.at[d])

    loop(1, NS, iq_here)
    my_query = iota((QL, JL, 128), 2) == me_s * QL + iota((QL, JL, 128), 0)

    def weigh(src):
        weight = jnp.where(my_query, iwr[src][None], 0.0)
        weight = jnp.sum(weight, axis=2, keepdims=True).reshape(QJ, 1)
        wv[src] = jnp.broadcast_to(weight, (QJ, 128))
        iqt[:, span(src, 128)] = iqr[src].T

    loop(0, NS, weigh)

    fwd_from = jnp.where(c == 0, zm, zp)
    fwd_to = jnp.where(c == 0, zp, zm)
    c2 = ATTN_SCALE * LOG2E

    def chunk_ref(chunk, f):
        return kb.at[span(chunk, CH), f * HALF:(f + 1) * HALF]

    routes = (
        (me_s, mate),
        (me_s, fwd_to * 2 + c),
        (me_s, fwd_from * 2 + c),
        (fwd_from * 2 + c, fwd_to * 2 + c),
        (fwd_from * 2 + c, mate),
        (fwd_to * 2 + c, mate),
        (zo * 2 + c, mate),
    )

    def pass_on(f, *which):
        for lane in which:
            chunk, sq = routes[lane]
            send(chunk_ref(chunk, f), chunk_ref(chunk, f), ag_ss.at[f, lane], ag_rs.at[f, chunk], me_k, sq)

    def chunk_here(f, chunk):
        arrived(chunk_ref(chunk, f), ag_ss.at[f, 0], ag_rs.at[f, chunk])

    def meet(chunk):
        at = span(chunk, CH)

        for lo in range(0, ROWS, 512):
            lane = slice(lo, lo + 512)
            s = dot(kb[at, 0:KD], qt[:, lane]) * c2
            dp = dot_nt(kb[at, 0:LAT], dov[lane, :])
            sv[at, lane] = s
            s = s.reshape(CH // 8, 8, 512)
            old = topv[:, lane]
            top = jnp.maximum(old, jnp.max(s, axis=0))
            e = jnp.exp2(s - top[None])
            fade = jnp.exp2(old - top)
            topv[:, lane] = top
            totv[:, lane] = totv[:, lane] * fade + jnp.sum(e, axis=0)
            dotv[:, lane] = dotv[:, lane] * fade + jnp.sum(e * dp.reshape(CH // 8, 8, 512), axis=0)

        keys = kb[at, IO:W]
        acc = jnp.zeros((QJ, CH), F32)
        for src in range(NS):
            acc = acc + jnp.maximum(dot_nt(iqr[src], keys), 0.0) * jnp.tile(wv[src], (1, CH // 128))
        lgv[:, at] = INDEX_SCALE * jnp.sum(acc.reshape(QL, JL, CH), axis=1)

    for f in range(2):
        loop(1, NK, lambda d: fetch(f, d).wait_recv())
        for p in range(PICKS):
            kb[pl.ds(pl.multiple_of(me_s * CH + p * SUB, SUB), SUB), f * HALF:(f + 1) * HALF] = recvb[f][slot[p]]
        pass_on(f, 0, 1, 2)

    def via_from(f):
        chunk_here(f, fwd_from * 2 + c)
        pass_on(f, 3, 4)

    def via_to(f):
        chunk_here(f, fwd_to * 2 + c)
        pass_on(f, 5)

    def via_far(f):
        chunk_here(f, zo * 2 + c)
        pass_on(f, 6)

    def gather_step(i):
        side = jnp.where(
            i < 2, z, jnp.where((i == 2) | (i == 5), fwd_from, jnp.where((i == 3) | (i == 4), fwd_to, zo))
        )
        own_core = lax.rem(i, 2) == 0

        @pl.when(i == 1)
        def _():
            via_from(0)
            via_to(0)

        @pl.when(i == 2)
        def _():
            via_from(1)

        @pl.when(i == 4)
        def _():
            via_to(1)
            via_far(0)

        @pl.when(i == 6)
        def _():
            via_far(1)

        @pl.when(jnp.logical_not(own_core))
        def _():
            for f in range(2):
                chunk_here(f, side * 2 + 1 - c)

        meet(side * 2 + jnp.where(own_core, c, 1 - c))

    loop(0, NS, gather_step)

    def attend(step):
        at = span(step, R)
        do = dov[at, :]
        top = jnp.max(topv[:, at], axis=0, keepdims=True)
        fade = jnp.exp2(topv[:, at] - top)
        total = jnp.sum(totv[:, at] * fade, axis=0, keepdims=True)
        rowdot = jnp.sum(dotv[:, at] * fade, axis=0, keepdims=True) / total
        top = top + jnp.log2(total)
        for k in range(0, KEYS, KC):
            dp = dot_nt(kb[k:k + KC, 0:LAT], do)
            p = jnp.exp2(sv[k:k + KC, at] - top)
            pt[k:k + KC, at] = p.astype(BF16)
            dst[k:k + KC, at] = (p * (dp - rowdot)).astype(BF16)
            heads = p[:, 0:QT]
            for h in range(QT, R, QT):
                heads = heads + p[:, h:h + QT]
            masst[k:k + KC, :] += heads

    loop(0, ROWS // R, attend)

    for k in range(0, KEYS, KC):
        massq[:, k:k + KC] = masst[k:k + KC, :].T

    def mass_pair(i):
        send(rows(massq, 2 * i + (1 - c), QL), mcr.at[i], m_ss.at[i], m_rs.at[i], me_k, mate)

    loop(0, NZ, mass_pair)

    def at_step(i):
        return jnp.where(i == 0, zo, jnp.where(i == 1, fwd_from, jnp.where(i == 2, fwd_to, z)))

    to_sq = fwd_to * 2 + c
    from_sq = fwd_from * 2 + c

    def spot(g, core, i):
        rows_at = pl.ds(pl.multiple_of((2 * min(g, 2) + core) * CH, CH), CH)
        return rows_at, pl.ds(pl.multiple_of(i * GW + (128 if g == 3 else 0), 128), WIDTHS[g])

    def cut(ref, g, *at):
        return ref.at[(g, *at, slice(None), slice(0, WIDTHS[g]))]

    def of_chip(g, i):
        there = at_step(i)
        arrived(cut(gcr, g, there), g_ss.at[g, there], g_rs.at[g, there])
        return gown[spot(g, c, i)] + cut(gcr, g, there)[...].astype(F32)

    def to_mate(g, i):
        there = at_step(i)
        cut(gs, g, there)[...] = gown[spot(g, 1 - c, i)].astype(BF16)
        send(cut(gs, g, there), cut(gcr, g, there), g_ss.at[g, there], g_rs.at[g, there], me_k, mate)

    def along(g, way, sq):
        send(cut(gzs, g, way), cut(gzr, g, way), gz_ss.at[g, way], gz_rs.at[g, way], me_k, sq)

    def direct(g):
        for way, sq in ((0, zo * 2 + c), (1, from_sq), (2, to_sq)):
            cut(gzs, g, way)[...] = of_chip(g, way).astype(BF16)
            along(g, way, sq)

    def relay(g):
        gzs[g, 0] = of_chip(g, 0).astype(BF16)
        along(g, 0, to_sq)

    def back(g):
        gzs[g, 1] = of_chip(g, 1).astype(BF16)
        along(g, 1, from_sq)

    def onward(g):
        arrived(gzr.at[g, 0], gz_ss.at[g, 0], gz_rs.at[g, 0])
        gzs[g, 2] = (of_chip(g, 2) + gzr[g, 0].astype(F32)).astype(BF16)
        along(g, 2, to_sq)

    def key_group(g, acts):
        lo = g * GW

        def step(i):
            at = span(at_step(i), 2 * CH)
            gown[g * 512:(g + 1) * 512, span(i, GW)] = (
                dot_nt(dst[at, :], qt[lo:lo + GW, :]) * ATTN_SCALE + dot(pt[at, :], dov[:, lo:lo + GW])
            )
            to_mate(g, i)
            for n, act in acts:
                pl.when(i == n)(act)

        loop(0, NZ, step)

    def rope_part(i):
        at = span(at_step(i), 2 * CH)
        rope = dot_nt(dst[at, :], qt[LAT:KD, :]) * ATTN_SCALE
        lane = pl.ds(pl.multiple_of(i * GW, 128), 128)
        gown[1024:1536, lane] = jnp.concatenate([rope, jnp.zeros((2 * CH, 128 - KD + LAT), F32)], axis=1)
        to_mate(2, i)

    def index_pair(i):
        lane = pl.ds(pl.multiple_of(i * GW + 128, 128), 128)
        gown[1024:1536, lane] = masst[span(at_step(i), 2 * CH), :]
        to_mate(3, i)

    def ship_home(g):
        acc = of_chip(g, 3)
        for way in (1, 2) if g < 2 else (0, 1, 2):
            arrived(cut(gzr, g, way), gz_ss.at[g, way], gz_rs.at[g, way])
            acc = acc + cut(gzr, g, way)[...].astype(F32)
        lanes = slice(0, WIDTHS[g])
        ob[g, :, lanes] = dot(to_slot[...], acc.astype(BF16)).astype(BF16)
        loop(1, NK, lambda d: send(
            home_part(ob, g, peer_k(d)), home_part(orx, g, me_k), o_ss.at[g, d], o_rs.at[g, d], peer_k(d), me_s))
        own = span(me_k, CAP * SUB)
        orx[g, own, lanes] = ob[g, own, lanes]

    def home_part(ref, g, k):
        return ref.at[g, span(k, CAP * SUB), 0:WIDTHS[g]]

    def mass_sum(there):
        arrived(mcr.at[there], m_ss.at[there], m_rs.at[there])
        return massq[span(2 * there + c, QL), :] + mcr[there]

    def mass_first():
        mzs[0] = mass_sum(zo)
        send(mzs.at[0], mzr.at[0], mz_ss.at[0], mz_rs.at[0], me_k, to_sq)
        mzs[1] = mass_sum(fwd_from)
        send(mzs.at[1], mzr.at[1], mz_ss.at[1], mz_rs.at[1], me_k, from_sq)

    def mass_onward():
        arrived(mzr.at[0], mz_ss.at[0], mz_rs.at[0])
        mzs[2] = mass_sum(fwd_to) + mzr[0]
        send(mzs.at[2], mzr.at[2], mz_ss.at[2], mz_rs.at[2], me_k, to_sq)
        mzs[3] = mass_sum(z)

    def dq_copy(head):
        step = lax.div(head, 4)
        lane = span(lax.rem(head, 4), QT)
        return pltpu.make_async_copy(dqv.at[lax.rem(step, 2), :, lane], dq_out.at[head], dq_sem.at[head])

    def query_grad(step):
        at = span(step, 512)
        grad = (dot_tn(kb[:, 0:KD], dst[:, at]) * ATTN_SCALE).astype(BF16)

        @pl.when(step >= 2)
        def _():
            for h in range(4):
                dq_copy((step - 2) * 4 + h).wait()

        dqv[lax.rem(step, 2)] = grad
        for h in range(4):
            dq_copy(step * 4 + h).start()

    key_group(0, ((1, lambda: relay(0)), (2, lambda: back(0)), (3, mass_first)))
    key_group(1, ((1, lambda: relay(1)), (1, lambda: onward(0)), (2, lambda: back(1)), (3, mass_onward)))
    loop(0, NZ, rope_part)
    onward(1)
    ship_home(0)
    loop(0, 1, query_grad)
    direct(2)

    logits = lgv[...]
    e = jnp.exp(logits - jnp.max(logits, axis=1, keepdims=True))
    guess = e / jnp.sum(e, axis=1, keepdims=True)
    mass = mzs[3]
    for way in (1, 2):
        arrived(mzr.at[way], mz_ss.at[way], mz_rs.at[way])
        mass = mass + mzr[way]
    dlogit = INDEX_SCALE * (guess - mass * (1.0 / H))
    dlv[...] = jnp.broadcast_to(dlogit[:, None, :], (QL, JL, KEYS)).reshape(QJ, KEYS)
    ikt[...] = jnp.zeros(ikt.shape, F32)

    def ship_grads(d):
        there = peer_s(d)
        send(rows(diqs, there, QJ), rows(diq_out, me_s, QJ), b_ss.at[d], b_rs.at[d], me_k, there)
        send(diws.at[there], diwr.at[me_s], v_ss.at[d], v_rs.at[d], me_k, there)

    def index_part(d):
        src = peer_s(d)
        sim = dot_nt(iqr[src], kb[:, IO:W])
        dl = dlv[...]
        ds = jnp.where(sim > 0, dl * jnp.tile(wv[src], (1, KEYS // 128)), 0.0).astype(BF16)
        dw = jnp.sum(dl * jnp.maximum(sim, 0.0), axis=1, keepdims=True).reshape(QL, JL, 1)
        diws[src] = jnp.sum(jnp.where(my_query, dw, 0.0), axis=0)
        diqs[span(src, QJ), :] = dot(ds, kb[:, IO:W])
        ikt[...] += dot(iqt[:, span(src, 128)], ds)
        pl.when(d >= 1)(lambda: ship_grads(d))
        pl.when(d == 3)(lambda: ship_home(1))
        pl.when(d == 6)(lambda: ship_home(2))

    loop(0, NS, index_part)

    diwr[me_s] = diws[me_s]
    here_iq = pltpu.make_async_copy(rows(diqs, me_s, QJ), rows(diq_out, me_s, QJ), fin_sem.at[0])
    here_iq.start()

    for k in range(0, KEYS, KC):
        masst[k:k + KC, :] = ikt[:, k:k + KC].T

    loop(0, NZ, index_pair)
    direct(3)
    loop(1, 4, query_grad)
    ship_home(3)

    def grads_here(d):
        arrived(rows(diq_out, from_s(d), QJ), b_ss.at[d], b_rs.at[d])
        arrived(diwr.at[from_s(d)], v_ss.at[d], v_rs.at[d])

    loop(1, NS, grads_here)
    weight_grad = diwr[0]
    for src in range(1, NS):
        weight_grad = weight_grad + diwr[src]
    diw_v[...] = weight_grad
    out_iw = pltpu.make_async_copy(diw_v, diw_out, fin_sem.at[1])
    out_iw.start()

    def sent_s(d):
        gone(rows(iq_hbm, peer_s(d), QJ), iqr.at[me_s], iq_ss.at[d], iq_rs.at[d])
        gone(iw_hbm, iwr.at[me_s], iw_ss.at[d], iw_rs.at[d])
        gone(rows(diqs, peer_s(d), QJ), rows(diq_out, me_s, QJ), b_ss.at[d], b_rs.at[d])
        gone(diws.at[peer_s(d)], diwr.at[me_s], v_ss.at[d], v_rs.at[d])

    loop(1, NS, sent_s)
    for f in range(2):
        for lane, (chunk, _) in enumerate(routes):
            gone(chunk_ref(chunk, f), chunk_ref(chunk, f), ag_ss.at[f, lane], ag_rs.at[f, 0])
        loop(1, NK, lambda d: fetch(f, d).wait_send())

    def sent_pair(i):
        gone(rows(massq, 2 * i + (1 - c), QL), mcr.at[i], m_ss.at[i], m_rs.at[i])
        for g in range(GROUPS):
            gone(cut(gs, g, i), cut(gcr, g, i), g_ss.at[g, i], g_rs.at[g, i])

    loop(0, NZ, sent_pair)
    for way in range(3):
        gone(mzs.at[way], mzr.at[way], mz_ss.at[way], mz_rs.at[way])
        for g in range(GROUPS):
            gone(cut(gzs, g, way), cut(gzr, g, way), gz_ss.at[g, way], gz_rs.at[g, way])

    loop(HL // 2, HL, lambda h: dq_copy(h).wait())
    here_iq.wait()
    out_iw.wait()

    out_lat = pltpu.make_async_copy(dlat_v, dlat_out, fin_sem.at[2])
    for g in range(GROUPS):
        loop(1, NK, lambda d: arrived(home_part(orx, g, from_k(d)), o_ss.at[g, d], o_rs.at[g, d]))
        grads = dot(home[...], orx[g, :, 0:WIDTHS[g]])
        if g < 2:
            dlat_v[:, :, g * GW:(g + 1) * GW] = grads.reshape(NK, SUB, GW)
        elif g == 2:
            dlat_v[:, :, LAT:KD] = grads[:, 0:KD - LAT].reshape(NK, SUB, KD - LAT)
            out_lat.start()
        else:
            didx_v[...] = grads.reshape(NK, SUB, ID)
    out_idx = pltpu.make_async_copy(didx_v, didx_out, fin_sem.at[3])
    out_idx.start()
    for g in range(GROUPS):
        loop(1, NK, lambda d: gone(
            home_part(ob, g, peer_k(d)), home_part(orx, g, me_k), o_ss.at[g, d], o_rs.at[g, d]))
    out_lat.wait()
    out_idx.wait()


def body(queries, out_grad, latent_keys, index_queries, index_weights, index_keys, picks):
    hbm = pl.BlockSpec(memory_space=pl.ANY)
    dma = pltpu.SemaphoreType.DMA
    v = pltpu.VMEM
    outs = pl.pallas_call(
        kernel,
        out_shape=[
            jax.ShapeDtypeStruct((HL, KD, QT), BF16),
            jax.ShapeDtypeStruct((NK, SUB, KD), F32),
            jax.ShapeDtypeStruct((QT * JL, ID), F32),
            jax.ShapeDtypeStruct((JL, QT), F32),
            jax.ShapeDtypeStruct((NK, SUB, ID), F32),
        ],
        in_specs=[hbm] * 6 + [pl.BlockSpec(memory_space=pltpu.SMEM)],
        out_specs=[hbm] * 5,
        scratch_shapes=[
            v((KD, ROWS), BF16), v((ROWS, LAT), BF16),
            v((NK, SUB, ID), BF16), v((NK, SUB, W), BF16),
            v((2, SLOTS, SUB, HALF), BF16), v((SLOTS, SUB, HALF), BF16), v((SLOTS, SUB, HALF), BF16),
            v((KEYS, W), BF16),
            v((SLOTS * SUB, CH), BF16), v((SLOTS * SUB, CH), BF16), v((CH, SLOTS * SUB), BF16),
            v((KEYS, ROWS), F32),
            v((KEYS, ROWS), BF16), v((KEYS, ROWS), BF16), v((2, KD, 512), BF16), v((8, ROWS), F32),
            v((8, ROWS), F32), v((8, ROWS), F32),
            v((NS, QJ, ID), BF16), v((NS, JL, QT), F32), v((NS, QJ, 128), F32), v((QL, KEYS), F32),
            v((KEYS, QT), F32),
            v((NZ, QL, KEYS), F32), v((NZ, QL, KEYS), F32), v((NZ, QL, KEYS), F32),
            v((ID, NS * QJ), BF16), v((NS, JL, QT), F32), v((NS, JL, QT), F32),
            v((GROUPS, NZ, CH, GW), BF16), v((GROUPS, NZ, CH, GW), BF16),
            v((GROUPS, NZ, CH, GW), BF16), v((GROUPS, NZ, CH, GW), BF16),
            v((GROUPS, SLOTS * SUB, GW), BF16), v((GROUPS, SLOTS * SUB, GW), BF16),
            v((NK, SUB, KD), F32), v((NK, SUB, ID), F32), v((JL, QT), F32),
            pltpu.SMEM((NK, CAP), jnp.int32),
            dma((4,)), dma((HL,)), dma((NK,)), dma((NS,)), dma((NS,)), dma((NS,)), dma((NS,)),
            dma((2, NK)), dma((2, NK)), dma((2, NS)), dma((2, NS)), dma((HL,)),
            dma((NZ,)), dma((NZ,)), dma((NZ,)), dma((NZ,)),
            dma((GROUPS, NZ)), dma((GROUPS, NZ)), dma((GROUPS, NZ)), dma((GROUPS, NZ)),
            dma((GROUPS, NK)), dma((GROUPS, NK)), dma((NS,)), dma((NS,)), dma((NS,)), dma((NS,)), dma((4,)),
        ],
        compiler_params=pltpu.CompilerParams(
            collective_id=0, has_side_effects=True, vmem_limit_bytes=64 * 1024 * 1024
        ),
        name="sparse_attention_backward",
    )(
        queries.transpose(1, 2, 0),
        out_grad.reshape(ROWS, LAT),
        latent_keys.transpose(0, 2, 1),
        index_queries.reshape(QT * JL, ID),
        index_weights.T,
        index_keys,
        picks,
    )
    def hand_over(*refs):
        given, made, held, sems = refs[:5], refs[5:10], refs[10:15], refs[15]
        parts = []
        for i in range(5):
            count = 4 if i == 0 else 1
            size = given[i].shape[0] // count
            parts += [(i, pl.ds(n * size, size)) for n in range(count)]
        loads = [pltpu.make_async_copy(given[i].at[at], held[i].at[at], sems.at[n]) for n, (i, at) in enumerate(parts)]
        stores = [pltpu.make_async_copy(held[i].at[at], made[i].at[at], sems.at[n]) for n, (i, at) in enumerate(parts)]
        for load in loads:
            load.start()
        for load, store in zip(loads, stores):
            load.wait()
            store.start()
        for store in stores:
            store.wait()

    dq, dlat, diq, diw, didx = pl.pallas_call(
        hand_over,
        out_shape=[jax.ShapeDtypeStruct(o.shape, o.dtype) for o in outs],
        in_specs=[hbm] * 5,
        out_specs=[hbm] * 5,
        scratch_shapes=[v(o.shape, o.dtype) for o in outs] + [dma((8,))],
        compiler_params=pltpu.CompilerParams(vmem_limit_bytes=64 * 1024 * 1024),
        name="hand_over",
    )(*outs)
    return (dq.transpose(2, 0, 1), dlat, diq.reshape(QT, JL, ID), diw.T, didx)


def solution(mesh):
    placed = (
        P("sk", "sq", None),
        P("sk", "sq", None),
        P("sk", None, None),
        P("sk", "sq", None),
        P("sk", "sq"),
        P("sk", None, None),
        P(),
    )
    return jax.shard_map(
        body,
        mesh=mesh,
        in_specs=placed,
        out_specs=(
            P("sk", "sq", None),
            P("sk", "sq", None),
            P("sk", "sq", None),
            P("sk", "sq"),
            P("sk", "sq", None),
        ),
        check_vma=False,
    )
```
